128 devices in a mesh: wide: 16 (over x, y), grp: 8 (over z, core).
Axes of the slice: x: 4, y: 4, z: 4, core: 2. Of those that a mesh axis runs over, the one named last changes fastest.
Arguments:
- velocity: float32 [3, 768, 128, 512], P(None, 'wide', 'grp'), may hold values from -5 to 5
- scalar: float32 [768, 128, 512], P('wide', 'grp'), may hold values from -5 to 5
- marker_owner: int32 [131072], P(('wide', 'grp')), may hold values from 0 to 127, as said below
- marker_tile: int32 [131072], P(('wide', 'grp')), may hold values from 0 to 3071
- marker_offset: int32 [131072], P(('wide', 'grp')), may hold values from 0 to 127
- marker_target: float32 [4, 131072], P(None, ('wide', 'grp')), may hold values from -4 to 4
- marker_eta: float32 [131072], P(('wide', 'grp')), may hold values from 0.1 to 1
Outputs:
- velocity_out: float32 [3, 768, 128, 512], P(None, 'wide', 'grp')
- scalar_out: float32 [768, 128, 512], P('wide', 'grp')
- marker_force: float32 [4, 131072], P(None, ('wide', 'grp'))
The draws below stay inside these ranges and needn't reach their ends.
Inputs may be any that keep to these rules, and one draw needn't show every extreme that they name: `marker_owner`: in each device's aligned block of 1024 markers no owner is named more than 32 times; one owner, the same for all blocks, is named exactly 32 times in every block, and in every block 8 further owners, which may differ from block to block, are named exactly 32 times each.
All inputs are finite; a program needn't handle non-finite values.
Results may differ from the reference program's by a relative error of at most 0.0003.
Values sent between devices are 32-bit elements; how exact they have to be, the bound alone decides.
No kernel may reach another device: no remote copies, remote signals or barrier semaphores. Data moves between devices by JAX's collectives and lax.ppermute only.
A program may use at most 192 MiB of HBM per device.

```python
import math
import jax
import jax.numpy as jnp

NX = 512
CY = 48
CZ = 16
M_DEV = 1024
HEAVY = 8
OWNERS = 128
NY = 768
NZ = 128
TILES = 3072
CAP = 32
MARKERS = 131072
N_GRP = 8


def draw_velocity(key, part):
    shape = (3, NY, NZ, NX)
    return jnp.clip(jax.random.normal(key, shape, jnp.float32), -5.0, 5.0)


def draw_marker_owner(key, part):
    shared = jax.random.randint(jax.random.fold_in(key, 11), (), 0, OWNERS)
    position = jnp.arange(M_DEV, dtype=jnp.int32)
    light_pick = HEAVY + (position - (HEAVY + 1) * CAP) % (OWNERS - 1 - HEAVY)
    chooser = jnp.where(position < CAP, -1, jnp.where(position < (HEAVY + 1) * CAP, (position - CAP) // CAP, light_pick))

    def one_block(block_id):
        block_key = jax.random.fold_in(key, block_id)
        others = jax.random.permutation(jax.random.fold_in(block_key, 1), jnp.arange(OWNERS - 1, dtype=jnp.int32))
        chosen = others[jnp.clip(chooser, 0, OWNERS - 2)]
        chosen = chosen + (chosen >= shared).astype(jnp.int32)
        owner_rows = jnp.where(chooser < 0, shared, chosen)
        shuffle = jax.random.permutation(jax.random.fold_in(block_key, 2), jnp.arange(M_DEV, dtype=jnp.int32))
        return owner_rows[shuffle]
    return jax.vmap(one_block)(jnp.arange(OWNERS, dtype=jnp.int32)).reshape(-1).astype(jnp.int32)


def place_ends(drawn, own_key, low, top_value):
    spot = [jax.random.randint(jax.random.fold_in(own_key, axis), (), 0, length) for axis, length in enumerate(drawn.shape)]
    main_axis = drawn.shape.index(max(drawn.shape))
    neighbour = spot[:main_axis] + [(spot[main_axis] + 1) % drawn.shape[main_axis]] + spot[main_axis + 1:]
    return drawn.at[tuple(spot)].set(low).at[tuple(neighbour)].set(top_value)


def levels(own_key, shape, pieces, low, largest):
    def one(dim, blocks):
        steps = jax.random.uniform(jax.random.fold_in(jax.random.fold_in(own_key, 6), dim), (blocks,), jnp.float32, low / len(pieces), largest / len(pieces))
        return jnp.repeat(jnp.exp(steps), shape[dim] // blocks).reshape((-1,) + (1,) * (len(shape) - dim - 1))

    loudness = one(*pieces[0])
    for cut in pieces[1:]:
        loudness = loudness * one(*cut)
    return loudness


def normal_values(own_key, dims, scale, reach, cuts=(), kind=jnp.bfloat16):
    level = levels(own_key, dims, cuts, -0.22, 0.18) if cuts else 1.0
    values = jax.random.normal(own_key, dims, jnp.float32) * scale * level
    return jnp.minimum(jnp.maximum(values, -reach), reach).astype(kind)


def setup_inputs(seed: int = 0) -> dict:
    streams_of = jax.random.split(jax.random.key(seed), 8)
    return {
        "velocity": draw_velocity(jax.random.fold_in(streams_of[7], 71), 0),
        "scalar": normal_values(streams_of[1], (NY, NZ, NX), 1.0, 5.0, ((0, 16), (1, 8)), jnp.float32),
        "marker_owner": draw_marker_owner(jax.random.fold_in(streams_of[7], 71), 0),
        "marker_tile": place_ends(jax.random.randint(streams_of[3], (MARKERS,), 0, TILES), jax.random.fold_in(streams_of[3], 1), 0, TILES - 1).astype(jnp.int32),
        "marker_offset": place_ends(jax.random.randint(streams_of[4], (MARKERS,), 0, 128), jax.random.fold_in(streams_of[4], 1), 0, 127).astype(jnp.int32),
        "marker_target": normal_values(streams_of[5], (4, MARKERS), 1.0, 4.0, ((1, 128),), jnp.float32),
        "marker_eta": jnp.clip(jnp.exp(math.log(1.0) - 2.3025851 * jax.random.uniform(streams_of[6], (MARKERS,), jnp.float32) ** levels(streams_of[6], (MARKERS,), ((0, 128),), -0.2, 0.2)), 0.1, 1.0),
    }


time_step = 0.1
viscosity = 0.4
diffusivity = 0.25


def update(center, east, west, north, south, upper, lower):
    coeffs = jnp.array([viscosity, viscosity, viscosity, diffusivity], dtype=jnp.float32)[:, None, None, None]
    transport = center[0] * ((east - west) * 0.5) + center[1] * ((north - south) * 0.5) + center[2] * ((upper - lower) * 0.5)
    laplace = east + west + north + south + upper + lower - 6.0 * center
    return center + time_step * (coeffs * laplace - transport)


def wave_terms(index, length):
    theta = (2.0 * jnp.pi / length) * index.astype(jnp.float32)
    half_sin = jnp.sin(0.5 * theta)
    return -2.0 * half_sin * half_sin, jnp.sin(theta), 4.0 * half_sin * half_sin


def reference(velocity, scalar, marker_owner, marker_tile, marker_offset, marker_target, marker_eta):
    fields = jnp.concatenate([velocity, scalar[None]], axis=0)
    star = update(fields, jnp.roll(fields, -1, 3), jnp.roll(fields, 1, 3), jnp.roll(fields, -1, 1), jnp.roll(fields, 1, 1), jnp.roll(fields, -1, 2), jnp.roll(fields, 1, 2))
    local_cell = marker_tile * 128 + marker_offset
    index_y = (marker_owner // N_GRP) * CY + local_cell // (CZ * NX)
    index_z = (marker_owner % N_GRP) * CZ + (local_cell // NX) % CZ
    index_x = local_cell % NX
    flat_index = ((index_y * NZ + index_z) * NX + index_x).astype(jnp.int32)
    star_flat = star.reshape(4, NY * NZ * NX)
    sampled = star_flat[:, flat_index]
    marker_force = marker_eta[None, :] * (marker_target - sampled)
    forced = star_flat.at[:, flat_index].add(marker_force).reshape(4, NY, NZ, NX)
    spectra = jnp.fft.fftn(forced[:3], axes=(1, 2, 3))
    x_real, x_imag, x_square = wave_terms(jnp.arange(NX, dtype=jnp.int32), NX)
    y_real, y_imag, y_square = wave_terms(jnp.arange(NY, dtype=jnp.int32), NY)
    z_real, z_imag, z_square = wave_terms(jnp.arange(NZ, dtype=jnp.int32), NZ)
    factor_x = (x_real + 1j * x_imag)[None, None, :]
    factor_y = (y_real + 1j * y_imag)[:, None, None]
    factor_z = (z_real + 1j * z_imag)[None, :, None]
    total_square = x_square[None, None, :] + y_square[:, None, None] + z_square[None, :, None]
    inverse_square = jnp.where(total_square > 0, 1.0 / jnp.where(total_square > 0, total_square, 1.0), 0.0)
    divergence = factor_x * spectra[0] + factor_y * spectra[1] + factor_z * spectra[2]
    factors = [factor_x, factor_y, factor_z]
    projected = []
    for comp_index in range(3):
        corrected = spectra[comp_index] - jnp.conj(factors[comp_index]) * divergence * inverse_square
        projected.append(jnp.real(jnp.fft.ifftn(corrected)))
    velocity_out = jnp.stack(projected).astype(jnp.float32)
    return velocity_out, forced[3], marker_force
```

```python
import functools
import math

import jax
import jax.numpy as jnp
import ml_dtypes
import numpy as np
from jax import lax
from jax.experimental import pallas as pl
from jax.experimental.pallas import tpu as pltpu
from jax.sharding import PartitionSpec as P

time_step = 0.1
viscosity = 0.4
diffusivity = 0.25
f32 = jnp.float32
bf16 = jnp.bfloat16
lanes = 128
slots = 32
vmem = pl.BlockSpec(memory_space=pltpu.VMEM)


def iota(shape, dim):
    return lax.broadcasted_iota(jnp.int32, shape, dim)


def call(body, out, args, scratch=(), name=None, micros=0):
    shapes = [jax.ShapeDtypeStruct(s, d) for s, d in out]
    moved = sum(a.size * a.dtype.itemsize for a in args)
    moved += sum(s.size * s.dtype.itemsize for s in shapes)
    held = moved + sum(math.prod(s.shape) * 4 for s in scratch if hasattr(s, "dtype"))
    moved = max(moved, micros * 3000000)
    return pl.pallas_call(
        body,
        out_shape=shapes,
        in_specs=[vmem] * len(args),
        out_specs=[vmem] * len(out),
        scratch_shapes=list(scratch),
        compiler_params=pltpu.CompilerParams(vmem_limit_bytes=held + 6 * 2**20),
        cost_estimate=pl.CostEstimate(flops=0, bytes_accessed=moved, transcendentals=0),
        name=name,
    )(*args)


def passed_along(value, axis, steps):
    count = lax.axis_size(axis)
    return lax.ppermute(value, axis, [(i, (i + steps) % count) for i in range(count)])


def real_basis(length):
    place = np.arange(length)
    columns, squares = [], []
    for k in range(length // 2 + 1):
        angle = 2.0 * np.pi * ((k * place) % length) / length
        scale = math.sqrt((1.0 if k in (0, length // 2) else 2.0) / length)
        square = 4.0 * math.sin(math.pi * k / length) ** 2
        columns.append(scale * np.cos(angle))
        squares.append(square)
        if k not in (0, length // 2):
            columns.append(scale * np.sin(angle))
            squares.append(square)
    return np.stack(columns, axis=1), np.array(squares)


def two_parts(table):
    high = table.astype(np.float32).astype(ml_dtypes.bfloat16)
    low = (table - high.astype(np.float64)).astype(np.float32).astype(ml_dtypes.bfloat16)
    return high, low


def decay_tables(squares_x, squares_z, n_grp, n_wide, rows_y):
    full_y = n_wide * rows_y
    local = squares_x.shape[0] // n_grp
    square = squares_z[None, :, None] + squares_x.reshape(n_grp, 1, local)
    mean_mode = square == 0.0
    safe = np.where(mean_mode, 1.0, square)
    root = 1.0 / (1.0 + safe / 2.0 + np.sqrt(safe + safe * safe / 4.0))
    root = np.where(mean_mode, 0.0, root)
    gain = np.where(mean_mode, 0.0, -root / (1.0 - root * root))
    half = rows_y // 2
    full = np.stack([root, root**half, gain], axis=1)
    full = np.concatenate([full, full], axis=3)
    device = root**rows_y
    small = np.stack([device, 1.0 / (1.0 - root**full_y)], axis=1)
    upper = small.shape[2] // 2
    small = np.concatenate([small[:, :, :upper], small[:, :, upper:]], axis=3)
    share = upper // n_wide
    small = small.reshape(n_grp, 2, n_wide, share, 2 * local).transpose(0, 2, 1, 3, 4)
    small = np.concatenate([small, small], axis=3)
    return full.astype(np.float32), small.astype(np.float32)


def split_two(value):
    high = value.astype(bf16)
    return high, (value - high.astype(f32)).astype(bf16)


def split_three(value):
    high = value.astype(bf16)
    rest = value - high.astype(f32)
    middle = rest.astype(bf16)
    return high, middle, (rest - middle.astype(f32)).astype(bf16)


def dot(left, right, dims=((1,), (0,))):
    return lax.dot_general(left, right, (dims, ((), ())), preferred_element_type=f32)


def pack_body(owner_ref, tile_ref, offset_ref, target_ref, eta_ref, send_ref, rank_ref):
    owners = send_ref.shape[0]
    held = owner_ref.shape[1]
    onehot = owner_ref[...] == iota((owners, held), 0)
    onehot = jnp.where(onehot, 1.0, 0.0)
    upto = jnp.where(iota((lanes, lanes), 0) <= iota((lanes, lanes), 1), 1.0, 0.0).astype(bf16)
    carry = jnp.zeros((owners, 1), f32)
    ranks = []
    for start in range(0, held, lanes):
        piece = onehot[:, start : start + lanes]
        running = dot(piece.astype(bf16), upto) + carry
        ranks.append(jnp.sum(running * piece, axis=0, keepdims=True) - 1.0)
        carry = carry + jnp.sum(piece, axis=1, keepdims=True)
    rank = jnp.concatenate(ranks, axis=1).astype(jnp.int32)
    rank_ref[...] = rank
    chosen = rank == iota((slots, held), 0)
    cell = (tile_ref[...] * lanes + offset_ref[...]).astype(f32)
    values = [target_ref[k : k + 1, :] for k in range(4)] + [eta_ref[...], cell]
    onehot = onehot.astype(bf16)
    total = jnp.zeros((owners, 6 * slots), f32)
    for part in range(3):
        rows = [
            jnp.where(chosen, split_three(v)[part].astype(f32), 0.0).astype(bf16) for v in values
        ]
        total = total + dot(onehot, jnp.concatenate(rows, axis=0), ((1,), (1,)))
    column = iota((owners, 2 * lanes), 1)
    slot = column - 5 * slots
    spare = (slot >= 0) & (slot < slots) & (slot.astype(f32) >= carry)
    total = jnp.concatenate([total, jnp.zeros((owners, 2 * lanes - 6 * slots), f32)], axis=1)
    send_ref[...] = total + jnp.where(spare, (slot * lanes).astype(f32), 0.0)


def unpack_body(
    n_grp, all_rows, row_cells, owner_ref, rank_ref, back_ref, place_ref, force_ref, mean_ref
):
    size = back_ref.shape[1] // 3
    owners = back_ref.shape[0] * n_grp
    held = owner_ref.shape[1]
    onehot = jnp.where(owner_ref[...] == iota((owners, held), 0), 1.0, 0.0).astype(bf16)
    sums = back_ref[:, 2 * size, :]
    sums = jnp.concatenate([sums, jnp.zeros((lanes - sums.shape[0], lanes), f32)], axis=0).T
    mine = jnp.where(place_ref[...] == 0, sums, 0.0)
    mean = jnp.sum(jnp.sum(sums, axis=1, keepdims=True), axis=0, keepdims=True)
    mine = jnp.sum(mine, axis=1, keepdims=True) * (1.0 / row_cells)
    mean_ref[...] = jnp.broadcast_to(mine - mean * (1.0 / (all_rows * row_cells)), mean_ref.shape)
    back = back_ref[:, size : 2 * size, :].reshape(owners, lanes).T
    spread = sum(dot(part, onehot) for part in split_three(back))
    chosen = rank_ref[...] == iota((slots, held), 0)
    for k in range(4):
        piece = jnp.where(chosen, spread[k * slots : (k + 1) * slots], 0.0)
        force_ref[k : k + 1, :] = jnp.sum(piece, axis=0, keepdims=True)


def swap_groups(value):
    row = iota(value.shape, 0) & 3
    group = lax.shift_right_logical(iota(value.shape, 1), 5)
    count = value.shape[0]
    out = value
    for k in (1, 2, 3):
        moved = pltpu.roll(value, 32 * k, 1)
        moved = jnp.where(
            row + k < 4, pltpu.roll(moved, count - k, 0), pltpu.roll(moved, 4 - k, 0)
        )
        out = jnp.where(((group - row) & 3) == k, moved, out)
    return out


def marker_part(recv_ref, out_ref, force_ref, samp, table, index, sem, tiles_x, depth_z):
    sources = recv_ref.shape[0]
    wide_lane = iota((sources, lanes), 1)
    second = recv_ref[:, lanes : 2 * lanes]
    cell = pltpu.roll(second.astype(jnp.int32), lanes - 32, 1)
    tile = lax.shift_right_logical(cell, 7)
    shift_x = tiles_x.bit_length() - 1
    shift_z = shift_x + depth_z.bit_length() - 1
    row = lax.shift_right_logical(tile, shift_z) * tiles_x + (tile & (tiles_x - 1))
    row = row * depth_z + (lax.shift_right_logical(tile, shift_x) & (depth_z - 1))
    spot = (iota((sources, lanes), 0) & 3) * 32 + (wide_lane & 31)
    there = (spot - cell) & (lanes - 1)
    back = (cell - spot) & (lanes - 1)
    table[...] = jnp.where(
        wide_lane < 32,
        4 * row,
        jnp.where(wide_lane < 64, pltpu.roll(there, 32, 1), pltpu.roll(back, 64, 1)),
    )
    copy = pltpu.make_async_copy(table, index, sem)
    copy.start()
    copy.wait()
    lane = iota((4, lanes), 1)

    def at(place):
        return pl.ds(pl.multiple_of(place, 4), 4)

    def gather(batch, carry):
        found = jnp.zeros((4, lanes), f32)
        for q in range(4):
            for r in range(slots):
                source = 4 * batch + q
                value = out_ref[at(index[source, r]), :]
                value = pltpu.roll(value, index[source, 32 + r], 1)
                found = jnp.where(lane == 32 * q + r, value, found)
        samp[pl.ds(pl.multiple_of(4 * batch, 4), 4), :] = found
        return carry

    lax.fori_loop(0, sources // 4, gather, 0)
    eta = jnp.where(wide_lane < 32, second, 0.0)
    eta = eta + pltpu.roll(eta, 32, 1)
    eta = eta + pltpu.roll(eta, 64, 1)
    force = swap_groups(eta) * (swap_groups(recv_ref[:, 0:lanes]) - samp[...])
    samp[...] = force
    force_ref[...] = swap_groups(force)

    def scatter(batch, carry):
        mine = samp[pl.ds(pl.multiple_of(4 * batch, 4), 4), :]
        for sub in range(4):
            source = 4 * batch + sub
            terms = []
            for r in range(slots):
                only = jnp.where(lane == 32 * sub + r, mine, 0.0)
                terms.append(pltpu.roll(only, index[source, 64 + r], 1))
            for q in range(0, slots, 4):
                places = [index[source, q + j] for j in range(4)]
                values = [out_ref[at(place), :] for place in places]
                for j in range(4):
                    for i in range(j):
                        values[j] = jnp.where(places[i] == places[j], values[i], values[j])
                    values[j] = values[j] + terms[q + j]
                for j in range(4):
                    out_ref[at(places[j]), :] = values[j]
        return carry

    lax.fori_loop(0, sources // 4, scatter, 0)


def at_row(y, x, f, tiles_x, depth_z):
    return pl.ds((y * tiles_x + x) * (4 * depth_z) + f, depth_z, stride=4)


def stencil_part(vel_ref, scal_ref, ylo_ref, yhi_ref, zlo_ref, zhi_ref, out_ref):
    _, rows_y, depth_z, length_x = vel_ref.shape
    tiles_x = length_x // lanes
    level = iota((depth_z, length_x), 0)

    def one_row(y, carry):
        at_low = y == 0
        at_high = y == rows_y - 1
        below = jnp.maximum(y - 1, 0)
        above = jnp.minimum(y + 1, rows_y - 1)
        flow = [vel_ref[f, y] for f in range(3)]
        for f in range(4):
            if f < 3:
                center = flow[f]
                low, high = vel_ref[f, below], vel_ref[f, above]
            else:
                center = scal_ref[y]
                low, high = scal_ref[below], scal_ref[above]
            south = jnp.where(at_low, ylo_ref[f], low)
            north = jnp.where(at_high, yhi_ref[f], high)
            east = pltpu.roll(center, length_x - 1, 1)
            west = pltpu.roll(center, 1, 1)
            top = jnp.broadcast_to(zhi_ref[f, pl.ds(y, 1), :], center.shape)
            bottom = jnp.broadcast_to(zlo_ref[f, pl.ds(y, 1), :], center.shape)
            upper = jnp.where(level == depth_z - 1, top, pltpu.roll(center, depth_z - 1, 0))
            lower = jnp.where(level == 0, bottom, pltpu.roll(center, 1, 0))
            transport = (
                flow[0] * (east - west) + flow[1] * (north - south) + flow[2] * (upper - lower)
            )
            around = east + west + north + south + upper + lower
            coeff = viscosity if f < 3 else diffusivity
            star = (
                center * (1.0 - 6.0 * time_step * coeff)
                + (time_step * coeff) * around
                - (0.5 * time_step) * transport
            )
            for x in range(tiles_x):
                out_ref[at_row(y, x, f, tiles_x, depth_z), :] = star[:, x * lanes : (x + 1) * lanes]
        return carry

    lax.fori_loop(0, rows_y, one_row, 0)


def wide_row(ref, f, y, tiles_x, depth_z):
    return jnp.concatenate(
        [ref[at_row(y, x, f, tiles_x, depth_z), :] for x in range(tiles_x)], axis=1
    )


def packed_rows(rows_y, depth_z, n_wide):
    cells = rows_y // 2 * depth_z
    row = cells + depth_z // 2
    plane = row + rows_y // 2
    return cells, row, plane, plane + n_wide, plane + n_wide + 8


def halves(one, two, first_half):
    even = jnp.where(first_half, one, pltpu.roll(two, lanes // 2, 1))
    odd = jnp.where(first_half, pltpu.roll(one, lanes // 2, 1), two)
    return even, odd


def times_x(value, high_ref, low_ref):
    high, low = split_two(value)
    return dot(high, high_ref[...]) + dot(low, high_ref[...]) + dot(high, low_ref[...])


def divergence_part(forced_ref, div, sums, shape):
    rows_y, depth_z, length_x = shape
    tiles_x = length_x // lanes
    rows = rows_y * depth_z
    level = iota((depth_z, length_x), 0)
    sums[...] = jnp.zeros_like(sums)

    def one_row(y, carry):
        after = jnp.minimum(y + 1, rows_y - 1)
        along = wide_row(forced_ref, 0, y, tiles_x, depth_z)
        second = wide_row(forced_ref, 1, y, tiles_x, depth_z)
        third = wide_row(forced_ref, 2, y, tiles_x, depth_z)
        north = wide_row(forced_ref, 1, after, tiles_x, depth_z)
        north = jnp.where(y == rows_y - 1, 0.0, north)
        upper = jnp.where(level == depth_z - 1, 0.0, pltpu.roll(third, depth_z - 1, 0))
        total = pltpu.roll(along, length_x - 1, 1) - along + (north - second) + (upper - third)
        div[pl.ds(pl.multiple_of(y * depth_z, depth_z), depth_z), :] = total
        div[pl.ds(rows + depth_z + y, 1), :] = third[0:1, :]
        folded = sum(second[:, x * lanes : (x + 1) * lanes] for x in range(tiles_x))
        sums[pl.ds(y, 1), :] = jnp.sum(folded, axis=0, keepdims=True)
        return carry

    lax.fori_loop(0, rows_y, one_row, 0)
    div[rows : rows + depth_z, :] = wide_row(forced_ref, 1, 0, tiles_x, depth_z)


def first_body(
    vel_ref,
    scal_ref,
    ylo_ref,
    yhi_ref,
    zlo_ref,
    zhi_ref,
    recv_ref,
    high_ref,
    low_ref,
    forced_ref,
    out_ref,
    force,
    samp,
    table,
    div,
    modes,
    index,
    sem,
):
    _, rows_y, depth_z, length_x = vel_ref.shape
    n_grp = out_ref.shape[0]
    n_wide = recv_ref.shape[0] // n_grp
    rows = rows_y * depth_z
    tiles_x = length_x // lanes
    stencil_part(vel_ref, scal_ref, ylo_ref, yhi_ref, zlo_ref, zhi_ref, forced_ref)
    marker_part(recv_ref, forced_ref, force, samp, table, index, sem, tiles_x, depth_z)
    divergence_part(forced_ref, div, samp, (rows_y, depth_z, length_x))
    chunk = div.shape[0] // 4
    for start in range(0, 4 * chunk, chunk):
        modes[start : start + chunk, :] = times_x(div[start : start + chunk, :], high_ref, low_ref)
    cells, row, plane, forces, end = packed_rows(rows_y, depth_z, n_wide)

    def send(front, back, size, place):
        first_half = iota((size, lanes), 1) < lanes // 2
        for j in range(n_grp // 2):
            one = modes[pl.ds(front, size), j * lanes : (j + 1) * lanes]
            two = modes[pl.ds(back, size), j * lanes : (j + 1) * lanes]
            even, odd = halves(one, two, first_half)
            out_ref[2 * j, pl.ds(place, size), :] = even
            out_ref[2 * j + 1, pl.ds(place, size), :] = odd

    def shuffle(y, carry):
        front = pl.multiple_of(y * depth_z, depth_z)
        back = pl.multiple_of((y + rows_y // 2) * depth_z, depth_z)
        send(front, back, depth_z, front)
        return carry

    lax.fori_loop(0, rows_y // 2, shuffle, 0)
    send(rows, rows + depth_z // 2, depth_z // 2, cells)
    send(rows + depth_z, rows + depth_z + rows_y // 2, rows_y // 2, row)
    total = jnp.broadcast_to(jnp.sum(samp[...].T, axis=0, keepdims=True), (end - forces, lanes))
    for g in range(n_grp):
        out_ref[g, plane:forces, :] = force[pl.ds(g, n_wide, stride=n_grp), :]
        out_ref[g, forces:end, :] = total


def times_z(value, high_ref, low_ref):
    high, low = split_two(value)
    return dot(high_ref[...], high) + dot(high_ref[...], low) + dot(low_ref[...], high)


def forward_z_body(
    rows_y, recv_ref, high_ref, low_ref, table_ref, coef_ref, ends_ref, small_ref
):
    n_grp = recv_ref.shape[0]
    n_wide = small_ref.shape[0]
    steps, full_z, _ = coef_ref.shape
    depth_z = full_z // n_grp
    cells, row, plane, forces, end = packed_rows(rows_y, depth_z, n_wide)
    root = table_ref[0]
    last = iota((n_grp, depth_z, lanes), 1) == depth_z - 1
    first_half = iota((full_z, lanes), 1) < lanes // 2

    def cells_of(step):
        value = recv_ref[:, pl.ds(pl.multiple_of(step * depth_z, depth_z), depth_z), :]
        edge = recv_ref[:, pl.ds(row + step, 1), :]
        edge = jnp.concatenate([edge[1:], edge[:1]], axis=0)
        value = value + jnp.where(last, jnp.broadcast_to(edge, value.shape), 0.0)
        return value.reshape(full_z, lanes)

    def one_pair(pair, total):
        value = jnp.concatenate([cells_of(2 * pair), cells_of(2 * pair + 1)], axis=1)
        found = times_z(value, high_ref, low_ref)
        coef_ref[2 * pair] = found[:, :lanes]
        coef_ref[2 * pair + 1] = found[:, lanes:]
        return found[:, lanes:] + root * (found[:, :lanes] + root * total)

    packed = recv_ref[:, cells:row, :]
    other = jnp.stack([pltpu.roll(packed[g], lanes // 2, 1) for g in range(n_grp)], axis=0)
    extra = jnp.concatenate([packed, other], axis=1).reshape(full_z, lanes)
    extra = jnp.where(first_half, times_z(extra, high_ref, low_ref), 0.0)
    ends_ref[2] = extra
    up = lax.fori_loop(0, steps // 2, one_pair, extra)
    down = lax.fori_loop(
        0,
        steps,
        lambda i, total: coef_ref[steps - 1 - i] + root * total,
        jnp.zeros((full_z, lanes), f32),
    )
    down = root * down
    ends_ref[0] = up
    ends_ref[1] = down
    over = table_ref[1]
    up_other = pltpu.roll(up, lanes // 2, 1)
    down_other = pltpu.roll(down, lanes // 2, 1)
    up = jnp.where(first_half, up_other + over * up, up + over * up_other)
    down = jnp.where(first_half, down + over * down_other, down_other + over * down)
    down = down + extra + pltpu.roll(extra, lanes // 2, 1)
    upper = full_z // 2
    share = upper // n_wide
    for k, value in enumerate((up, down)):
        value = jnp.where(first_half[:upper], value[:upper], value[upper:])
        for i in range(n_wide):
            small_ref[i, k * share : (k + 1) * share, :] = value[i * share : (i + 1) * share]
    sums = sum(recv_ref[g, forces:end, :] for g in range(n_grp))
    for i in range(n_wide):
        for g in range(n_grp):
            place = 2 * share + g
            small_ref[i, place : place + 1, :] = recv_ref[g, plane + i : plane + i + 1, :]
        small_ref[i, 2 * share + n_grp : 2 * share + n_grp + 8, :] = sums


def widen(small):
    first_half = iota(small.shape, 1) < lanes // 2
    other = pltpu.roll(small, lanes // 2, 1)
    return jnp.concatenate(
        [jnp.where(first_half, small, other), jnp.where(first_half, other, small)], axis=0
    )


def backward_z_body(
    rows_y, coef_ref, ends_ref, small_ref, table_ref, high_ref, low_ref, out_ref, ups, small
):
    n_grp = out_ref.shape[0]
    steps, full_z, _ = coef_ref.shape
    depth_z = full_z // n_grp
    cells, row, _, _, _ = packed_rows(rows_y, depth_z, small_ref.shape[0])
    root, over, gain = table_ref[0], table_ref[1], table_ref[2]
    first_half = iota((full_z, lanes), 1) < lanes // 2
    share = small_ref.shape[1] // 2
    for i in range(small_ref.shape[0]):
        for k in range(2):
            small[k, i * share : (i + 1) * share] = small_ref[i, k * share : (k + 1) * share]
    up_in = widen(small[0])
    down_in = widen(small[1])
    up_start = jnp.where(
        first_half,
        up_in + ends_ref[2],
        pltpu.roll(ends_ref[0], lanes // 2, 1) + over * up_in,
    )
    down = jnp.where(
        first_half, pltpu.roll(ends_ref[1], lanes // 2, 1) + over * down_in, down_in
    )

    def rising(step, total):
        total = coef_ref[step] + root * total
        ups[step] = total
        return total

    lax.fori_loop(0, steps, rising, up_start)

    def falling(i, total):
        pair = steps // 2 - 1 - i
        second = gain * (ups[2 * pair + 1] + total)
        total = root * (coef_ref[2 * pair + 1] + total)
        first = gain * (ups[2 * pair] + total)
        total = root * (coef_ref[2 * pair] + total)
        found = times_z(jnp.concatenate([first, second], axis=1), high_ref, low_ref)
        for j in range(2):
            step = 2 * pair + j
            value = found[:, j * lanes : (j + 1) * lanes]
            start = pl.multiple_of(step * depth_z, depth_z)
            out_ref[:, pl.ds(start, depth_z), :] = value.reshape(n_grp, depth_z, lanes)
            for g in range(n_grp):
                before = (g * depth_z - 1) % full_z
                out_ref[g, pl.ds(row + step, 1), :] = value[before : before + 1, :]
        return total

    down = lax.fori_loop(0, steps // 2, falling, down)
    extra = times_z(gain * (up_start + down), high_ref, low_ref)
    half = depth_z // 2
    for g in range(n_grp):
        start = g * depth_z
        out_ref[g, cells:row, :] = jnp.where(
            first_half[:half],
            extra[start : start + half],
            pltpu.roll(extra[start + half : start + depth_z], lanes // 2, 1),
        )


def last_body(recv_ref, forced_ref, mean_ref, high_ref, low_ref, vel_ref, scal_ref, modes, press_ref):
    n_grp = recv_ref.shape[0]
    _, rows_y, depth_z, length_x = vel_ref.shape
    rows = rows_y * depth_z
    tiles_x = length_x // lanes
    cells, row, _, _, _ = packed_rows(rows_y, depth_z, 0)

    def take(front, back, size, place):
        first_half = iota((size, lanes), 1) < lanes // 2
        for j in range(n_grp // 2):
            even = recv_ref[2 * j, pl.ds(place, size), :]
            odd = recv_ref[2 * j + 1, pl.ds(place, size), :]
            one, two = halves(even, odd, first_half)
            modes[pl.ds(front, size), j * lanes : (j + 1) * lanes] = one
            modes[pl.ds(back, size), j * lanes : (j + 1) * lanes] = two

    def shuffle(y, carry):
        front = pl.multiple_of(y * depth_z, depth_z)
        back = pl.multiple_of((y + rows_y // 2) * depth_z, depth_z)
        take(front, back, depth_z, front)
        return carry

    lax.fori_loop(0, rows_y // 2, shuffle, 0)
    take(rows, rows + depth_z // 2, depth_z // 2, cells)
    take(rows + depth_z, rows + depth_z + rows_y // 2, rows_y // 2, row)
    chunk = modes.shape[0] // 4
    for start in range(0, 4 * chunk, chunk):
        press_ref[start : start + chunk, :] = times_x(
            modes[start : start + chunk, :], high_ref, low_ref
        )
    level = iota((depth_z, length_x), 0)

    def one_row(y, carry):
        start = pl.multiple_of(y * depth_z, depth_z)
        before = pl.multiple_of(jnp.where(y == 0, rows, start - depth_z), depth_z)
        press = press_ref[pl.ds(start, depth_z), :]
        south = press_ref[pl.ds(before, depth_z), :]
        below = jnp.broadcast_to(press_ref[pl.ds(rows + depth_z + y, 1), :], press.shape)
        lower = jnp.where(level == 0, below, pltpu.roll(press, 1, 0))
        west = pltpu.roll(press, 1, 1)
        mean = mean_ref[pl.ds(y, 1), :]
        mean = jnp.concatenate([mean] * tiles_x, axis=1)
        vel_ref[0, y] = wide_row(forced_ref, 0, y, tiles_x, depth_z) - (press - west)
        vel_ref[1, y] = wide_row(forced_ref, 1, y, tiles_x, depth_z) - (press - south) - mean
        vel_ref[2, y] = wide_row(forced_ref, 2, y, tiles_x, depth_z) - (press - lower)
        scal_ref[y] = wide_row(forced_ref, 3, y, tiles_x, depth_z)
        return carry

    lax.fori_loop(0, rows_y, one_row, 0)


def ring_body(recv_ref, table_ref, out_ref):
    count, size, _ = out_ref.shape
    rising = iota((size, lanes), 0) < size // 2
    ends = [
        jnp.where(rising, recv_ref[i, 0:size, :], recv_ref[count - 1 - i, 0:size, :])
        for i in range(count)
    ]
    step, whole = table_ref[0], table_ref[1]
    total = ends[0]
    for i in range(1, count):
        total = ends[i] + step * total
    total = whole * total
    reached = []
    for i in range(count):
        reached.append(total)
        total = ends[i] + step * total
    for i in range(count):
        out_ref[i] = jnp.where(rising, reached[i], reached[count - 1 - i])


def per_device(
    tables, velocity, scalar, marker_owner, marker_tile, marker_offset, marker_target, marker_eta
):
    _, rows_y, depth_z, length_x = velocity.shape
    n_wide = lax.axis_size("wide")
    n_grp = lax.axis_size("grp")
    owners = n_wide * n_grp
    full_z = depth_z * n_grp
    rows = rows_y * depth_z
    tiles_x = length_x // lanes
    held = marker_owner.shape[0]
    x_high, x_low, xt_high, xt_low, z_high, z_low, zt_high, zt_low, full, small_table = tables
    my_grp = lax.axis_index("grp")
    my_wide = lax.axis_index("wide")
    full = lax.dynamic_index_in_dim(full, my_grp, 0, keepdims=False)
    small_table = lax.dynamic_slice(
        small_table, (my_grp, my_wide, 0, 0, 0), (1, 1) + small_table.shape[2:]
    )[0, 0]

    def edge(part, dim):
        index = 0 if part == 0 else velocity.shape[dim] - 1
        return jnp.concatenate(
            [
                lax.index_in_dim(velocity, index, dim, keepdims=False),
                lax.index_in_dim(scalar, index, dim - 1, keepdims=False)[None],
            ],
            axis=0,
        )

    y_low = passed_along(edge(1, 1), "wide", 1)
    y_high = passed_along(edge(0, 1), "wide", -1)
    z_low_cells = passed_along(edge(1, 2), "grp", 1)
    z_high_cells = passed_along(edge(0, 2), "grp", -1)

    owner = marker_owner[None, :]
    send, rank = call(
        pack_body,
        [((owners, 2 * lanes), f32), ((1, held), jnp.int32)],
        [owner, marker_tile[None, :], marker_offset[None, :], marker_target, marker_eta[None, :]],
        name="pack",
    )
    recv = lax.all_to_all(send, ("wide", "grp"), split_axis=0, concat_axis=0, tiled=True)
    flat = 4 * tiles_x * rows
    sent_rows = packed_rows(rows_y, depth_z, n_wide)[-1]
    back_rows = packed_rows(rows_y, depth_z, n_wide)[2]
    with_edges = rows + depth_z + rows_y
    forced, chunks = call(
        first_body,
        [((flat, lanes), f32), ((n_grp, sent_rows, lanes), f32)],
        [velocity, scalar, y_low, y_high, z_low_cells, z_high_cells, recv, x_high, x_low],
        [
            pltpu.VMEM((owners, lanes), f32),
            pltpu.VMEM((owners, lanes), f32),
            pltpu.VMEM((owners, lanes), jnp.int32),
            pltpu.VMEM((with_edges, length_x), f32),
            pltpu.VMEM((with_edges, length_x), f32),
            pltpu.SMEM((owners, lanes), jnp.int32),
            pltpu.SemaphoreType.DMA(()),
        ],
        name="first",
        micros=40,
    )
    chunks = lax.all_to_all(chunks, "grp", split_axis=0, concat_axis=0, tiled=True)
    ends_size = full_z // n_wide
    coef, ends, small = call(
        functools.partial(forward_z_body, rows_y),
        [
            ((rows_y // 2, full_z, lanes), f32),
            ((3, full_z, lanes), f32),
            ((n_wide, ends_size + n_grp + 8, lanes), f32),
        ],
        [chunks, z_high, z_low, full],
        name="forward_z",
    )
    small = lax.all_to_all(small, "wide", split_axis=0, concat_axis=0, tiled=True)
    (reach,) = call(
        ring_body, [((n_wide, ends_size, lanes), f32)], [small, small_table], name="ring"
    )
    reach = lax.all_to_all(reach, "wide", split_axis=0, concat_axis=0, tiled=True)
    place = (jnp.arange(lanes, dtype=jnp.int32) - my_wide)[None, :]
    marker_force, mine = call(
        functools.partial(unpack_body, n_grp, n_wide * rows_y, length_x * depth_z * n_grp),
        [((4, held), f32), ((lanes, lanes), f32)],
        [owner, rank, small, place],
        name="unpack",
    )
    (chunks,) = call(
        functools.partial(backward_z_body, rows_y),
        [((n_grp, back_rows, lanes), f32)],
        [coef, ends, reach, full, zt_high, zt_low],
        [
            pltpu.VMEM((rows_y // 2, full_z, lanes), f32),
            pltpu.VMEM((2, full_z // 2, lanes), f32),
        ],
        name="backward_z",
    )
    chunks = lax.all_to_all(chunks, "grp", split_axis=0, concat_axis=0, tiled=True)
    velocity_out, scalar_out = call(
        last_body,
        [(velocity.shape, f32), (scalar.shape, f32)],
        [chunks, forced, mine, xt_high, xt_low],
        [pltpu.VMEM((with_edges, length_x), f32), pltpu.VMEM((with_edges, length_x), f32)],
        name="last",
    )
    return velocity_out, scalar_out, marker_force


def solution(mesh):
    n_wide, n_grp = mesh.shape["wide"], mesh.shape["grp"]
    rows_y, full_z, length_x = 48, 128, 512
    basis_x, squares_x = real_basis(length_x)
    basis_z, squares_z = real_basis(full_z)
    parts = (
        two_parts(basis_x)
        + two_parts(basis_x.T)
        + two_parts(basis_z.T)
        + two_parts(basis_z)
        + decay_tables(squares_x, squares_z, n_grp, n_wide, rows_y)
    )

    def whole(*args):
        tables = tuple(jnp.asarray(part) for part in parts)
        return per_device(tables, *args)

    return jax.shard_map(
        whole,
        mesh=mesh,
        in_specs=(
            P(None, "wide", "grp", None),
            P("wide", "grp", None),
            P(("wide", "grp")),
            P(("wide", "grp")),
            P(("wide", "grp")),
            P(None, ("wide", "grp")),
            P(("wide", "grp")),
        ),
        out_specs=(P(None, "wide", "grp", None), P("wide", "grp", None), P(None, ("wide", "grp"))),
        check_vma=False,
    )
```

```python
import functools
import math

import jax
import jax.numpy as jnp
import ml_dtypes
import numpy as np
from jax import lax
from jax.experimental import pallas as pl
from jax.experimental.pallas import tpu as pltpu
from jax.sharding import PartitionSpec as P

time_step = 0.1
viscosity = 0.4
diffusivity = 0.25
f32 = jnp.float32
bf16 = jnp.bfloat16
lanes = 128
slots = 32
vmem = pl.BlockSpec(memory_space=pltpu.VMEM)
hbm = pl.BlockSpec(memory_space=pltpu.HBM)


def iota(shape, dim):
    return lax.broadcasted_iota(jnp.int32, shape, dim)


def call(body, out, args, scratch=(), name=None, micros=0, far_in=(), far_out=(), room=0):
    shapes = [jax.ShapeDtypeStruct(s, d) for s, d in out]
    moved = sum(a.size * a.dtype.itemsize for a in args)
    moved += sum(s.size * s.dtype.itemsize for s in shapes)
    near = [a for i, a in enumerate(args) if i not in far_in]
    near += [s for i, s in enumerate(shapes) if i not in far_out]
    held = sum(a.size * a.dtype.itemsize for a in near)
    held += sum(math.prod(s.shape) * 4 for s in scratch if s.shape)
    moved = max(moved, micros * 3000000)
    return pl.pallas_call(
        body,
        out_shape=shapes,
        in_specs=[hbm if i in far_in else vmem for i in range(len(args))],
        out_specs=[hbm if i in far_out else vmem for i in range(len(out))],
        scratch_shapes=list(scratch),
        compiler_params=pltpu.CompilerParams(vmem_limit_bytes=max(held + 6 * 2**20, room * 2**20)),
        cost_estimate=pl.CostEstimate(flops=0, bytes_accessed=moved, transcendentals=0),
        name=name,
    )(*args)


def passed_along(value, axis, steps):
    count = lax.axis_size(axis)
    return lax.ppermute(value, axis, [(i, (i + steps) % count) for i in range(count)])


def real_basis(length):
    place = np.arange(length)
    columns, squares = [], []
    for k in range(length // 2 + 1):
        angle = 2.0 * np.pi * ((k * place) % length) / length
        scale = math.sqrt((1.0 if k in (0, length // 2) else 2.0) / length)
        square = 4.0 * math.sin(math.pi * k / length) ** 2
        columns.append(scale * np.cos(angle))
        squares.append(square)
        if k not in (0, length // 2):
            columns.append(scale * np.sin(angle))
            squares.append(square)
    return np.stack(columns, axis=1), np.array(squares)


def two_parts(table):
    high = table.astype(np.float32).astype(ml_dtypes.bfloat16)
    low = (table - high.astype(np.float64)).astype(np.float32).astype(ml_dtypes.bfloat16)
    return high, low


def decay_tables(squares_x, squares_z, n_grp, n_wide, rows_y):
    full_y = n_wide * rows_y
    local = squares_x.shape[0] // n_grp
    square = squares_z[None, :, None] + squares_x.reshape(n_grp, 1, local)
    mean_mode = square == 0.0
    safe = np.where(mean_mode, 1.0, square)
    root = 1.0 / (1.0 + safe / 2.0 + np.sqrt(safe + safe * safe / 4.0))
    root = np.where(mean_mode, 0.0, root)
    gain = np.where(mean_mode, 0.0, -root / (1.0 - root * root))
    half = rows_y // 2
    full = np.stack([root, root**half, gain], axis=1)
    full = np.concatenate([full, full], axis=3)
    device = root**rows_y
    small = np.stack([device, 1.0 / (1.0 - root**full_y)], axis=1)
    upper = small.shape[2] // 2
    small = np.concatenate([small[:, :, :upper], small[:, :, upper:]], axis=3)
    share = upper // n_wide
    small = small.reshape(n_grp, 2, n_wide, share, 2 * local).transpose(0, 2, 1, 3, 4)
    small = np.concatenate([small, small], axis=3)
    return full.astype(np.float32), small.astype(np.float32)


def split_two(value):
    high = value.astype(bf16)
    return high, (value - high.astype(f32)).astype(bf16)


def split_three(value):
    high = value.astype(bf16)
    rest = value - high.astype(f32)
    middle = rest.astype(bf16)
    return high, middle, (rest - middle.astype(f32)).astype(bf16)


def dot(left, right, dims=((1,), (0,))):
    return lax.dot_general(left, right, (dims, ((), ())), preferred_element_type=f32)


def pack_body(*refs):
    far, near, sems = refs[:7], refs[13:20], refs[20]
    send_ref, rank_ref, y_first, y_last, z_first, z_last = refs[7:13]
    owner_ref, tile_ref, offset_ref, target_ref, eta_ref, vel_ref, scal_ref = near
    copies = [pltpu.make_async_copy(a, b, sems.at[i]) for i, (a, b) in enumerate(zip(far, near))]
    for copy in copies:
        copy.start()
    for copy in copies[:5]:
        copy.wait()
    pack_markers(owner_ref, tile_ref, offset_ref, target_ref, eta_ref, send_ref, rank_ref)
    for copy in copies[5:]:
        copy.wait()
    rows_y, depth_z, _ = scal_ref.shape

    def edges(y, carry):
        for z, out in ((0, z_first), (depth_z - 1, z_last)):
            for f in range(3):
                out[f, pl.ds(y, 1), :] = vel_ref[f, y, z : z + 1, :]
            out[3, pl.ds(y, 1), :] = scal_ref[y, z : z + 1, :]
        return carry

    lax.fori_loop(0, rows_y, edges, 0)
    for y, out in ((0, y_first), (rows_y - 1, y_last)):
        for f in range(3):
            out[f] = vel_ref[f, y]
        out[3] = scal_ref[y]


def pack_markers(owner_ref, tile_ref, offset_ref, target_ref, eta_ref, send_ref, rank_ref):
    owners = send_ref.shape[0]
    held = owner_ref.shape[1]
    onehot = owner_ref[...] == iota((owners, held), 0)
    onehot = jnp.where(onehot, 1.0, 0.0)
    upto = jnp.where(iota((lanes, lanes), 0) <= iota((lanes, lanes), 1), 1.0, 0.0).astype(bf16)
    carry = jnp.zeros((owners, 1), f32)
    ranks = []
    for start in range(0, held, lanes):
        piece = onehot[:, start : start + lanes]
        running = dot(piece.astype(bf16), upto) + carry
        ranks.append(jnp.sum(running * piece, axis=0, keepdims=True) - 1.0)
        carry = carry + jnp.sum(piece, axis=1, keepdims=True)
    rank = jnp.concatenate(ranks, axis=1).astype(jnp.int32)
    rank_ref[...] = rank
    chosen = rank == iota((slots, held), 0)
    cell = (tile_ref[...] * lanes + offset_ref[...]).astype(f32)
    values = [target_ref[k : k + 1, :] for k in range(4)] + [eta_ref[...], cell]
    onehot = onehot.astype(bf16)
    total = jnp.zeros((owners, 6 * slots), f32)
    for part in range(3):
        rows = [
            jnp.where(chosen, split_three(v)[part].astype(f32), 0.0).astype(bf16) for v in values
        ]
        total = total + dot(onehot, jnp.concatenate(rows, axis=0), ((1,), (1,)))
    column = iota((owners, 2 * lanes), 1)
    slot = column - 5 * slots
    spare = (slot >= 0) & (slot < slots) & (slot.astype(f32) >= carry)
    total = jnp.concatenate([total, jnp.zeros((owners, 2 * lanes - 6 * slots), f32)], axis=1)
    send_ref[...] = total + jnp.where(spare, (slot * lanes).astype(f32), 0.0)


def unpack_body(
    n_grp, all_rows, row_cells, owner_ref, rank_ref, back_ref, place_ref, force_ref, mean_ref
):
    size = back_ref.shape[1] // 3
    owners = back_ref.shape[0] * n_grp
    held = owner_ref.shape[1]
    onehot = jnp.where(owner_ref[...] == iota((owners, held), 0), 1.0, 0.0).astype(bf16)
    sums = back_ref[:, 2 * size, :]
    sums = jnp.concatenate([sums, jnp.zeros((lanes - sums.shape[0], lanes), f32)], axis=0).T
    mine = jnp.where(place_ref[...] == 0, sums, 0.0)
    mean = jnp.sum(jnp.sum(sums, axis=1, keepdims=True), axis=0, keepdims=True)
    mine = jnp.sum(mine, axis=1, keepdims=True) * (1.0 / row_cells)
    mean_ref[...] = jnp.broadcast_to(mine - mean * (1.0 / (all_rows * row_cells)), mean_ref.shape)
    back = back_ref[:, size : 2 * size, :].reshape(owners, lanes).T
    spread = sum(dot(part, onehot) for part in split_three(back))
    chosen = rank_ref[...] == iota((slots, held), 0)
    for k in range(4):
        piece = jnp.where(chosen, spread[k * slots : (k + 1) * slots], 0.0)
        force_ref[k : k + 1, :] = jnp.sum(piece, axis=0, keepdims=True)


def swap_groups(value):
    row = iota(value.shape, 0) & 3
    group = lax.shift_right_logical(iota(value.shape, 1), 5)
    count = value.shape[0]
    out = value
    for k in (1, 2, 3):
        moved = pltpu.roll(value, 32 * k, 1)
        moved = jnp.where(
            row + k < 4, pltpu.roll(moved, count - k, 0), pltpu.roll(moved, 4 - k, 0)
        )
        out = jnp.where(((group - row) & 3) == k, moved, out)
    return out


def marker_part(recv_ref, out_ref, force_ref, samp, table, index, sem, tiles_x, depth_z):
    sources = recv_ref.shape[0]
    wide_lane = iota((sources, lanes), 1)
    second = recv_ref[:, lanes : 2 * lanes]
    cell = pltpu.roll(second.astype(jnp.int32), lanes - 32, 1)
    tile = lax.shift_right_logical(cell, 7)
    shift_x = tiles_x.bit_length() - 1
    shift_z = shift_x + depth_z.bit_length() - 1
    row = lax.shift_right_logical(tile, shift_z) * tiles_x + (tile & (tiles_x - 1))
    row = row * depth_z + (lax.shift_right_logical(tile, shift_x) & (depth_z - 1))
    spot = (iota((sources, lanes), 0) & 3) * 32 + (wide_lane & 31)
    there = (spot - cell) & (lanes - 1)
    back = (cell - spot) & (lanes - 1)
    table[...] = jnp.where(
        wide_lane < 32,
        4 * row,
        jnp.where(wide_lane < 64, pltpu.roll(there, 32, 1), pltpu.roll(back, 64, 1)),
    )
    copy = pltpu.make_async_copy(table, index, sem)
    copy.start()
    copy.wait()
    lane = iota((4, lanes), 1)

    def at(place):
        return pl.ds(pl.multiple_of(place, 4), 4)

    def gather(batch, carry):
        found = jnp.zeros((4, lanes), f32)
        for q in range(4):
            for r in range(slots):
                source = 4 * batch + q
                value = out_ref[at(index[source, r]), :]
                value = pltpu.roll(value, index[source, 32 + r], 1)
                found = jnp.where(lane == 32 * q + r, value, found)
        samp[pl.ds(pl.multiple_of(4 * batch, 4), 4), :] = found
        return carry

    lax.fori_loop(0, sources // 4, gather, 0)
    eta = jnp.where(wide_lane < 32, second, 0.0)
    eta = eta + pltpu.roll(eta, 32, 1)
    eta = eta + pltpu.roll(eta, 64, 1)
    force = swap_groups(eta) * (swap_groups(recv_ref[:, 0:lanes]) - samp[...])
    samp[...] = force
    force_ref[...] = swap_groups(force)

    def scatter(batch, carry):
        mine = samp[pl.ds(pl.multiple_of(4 * batch, 4), 4), :]
        for sub in range(4):
            source = 4 * batch + sub
            terms = []
            for r in range(slots):
                only = jnp.where(lane == 32 * sub + r, mine, 0.0)
                terms.append(pltpu.roll(only, index[source, 64 + r], 1))
            for q in range(0, slots, 4):
                places = [index[source, q + j] for j in range(4)]
                values = [out_ref[at(place), :] for place in places]
                for j in range(4):
                    for i in range(j):
                        values[j] = jnp.where(places[i] == places[j], values[i], values[j])
                    values[j] = values[j] + terms[q + j]
                for j in range(4):
                    out_ref[at(places[j]), :] = values[j]
        return carry

    lax.fori_loop(0, sources // 4, scatter, 0)


def at_row(y, x, f, tiles_x, depth_z):
    return pl.ds((y * tiles_x + x) * (4 * depth_z) + f, depth_z, stride=4)


def stencil_part(
    vel_far, scal_far, ylo_ref, yhi_ref, zlo_ref, zhi_ref, vel_ref, scal_ref, out_ref, sems
):
    _, rows_y, depth_z, length_x = vel_ref.shape
    tiles_x = length_x // lanes
    level = iota((depth_z, length_x), 0)

    def one_row(y, carry):
        at_low = y == 0
        at_high = y == rows_y - 1
        below = jnp.maximum(y - 1, 0)
        above = jnp.minimum(y + 1, rows_y - 1)
        flow = [vel_ref[f, y] for f in range(3)]
        for f in range(4):
            if f < 3:
                center = flow[f]
                low, high = vel_ref[f, below], vel_ref[f, above]
            else:
                center = scal_ref[y]
                low, high = scal_ref[below], scal_ref[above]
            south = jnp.where(at_low, ylo_ref[f], low)
            north = jnp.where(at_high, yhi_ref[f], high)
            east = pltpu.roll(center, length_x - 1, 1)
            west = pltpu.roll(center, 1, 1)
            top = jnp.broadcast_to(zhi_ref[f, pl.ds(y, 1), :], center.shape)
            bottom = jnp.broadcast_to(zlo_ref[f, pl.ds(y, 1), :], center.shape)
            upper = jnp.where(level == depth_z - 1, top, pltpu.roll(center, depth_z - 1, 0))
            lower = jnp.where(level == 0, bottom, pltpu.roll(center, 1, 0))
            transport = (
                flow[0] * (east - west) + flow[1] * (north - south) + flow[2] * (upper - lower)
            )
            around = east + west + north + south + upper + lower
            coeff = viscosity if f < 3 else diffusivity
            star = (
                center * (1.0 - 6.0 * time_step * coeff)
                + (time_step * coeff) * around
                - (0.5 * time_step) * transport
            )
            for x in range(tiles_x):
                out_ref[at_row(y, x, f, tiles_x, depth_z), :] = star[:, x * lanes : (x + 1) * lanes]
        return carry

    pieces = sems.shape[0] // 2
    size = rows_y // pieces
    fetches = []
    for piece in range(pieces):
        part = pl.ds(piece * size, size)
        fetches.append(
            [
                pltpu.make_async_copy(
                    vel_far.at[:, part], vel_ref.at[:, part], sems.at[2 * piece]
                ),
                pltpu.make_async_copy(
                    scal_far.at[part], scal_ref.at[part], sems.at[2 * piece + 1]
                ),
            ]
        )
        for copy in fetches[-1]:
            copy.start()
    for copy in fetches[0]:
        copy.wait()
    for piece in range(pieces):
        for copy in fetches[piece + 1] if piece + 1 < pieces else ():
            copy.wait()
        lax.fori_loop(piece * size, (piece + 1) * size, one_row, 0)


def wide_row(ref, f, y, tiles_x, depth_z):
    return jnp.concatenate(
        [ref[at_row(y, x, f, tiles_x, depth_z), :] for x in range(tiles_x)], axis=1
    )


def packed_rows(rows_y, depth_z, n_wide):
    cells = rows_y // 2 * depth_z
    row = cells + depth_z // 2
    plane = row + rows_y // 2
    return cells, row, plane, plane + n_wide, plane + n_wide + 8


partners = (4, 5, 2, 3, 6, 7, 1, 0)


def by_partner(ref, parts):
    mine = lax.axis_index("grp")
    for d, part in zip(partners, parts):
        part[...] = ref[jnp.bitwise_xor(mine, d)]


def from_partner(parts, ref):
    mine = lax.axis_index("grp")
    for d, part in zip(partners, parts):
        ref[jnp.bitwise_xor(mine, d)] = part[...]


def exchanged(parts):
    count = len(parts)
    return [
        part if d == 0 else lax.ppermute(part, "grp", [(i, i ^ d) for i in range(count)])
        for d, part in zip(partners, parts)
    ]


def halves(one, two, first_half):
    even = jnp.where(first_half, one, pltpu.roll(two, lanes // 2, 1))
    odd = jnp.where(first_half, pltpu.roll(one, lanes // 2, 1), two)
    return even, odd


def times_x(value, high_ref, low_ref):
    high, low = split_two(value)
    return dot(high, high_ref[...]) + dot(low, high_ref[...]) + dot(high, low_ref[...])


def divergence_part(forced_ref, div, sums, shape):
    rows_y, depth_z, length_x = shape
    tiles_x = length_x // lanes
    rows = rows_y * depth_z
    level = iota((depth_z, length_x), 0)
    sums[...] = jnp.zeros_like(sums)

    def one_row(y, carry):
        after = jnp.minimum(y + 1, rows_y - 1)
        along = wide_row(forced_ref, 0, y, tiles_x, depth_z)
        second = wide_row(forced_ref, 1, y, tiles_x, depth_z)
        third = wide_row(forced_ref, 2, y, tiles_x, depth_z)
        north = wide_row(forced_ref, 1, after, tiles_x, depth_z)
        north = jnp.where(y == rows_y - 1, 0.0, north)
        upper = jnp.where(level == depth_z - 1, 0.0, pltpu.roll(third, depth_z - 1, 0))
        total = pltpu.roll(along, length_x - 1, 1) - along + (north - second) + (upper - third)
        div[pl.ds(pl.multiple_of(y * depth_z, depth_z), depth_z), :] = total
        div[pl.ds(rows + depth_z + y, 1), :] = third[0:1, :]
        folded = sum(second[:, x * lanes : (x + 1) * lanes] for x in range(tiles_x))
        sums[pl.ds(y, 1), :] = jnp.sum(folded, axis=0, keepdims=True)
        return carry

    lax.fori_loop(0, rows_y, one_row, 0)
    div[rows : rows + depth_z, :] = wide_row(forced_ref, 1, 0, tiles_x, depth_z)


def first_body(shape, *refs):
    vel_far, scal_far, ylo, yhi, zlo, zhi, recv_ref, high_ref, low_ref, far_ref, *rest = refs
    out_refs, rest = rest[:-13], rest[-13:]
    vel_ref, scal_ref, sems, forced_ref, out_ref, *rest = rest
    force, samp, table, div, modes, index, sem, far_sem = rest
    rows_y, depth_z, length_x = shape
    n_grp = out_ref.shape[0]
    n_wide = recv_ref.shape[0] // n_grp
    rows = rows_y * depth_z
    tiles_x = length_x // lanes
    stencil_part(vel_far, scal_far, ylo, yhi, zlo, zhi, vel_ref, scal_ref, forced_ref, sems)
    marker_part(recv_ref, forced_ref, force, samp, table, index, sem, tiles_x, depth_z)
    keep = pltpu.make_async_copy(forced_ref, far_ref, far_sem)
    keep.start()
    divergence_part(forced_ref, div, samp, (rows_y, depth_z, length_x))
    chunk = div.shape[0] // 4
    for start in range(0, 4 * chunk, chunk):
        modes[start : start + chunk, :] = times_x(div[start : start + chunk, :], high_ref, low_ref)
    row, plane, forces, sums_row, end = packed_rows(rows_y, depth_z, n_wide)

    def send(front, back, size, place):
        first_half = iota((size, lanes), 1) < lanes // 2
        for j in range(n_grp // 2):
            one = modes[pl.ds(front, size), j * lanes : (j + 1) * lanes]
            two = modes[pl.ds(back, size), j * lanes : (j + 1) * lanes]
            even, odd = halves(one, two, first_half)
            out_ref[2 * j, pl.ds(place, size), :] = even
            out_ref[2 * j + 1, pl.ds(place, size), :] = odd

    def shuffle(y, carry):
        front = pl.multiple_of(y * depth_z, depth_z)
        back = pl.multiple_of((y + rows_y // 2) * depth_z, depth_z)
        send(front, back, depth_z, front)
        return carry

    lax.fori_loop(0, rows_y // 2, shuffle, 0)
    send(rows, rows + depth_z // 2, depth_z // 2, row)
    send(rows + depth_z, rows + depth_z + rows_y // 2, rows_y // 2, plane)
    total = jnp.broadcast_to(jnp.sum(samp[...].T, axis=0, keepdims=True), (end - sums_row, lanes))
    for g in range(n_grp):
        out_ref[g, forces:sums_row, :] = force[pl.ds(g, n_wide, stride=n_grp), :]
        out_ref[g, sums_row:end, :] = total
    by_partner(out_ref, out_refs)
    keep.wait()


def times_z(value, high_ref, low_ref):
    high, low = split_two(value)
    return dot(high_ref[...], high) + dot(high_ref[...], low) + dot(low_ref[...], high)


def forward_z_body(rows_y, *refs):
    recv_refs, refs = refs[:-7], refs[-7:]
    high_ref, low_ref, table_ref, coef_ref, ends_ref, small_ref, recv_ref = refs
    n_grp = recv_ref.shape[0]
    from_partner(recv_refs, recv_ref)
    n_wide = small_ref.shape[0]
    steps, full_z, _ = coef_ref.shape
    depth_z = full_z // n_grp
    row, plane, forces, sums_row, end = packed_rows(rows_y, depth_z, n_wide)
    root = table_ref[0]
    last = iota((n_grp, depth_z, lanes), 1) == depth_z - 1
    first_half = iota((full_z, lanes), 1) < lanes // 2

    def cells_of(step):
        value = recv_ref[:, pl.ds(pl.multiple_of(step * depth_z, depth_z), depth_z), :]
        edge = recv_ref[:, pl.ds(plane + step, 1), :]
        edge = jnp.concatenate([edge[1:], edge[:1]], axis=0)
        value = value + jnp.where(last, jnp.broadcast_to(edge, value.shape), 0.0)
        return value.reshape(full_z, lanes)

    def one_pair(pair, total):
        value = jnp.concatenate([cells_of(2 * pair), cells_of(2 * pair + 1)], axis=1)
        found = times_z(value, high_ref, low_ref)
        coef_ref[2 * pair] = found[:, :lanes]
        coef_ref[2 * pair + 1] = found[:, lanes:]
        return found[:, lanes:] + root * (found[:, :lanes] + root * total)

    packed = recv_ref[:, row:plane, :]
    other = jnp.stack([pltpu.roll(packed[g], lanes // 2, 1) for g in range(n_grp)], axis=0)
    extra = jnp.concatenate([packed, other], axis=1).reshape(full_z, lanes)
    extra = jnp.where(first_half, times_z(extra, high_ref, low_ref), 0.0)
    ends_ref[2] = extra
    up = lax.fori_loop(0, steps // 2, one_pair, extra)
    down = lax.fori_loop(
        0,
        steps,
        lambda i, total: coef_ref[steps - 1 - i] + root * total,
        jnp.zeros((full_z, lanes), f32),
    )
    down = root * down
    ends_ref[0] = up
    ends_ref[1] = down
    over = table_ref[1]
    up_other = pltpu.roll(up, lanes // 2, 1)
    down_other = pltpu.roll(down, lanes // 2, 1)
    up = jnp.where(first_half, up_other + over * up, up + over * up_other)
    down = jnp.where(first_half, down + over * down_other, down_other + over * down)
    down = down + extra + pltpu.roll(extra, lanes // 2, 1)
    upper = full_z // 2
    share = upper // n_wide
    for k, value in enumerate((up, down)):
        value = jnp.where(first_half[:upper], value[:upper], value[upper:])
        for i in range(n_wide):
            small_ref[i, k * share : (k + 1) * share, :] = value[i * share : (i + 1) * share]
    sums = sum(recv_ref[g, sums_row:end, :] for g in range(n_grp))
    for i in range(n_wide):
        for g in range(n_grp):
            place = 2 * share + g
            small_ref[i, place : place + 1, :] = recv_ref[g, forces + i : forces + i + 1, :]
        small_ref[i, 2 * share + n_grp : 2 * share + n_grp + 8, :] = sums


def widen(small):
    first_half = iota(small.shape, 1) < lanes // 2
    other = pltpu.roll(small, lanes // 2, 1)
    return jnp.concatenate(
        [jnp.where(first_half, small, other), jnp.where(first_half, other, small)], axis=0
    )


def backward_z_body(
    rows_y, coef_ref, ends_ref, small_ref, table_ref, high_ref, low_ref, *rest
):
    out_refs, rest = rest[:-3], rest[-3:]
    out_ref, ups, small = rest
    n_grp = out_ref.shape[0]
    steps, full_z, _ = coef_ref.shape
    depth_z = full_z // n_grp
    row, plane, _, _, _ = packed_rows(rows_y, depth_z, small_ref.shape[0])
    root, over, gain = table_ref[0], table_ref[1], table_ref[2]
    first_half = iota((full_z, lanes), 1) < lanes // 2
    share = small_ref.shape[1] // 2
    for i in range(small_ref.shape[0]):
        for k in range(2):
            small[k, i * share : (i + 1) * share] = small_ref[i, k * share : (k + 1) * share]
    up_in = widen(small[0])
    down_in = widen(small[1])
    up_start = jnp.where(
        first_half,
        up_in + ends_ref[2],
        pltpu.roll(ends_ref[0], lanes // 2, 1) + over * up_in,
    )
    down = jnp.where(
        first_half, pltpu.roll(ends_ref[1], lanes // 2, 1) + over * down_in, down_in
    )

    def rising(step, total):
        total = coef_ref[step] + root * total
        ups[step] = total
        return total

    lax.fori_loop(0, steps, rising, up_start)

    def falling(i, total):
        pair = steps // 2 - 1 - i
        second = gain * (ups[2 * pair + 1] + total)
        total = root * (coef_ref[2 * pair + 1] + total)
        first = gain * (ups[2 * pair] + total)
        total = root * (coef_ref[2 * pair] + total)
        found = times_z(jnp.concatenate([first, second], axis=1), high_ref, low_ref)
        for j in range(2):
            step = 2 * pair + j
            value = found[:, j * lanes : (j + 1) * lanes]
            start = pl.multiple_of(step * depth_z, depth_z)
            out_ref[:, pl.ds(start, depth_z), :] = value.reshape(n_grp, depth_z, lanes)
            for g in range(n_grp):
                before = (g * depth_z - 1) % full_z
                out_ref[g, pl.ds(plane + step, 1), :] = value[before : before + 1, :]
        return total

    down = lax.fori_loop(0, steps // 2, falling, down)
    extra = times_z(gain * (up_start + down), high_ref, low_ref)
    half = depth_z // 2
    for g in range(n_grp):
        start = g * depth_z
        out_ref[g, row:plane, :] = jnp.where(
            first_half[:half],
            extra[start : start + half],
            pltpu.roll(extra[start + half : start + depth_z], lanes // 2, 1),
        )
    by_partner(out_ref, out_refs)


def last_body(far_ref, mean_ref, high_ref, low_ref, *refs):
    recv_refs, refs = refs[:-10], refs[-10:]
    vel_far, scal_far, vel_ref, scal_ref, recv_ref, forced_ref, modes, press_ref, sem, sems = refs
    fetch = pltpu.make_async_copy(far_ref, forced_ref, sem)
    fetch.start()
    from_partner(recv_refs, recv_ref)
    n_grp = recv_ref.shape[0]
    _, rows_y, depth_z, length_x = vel_ref.shape
    rows = rows_y * depth_z
    tiles_x = length_x // lanes
    row, plane, _, _, _ = packed_rows(rows_y, depth_z, 0)

    def take(front, back, size, place):
        first_half = iota((size, lanes), 1) < lanes // 2
        for j in range(n_grp // 2):
            even = recv_ref[2 * j, pl.ds(place, size), :]
            odd = recv_ref[2 * j + 1, pl.ds(place, size), :]
            one, two = halves(even, odd, first_half)
            modes[pl.ds(front, size), j * lanes : (j + 1) * lanes] = one
            modes[pl.ds(back, size), j * lanes : (j + 1) * lanes] = two

    def shuffle(y, carry):
        front = pl.multiple_of(y * depth_z, depth_z)
        back = pl.multiple_of((y + rows_y // 2) * depth_z, depth_z)
        take(front, back, depth_z, front)
        return carry

    lax.fori_loop(0, rows_y // 2, shuffle, 0)
    take(rows, rows + depth_z // 2, depth_z // 2, row)
    take(rows + depth_z, rows + depth_z + rows_y // 2, rows_y // 2, plane)
    chunk = modes.shape[0] // 4
    for start in range(0, 4 * chunk, chunk):
        press_ref[start : start + chunk, :] = times_x(
            modes[start : start + chunk, :], high_ref, low_ref
        )
    level = iota((depth_z, length_x), 0)

    def one_row(y, carry):
        start = pl.multiple_of(y * depth_z, depth_z)
        before = pl.multiple_of(jnp.where(y == 0, rows, start - depth_z), depth_z)
        press = press_ref[pl.ds(start, depth_z), :]
        south = press_ref[pl.ds(before, depth_z), :]
        below = jnp.broadcast_to(press_ref[pl.ds(rows + depth_z + y, 1), :], press.shape)
        lower = jnp.where(level == 0, below, pltpu.roll(press, 1, 0))
        west = pltpu.roll(press, 1, 1)
        mean = mean_ref[pl.ds(y, 1), :]
        mean = jnp.concatenate([mean] * tiles_x, axis=1)
        vel_ref[0, y] = wide_row(forced_ref, 0, y, tiles_x, depth_z) - (press - west)
        vel_ref[1, y] = wide_row(forced_ref, 1, y, tiles_x, depth_z) - (press - south) - mean
        vel_ref[2, y] = wide_row(forced_ref, 2, y, tiles_x, depth_z) - (press - lower)
        scal_ref[y] = wide_row(forced_ref, 3, y, tiles_x, depth_z)
        return carry

    fetch.wait()
    pieces = sems.shape[0] // 2
    size = rows_y // pieces
    copies = []
    for piece in range(pieces):
        lax.fori_loop(piece * size, (piece + 1) * size, one_row, 0)
        part = pl.ds(piece * size, size)
        copies += [
            pltpu.make_async_copy(
                vel_ref.at[:, part], vel_far.at[:, part], sems.at[2 * piece]
            ),
            pltpu.make_async_copy(
                scal_ref.at[part], scal_far.at[part], sems.at[2 * piece + 1]
            ),
        ]
        copies[-2].start()
        copies[-1].start()
    for copy in copies:
        copy.wait()


def ring_body(recv_ref, table_ref, out_ref):
    count, size, _ = out_ref.shape
    rising = iota((size, lanes), 0) < size // 2
    ends = [
        jnp.where(rising, recv_ref[i, 0:size, :], recv_ref[count - 1 - i, 0:size, :])
        for i in range(count)
    ]
    step, whole = table_ref[0], table_ref[1]
    total = ends[0]
    for i in range(1, count):
        total = ends[i] + step * total
    total = whole * total
    reached = []
    for i in range(count):
        reached.append(total)
        total = ends[i] + step * total
    for i in range(count):
        out_ref[i] = jnp.where(rising, reached[i], reached[count - 1 - i])


def per_device(
    tables, velocity, scalar, marker_owner, marker_tile, marker_offset, marker_target, marker_eta
):
    _, rows_y, depth_z, length_x = velocity.shape
    n_wide = lax.axis_size("wide")
    n_grp = lax.axis_size("grp")
    owners = n_wide * n_grp
    full_z = depth_z * n_grp
    rows = rows_y * depth_z
    tiles_x = length_x // lanes
    held = marker_owner.shape[0]
    x_high, x_low, xt_high, xt_low, fz_high, fz_low, bz_high, bz_low, full, small_table = tables
    my_grp = lax.axis_index("grp")
    my_wide = lax.axis_index("wide")
    full = lax.dynamic_index_in_dim(full, my_grp, 0, keepdims=False)
    small_table = lax.dynamic_slice(
        small_table, (my_grp, my_wide, 0, 0, 0), (1, 1) + small_table.shape[2:]
    )[0, 0]

    owner = marker_owner[None, :]
    send, rank, y_first, y_last, z_first, z_last = call(
        pack_body,
        [((owners, 2 * lanes), f32), ((1, held), jnp.int32)]
        + [((4, depth_z, length_x), f32)] * 2
        + [((4, rows_y, length_x), f32)] * 2,
        [
            owner,
            marker_tile[None, :],
            marker_offset[None, :],
            marker_target,
            marker_eta[None, :],
            velocity,
            scalar,
        ],
        [
            pltpu.VMEM((1, held), jnp.int32),
            pltpu.VMEM((1, held), jnp.int32),
            pltpu.VMEM((1, held), jnp.int32),
            pltpu.VMEM((4, held), f32),
            pltpu.VMEM((1, held), f32),
            pltpu.VMEM(velocity.shape, f32),
            pltpu.VMEM(scalar.shape, f32),
            pltpu.SemaphoreType.DMA((7,)),
        ],
        name="pack",
        room=58,
        far_in=range(7),
    )
    z_low = passed_along(z_last, "grp", 1)
    z_high = passed_along(z_first, "grp", -1)
    y_low = passed_along(y_last, "wide", 1)
    y_high = passed_along(y_first, "wide", -1)
    recv = lax.all_to_all(send, ("wide", "grp"), split_axis=0, concat_axis=0, tiled=True)
    flat = 4 * tiles_x * rows
    sent_rows = packed_rows(rows_y, depth_z, n_wide)[-1]
    back_rows = packed_rows(rows_y, depth_z, n_wide)[2]
    with_edges = rows + depth_z + rows_y
    forced, *chunks = call(
        functools.partial(first_body, scalar.shape),
        [((flat, lanes), f32)] + [((sent_rows, lanes), f32)] * n_grp,
        [velocity, scalar, y_low, y_high, z_low, z_high, recv, x_high, x_low],
        [
            pltpu.VMEM(velocity.shape, f32),
            pltpu.VMEM(scalar.shape, f32),
            pltpu.SemaphoreType.DMA((8,)),
            pltpu.VMEM((flat, lanes), f32),
            pltpu.VMEM((n_grp, sent_rows, lanes), f32),
            pltpu.VMEM((owners, lanes), f32),
            pltpu.VMEM((owners, lanes), f32),
            pltpu.VMEM((owners, lanes), jnp.int32),
            pltpu.VMEM((with_edges, length_x), f32),
            pltpu.VMEM((with_edges, length_x), f32),
            pltpu.SMEM((owners, lanes), jnp.int32),
            pltpu.SemaphoreType.DMA(()),
            pltpu.SemaphoreType.DMA(()),
        ],
        name="first",
        room=58,
        micros=40,
        far_in=(0, 1),
        far_out=(0,),
    )
    chunks = exchanged(chunks)
    ends_size = full_z // n_wide
    coef, ends, small = call(
        functools.partial(forward_z_body, rows_y),
        [
            ((rows_y // 2, full_z, lanes), f32),
            ((3, full_z, lanes), f32),
            ((n_wide, ends_size + n_grp + 8, lanes), f32),
        ],
        [*chunks, fz_high, fz_low, full],
        [
            pltpu.VMEM((n_grp, sent_rows, lanes), f32),
        ],
        name="forward_z",
    )
    small = lax.all_to_all(small, "wide", split_axis=0, concat_axis=0, tiled=True)
    (reach,) = call(
        ring_body, [((n_wide, ends_size, lanes), f32)], [small, small_table], name="ring"
    )
    reach = lax.all_to_all(reach, "wide", split_axis=0, concat_axis=0, tiled=True)
    place = (jnp.arange(lanes, dtype=jnp.int32) - my_wide)[None, :]
    marker_force, mine = call(
        functools.partial(unpack_body, n_grp, n_wide * rows_y, length_x * depth_z * n_grp),
        [((4, held), f32), ((lanes, lanes), f32)],
        [owner, rank, small, place],
        name="unpack",
    )
    chunks = call(
        functools.partial(backward_z_body, rows_y),
        [((back_rows, lanes), f32)] * n_grp,
        [coef, ends, reach, full, bz_high, bz_low],
        [
            pltpu.VMEM((n_grp, back_rows, lanes), f32),
            pltpu.VMEM((rows_y // 2, full_z, lanes), f32),
            pltpu.VMEM((2, full_z // 2, lanes), f32),
        ],
        name="backward_z",
    )
    chunks = exchanged(chunks)
    velocity_out, scalar_out = call(
        last_body,
        [(velocity.shape, f32), (scalar.shape, f32)],
        [forced, mine, xt_high, xt_low, *chunks],
        [
            pltpu.VMEM(velocity.shape, f32),
            pltpu.VMEM(scalar.shape, f32),
            pltpu.VMEM((n_grp, back_rows, lanes), f32),
            pltpu.VMEM((flat, lanes), f32),
            pltpu.VMEM((with_edges, length_x), f32),
            pltpu.VMEM((with_edges, length_x), f32),
            pltpu.SemaphoreType.DMA(()),
            pltpu.SemaphoreType.DMA((8,)),
        ],
        name="last",
        room=54,
        far_in=(0,),
        far_out=(0, 1),
    )
    return velocity_out, scalar_out, marker_force


def solution(mesh):
    n_wide, n_grp = mesh.shape["wide"], mesh.shape["grp"]
    rows_y, full_z, length_x = 48, 128, 512
    basis_x, squares_x = real_basis(length_x)
    basis_z, squares_z = real_basis(full_z)
    parts = (
        two_parts(basis_x)
        + two_parts(basis_x.T)
        + two_parts(basis_z.T)
        + two_parts(basis_z)
        + decay_tables(squares_x, squares_z, n_grp, n_wide, rows_y)
    )

    def whole(*args):
        tables = tuple(jnp.asarray(part) for part in parts)
        return per_device(tables, *args)

    return jax.shard_map(
        whole,
        mesh=mesh,
        in_specs=(
            P(None, "wide", "grp", None),
            P("wide", "grp", None),
            P(("wide", "grp")),
            P(("wide", "grp")),
            P(("wide", "grp")),
            P(None, ("wide", "grp")),
            P(("wide", "grp")),
        ),
        out_specs=(P(None, "wide", "grp", None), P("wide", "grp", None), P(None, ("wide", "grp"))),
        check_vma=False,
    )
```

```python
import functools
import math

import jax
import jax.numpy as jnp
import ml_dtypes
import numpy as np
from jax import lax
from jax.experimental import pallas as pl
from jax.experimental.pallas import tpu as pltpu
from jax.sharding import PartitionSpec as P

time_step = 0.1
viscosity = 0.4
diffusivity = 0.25
f32 = jnp.float32
bf16 = jnp.bfloat16
lanes = 128
slots = 32
vmem = pl.BlockSpec(memory_space=pltpu.VMEM)
hbm = pl.BlockSpec(memory_space=pltpu.HBM)


def iota(shape, dim):
    return lax.broadcasted_iota(jnp.int32, shape, dim)


def call(body, out, args, scratch=(), name=None, micros=0, far_in=(), far_out=(), room=0):
    shapes = [jax.ShapeDtypeStruct(s, d) for s, d in out]
    moved = sum(a.size * a.dtype.itemsize for a in args)
    moved += sum(s.size * s.dtype.itemsize for s in shapes)
    near = [a for i, a in enumerate(args) if i not in far_in]
    near += [s for i, s in enumerate(shapes) if i not in far_out]
    held = sum(a.size * a.dtype.itemsize for a in near)
    held += sum(math.prod(s.shape) * 4 for s in scratch if s.shape)
    moved = max(moved, micros * 3000000)
    return pl.pallas_call(
        body,
        out_shape=shapes,
        in_specs=[hbm if i in far_in else vmem for i in range(len(args))],
        out_specs=[hbm if i in far_out else vmem for i in range(len(out))],
        scratch_shapes=list(scratch),
        compiler_params=pltpu.CompilerParams(vmem_limit_bytes=max(held + 6 * 2**20, room * 2**20)),
        cost_estimate=pl.CostEstimate(flops=0, bytes_accessed=moved, transcendentals=0),
        name=name,
    )(*args)


def loop(low, high, body, init, by):
    def several(turn, carry):
        for i in range(by):
            carry = body(low + turn * by + i, carry)
        return carry

    return lax.fori_loop(0, (high - low) // by, several, init)


def passed_along(value, axis, steps):
    count = lax.axis_size(axis)
    return lax.ppermute(value, axis, [(i, (i + steps) % count) for i in range(count)])


def real_basis(length):
    place = np.arange(length)
    columns, squares = [], []
    for k in range(length // 2 + 1):
        angle = 2.0 * np.pi * ((k * place) % length) / length
        scale = math.sqrt((1.0 if k in (0, length // 2) else 2.0) / length)
        square = 4.0 * math.sin(math.pi * k / length) ** 2
        columns.append(scale * np.cos(angle))
        squares.append(square)
        if k not in (0, length // 2):
            columns.append(scale * np.sin(angle))
            squares.append(square)
    return np.stack(columns, axis=1), np.array(squares)


def two_parts(table):
    high = table.astype(np.float32).astype(ml_dtypes.bfloat16)
    low = (table - high.astype(np.float64)).astype(np.float32).astype(ml_dtypes.bfloat16)
    return high, low


def decay_tables(squares_x, squares_z, n_grp, n_wide, rows_y):
    full_y = n_wide * rows_y
    local = squares_x.shape[0] // n_grp
    square = squares_z[None, :, None] + squares_x.reshape(n_grp, 1, local)
    mean_mode = square == 0.0
    safe = np.where(mean_mode, 1.0, square)
    root = 1.0 / (1.0 + safe / 2.0 + np.sqrt(safe + safe * safe / 4.0))
    root = np.where(mean_mode, 0.0, root)
    gain = np.where(mean_mode, 0.0, -root / (1.0 - root * root))
    half = rows_y // 2
    full = np.stack([root, root**half, gain], axis=1)
    full = np.concatenate([full, full], axis=3)
    device = root**rows_y
    small = np.stack([device, 1.0 / (1.0 - root**full_y)], axis=1)
    upper = small.shape[2] // 2
    small = np.concatenate([small[:, :, :upper], small[:, :, upper:]], axis=3)
    share = upper // n_wide
    small = small.reshape(n_grp, 2, n_wide, share, 2 * local).transpose(0, 2, 1, 3, 4)
    small = np.concatenate([small, small], axis=3)
    return full.astype(np.float32), small.astype(np.float32)


def split_two(value):
    high = value.astype(bf16)
    return high, (value - high.astype(f32)).astype(bf16)


def split_three(value):
    high = value.astype(bf16)
    rest = value - high.astype(f32)
    middle = rest.astype(bf16)
    return high, middle, (rest - middle.astype(f32)).astype(bf16)


def dot(left, right, dims=((1,), (0,))):
    return lax.dot_general(left, right, (dims, ((), ())), preferred_element_type=f32)


def pack_body(*refs):
    far, near, sems = refs[:7], refs[13:20], refs[20]
    send_ref, rank_ref, y_first, y_last, z_first, z_last = refs[7:13]
    owner_ref, tile_ref, offset_ref, target_ref, eta_ref, vel_ref, scal_ref = near
    copies = [pltpu.make_async_copy(a, b, sems.at[i]) for i, (a, b) in enumerate(zip(far, near))]
    for copy in copies:
        copy.start()
    for copy in copies[:5]:
        copy.wait()
    pack_markers(owner_ref, tile_ref, offset_ref, target_ref, eta_ref, send_ref, rank_ref)
    for copy in copies[5:]:
        copy.wait()
    rows_y, depth_z, _ = scal_ref.shape

    def edges(y, carry):
        for z, out in ((0, z_first), (depth_z - 1, z_last)):
            for f in range(3):
                out[f, pl.ds(y, 1), :] = vel_ref[f, y, z : z + 1, :]
            out[3, pl.ds(y, 1), :] = scal_ref[y, z : z + 1, :]
        return carry

    loop(0, rows_y, edges, 0, 4)
    for y, out in ((0, y_first), (rows_y - 1, y_last)):
        for f in range(3):
            out[f] = vel_ref[f, y]
        out[3] = scal_ref[y]


def pack_markers(owner_ref, tile_ref, offset_ref, target_ref, eta_ref, send_ref, rank_ref):
    owners = send_ref.shape[0]
    held = owner_ref.shape[1]
    onehot = owner_ref[...] == iota((owners, held), 0)
    onehot = jnp.where(onehot, 1.0, 0.0)
    upto = jnp.where(iota((lanes, lanes), 0) <= iota((lanes, lanes), 1), 1.0, 0.0).astype(bf16)
    carry = jnp.zeros((owners, 1), f32)
    ranks = []
    for start in range(0, held, lanes):
        piece = onehot[:, start : start + lanes]
        running = dot(piece.astype(bf16), upto) + carry
        ranks.append(jnp.sum(running * piece, axis=0, keepdims=True) - 1.0)
        carry = carry + jnp.sum(piece, axis=1, keepdims=True)
    rank = jnp.concatenate(ranks, axis=1).astype(jnp.int32)
    rank_ref[...] = rank
    chosen = rank == iota((slots, held), 0)
    cell = (tile_ref[...] * lanes + offset_ref[...]).astype(f32)
    values = [target_ref[k : k + 1, :] for k in range(4)] + [eta_ref[...], cell]
    onehot = onehot.astype(bf16)
    total = jnp.zeros((owners, 6 * slots), f32)
    for part in range(3):
        rows = [
            jnp.where(chosen, split_three(v)[part].astype(f32), 0.0).astype(bf16) for v in values
        ]
        total = total + dot(onehot, jnp.concatenate(rows, axis=0), ((1,), (1,)))
    column = iota((owners, 2 * lanes), 1)
    slot = column - 5 * slots
    spare = (slot >= 0) & (slot < slots) & (slot.astype(f32) >= carry)
    total = jnp.concatenate([total, jnp.zeros((owners, 2 * lanes - 6 * slots), f32)], axis=1)
    send_ref[...] = total + jnp.where(spare, (slot * lanes).astype(f32), 0.0)


def unpack_body(
    n_grp, all_rows, row_cells, owner_ref, rank_ref, back_ref, place_ref, force_ref, mean_ref
):
    size = back_ref.shape[1] // 3
    owners = back_ref.shape[0] * n_grp
    held = owner_ref.shape[1]
    onehot = jnp.where(owner_ref[...] == iota((owners, held), 0), 1.0, 0.0).astype(bf16)
    sums = back_ref[:, 2 * size, :]
    sums = jnp.concatenate([sums, jnp.zeros((lanes - sums.shape[0], lanes), f32)], axis=0).T
    mine = jnp.where(place_ref[...] == 0, sums, 0.0)
    mean = jnp.sum(jnp.sum(sums, axis=1, keepdims=True), axis=0, keepdims=True)
    mine = jnp.sum(mine, axis=1, keepdims=True) * (1.0 / row_cells)
    mean_ref[...] = jnp.broadcast_to(mine - mean * (1.0 / (all_rows * row_cells)), mean_ref.shape)
    back = back_ref[:, size : 2 * size, :].reshape(owners, lanes).T
    spread = sum(dot(part, onehot) for part in split_three(back))
    chosen = rank_ref[...] == iota((slots, held), 0)
    for k in range(4):
        piece = jnp.where(chosen, spread[k * slots : (k + 1) * slots], 0.0)
        force_ref[k : k + 1, :] = jnp.sum(piece, axis=0, keepdims=True)


def swap_groups(value):
    row = iota(value.shape, 0) & 3
    group = lax.shift_right_logical(iota(value.shape, 1), 5)
    count = value.shape[0]
    out = value
    for k in (1, 2, 3):
        moved = pltpu.roll(value, 32 * k, 1)
        moved = jnp.where(
            row + k < 4, pltpu.roll(moved, count - k, 0), pltpu.roll(moved, 4 - k, 0)
        )
        out = jnp.where(((group - row) & 3) == k, moved, out)
    return out


def marker_part(recv_ref, star_ref, out_ref, force_ref, samp, table, index, sem, tiles_x, depth_z):
    sources = recv_ref.shape[0]
    wide_lane = iota((sources, lanes), 1)
    second = recv_ref[:, lanes : 2 * lanes]
    cell = pltpu.roll(second.astype(jnp.int32), lanes - 32, 1)
    tile = lax.shift_right_logical(cell, 7)
    shift_x = tiles_x.bit_length() - 1
    shift_z = shift_x + depth_z.bit_length() - 1
    row = lax.shift_right_logical(tile, shift_z) * tiles_x + (tile & (tiles_x - 1))
    row = row * depth_z + (lax.shift_right_logical(tile, shift_x) & (depth_z - 1))
    spot = (iota((sources, lanes), 0) & 3) * 32 + (wide_lane & 31)
    there = (spot - cell) & (lanes - 1)
    back = (cell - spot) & (lanes - 1)
    table[...] = jnp.where(
        wide_lane < 32,
        4 * row,
        jnp.where(wide_lane < 64, pltpu.roll(there, 32, 1), pltpu.roll(back, 64, 1)),
    )
    copy = pltpu.make_async_copy(table, index, sem)
    copy.start()
    copy.wait()
    lane = iota((4, lanes), 1)

    def at(place):
        return pl.ds(pl.multiple_of(place, 4), 4)

    eta = jnp.where(wide_lane < 32, second, 0.0)
    eta = eta + pltpu.roll(eta, 32, 1)
    eta = eta + pltpu.roll(eta, 64, 1)
    force_ref[...] = swap_groups(eta)
    samp[...] = swap_groups(recv_ref[:, 0:lanes])

    def rows_of(batch):
        return pl.ds(pl.multiple_of(4 * batch, 4), 4)

    def look(source, q, r, found):
        value = star_ref[at(index[source, r]), :]
        value = pltpu.roll(value, index[source, 32 + r], 1)
        return jnp.where(lane == 32 * q + r, value, found)

    def force_of(batch, found):
        force = force_ref[rows_of(batch), :] * (samp[rows_of(batch), :] - found)
        samp[rows_of(batch), :] = force
        return force

    def add(source, q, first, mine):
        places = [index[source, first + j] for j in range(2)]
        values = [out_ref[at(place), :] for place in places]
        terms = []
        for j in range(2):
            only = jnp.where(lane == 32 * q + first + j, mine, 0.0)
            terms.append(pltpu.roll(only, index[source, 64 + first + j], 1))
        values[0] = values[0] + terms[0]
        values[1] = jnp.where(places[0] == places[1], values[0], values[1]) + terms[1]
        for j in range(2):
            out_ref[at(places[j]), :] = values[j]

    def both(batch, mine):
        found = jnp.zeros((4, lanes), f32)
        for q in range(4):
            source = 4 * batch + q
            for first in range(0, slots, 4):
                for r in range(first, first + 4):
                    found = look(source, q, r, found)
                for r in (first, first + 2):
                    add(source - 4, q, r, mine)
        return force_of(batch, found)

    found = jnp.zeros((4, lanes), f32)
    for q in range(4):
        for r in range(slots):
            found = look(q, q, r, found)
    mine = lax.fori_loop(1, sources // 4, both, force_of(0, found))
    for q in range(4):
        for r in range(0, slots, 2):
            add(sources - 4 + q, q, r, mine)
    force_ref[...] = swap_groups(samp[...])


def at_row(y, x, f, tiles_x, depth_z):
    return pl.ds((y * tiles_x + x) * (4 * depth_z) + f, depth_z, stride=4)


def stencil_part(
    vel_far, scal_far, ylo_ref, yhi_ref, zlo_ref, zhi_ref, vel_ref, scal_ref, out_ref, same_ref, sems
):
    _, rows_y, depth_z, length_x = vel_ref.shape
    tiles_x = length_x // lanes
    level = iota((depth_z, length_x), 0)

    def one_row(y, carry):
        at_low = y == 0
        at_high = y == rows_y - 1
        below = jnp.maximum(y - 1, 0)
        above = jnp.minimum(y + 1, rows_y - 1)
        flow = [vel_ref[f, y] for f in range(3)]
        for f in range(4):
            if f < 3:
                center = flow[f]
                low, high = vel_ref[f, below], vel_ref[f, above]
            else:
                center = scal_ref[y]
                low, high = scal_ref[below], scal_ref[above]
            south = jnp.where(at_low, ylo_ref[f], low)
            north = jnp.where(at_high, yhi_ref[f], high)
            east = pltpu.roll(center, length_x - 1, 1)
            west = pltpu.roll(center, 1, 1)
            top = jnp.broadcast_to(zhi_ref[f, pl.ds(y, 1), :], center.shape)
            bottom = jnp.broadcast_to(zlo_ref[f, pl.ds(y, 1), :], center.shape)
            upper = jnp.where(level == depth_z - 1, top, pltpu.roll(center, depth_z - 1, 0))
            lower = jnp.where(level == 0, bottom, pltpu.roll(center, 1, 0))
            transport = (
                flow[0] * (east - west) + flow[1] * (north - south) + flow[2] * (upper - lower)
            )
            around = east + west + north + south + upper + lower
            coeff = viscosity if f < 3 else diffusivity
            star = (
                center * (1.0 - 6.0 * time_step * coeff)
                + (time_step * coeff) * around
                - (0.5 * time_step) * transport
            )
            for x in range(tiles_x):
                place = at_row(y, x, f, tiles_x, depth_z)
                out_ref[place, :] = star[:, x * lanes : (x + 1) * lanes]
                same_ref[place, :] = star[:, x * lanes : (x + 1) * lanes]
        return carry

    pieces = sems.shape[0] // 2
    size = rows_y // pieces
    fetches = []
    for piece in range(pieces):
        part = pl.ds(piece * size, size)
        fetches.append(
            [
                pltpu.make_async_copy(
                    vel_far.at[:, part], vel_ref.at[:, part], sems.at[2 * piece]
                ),
                pltpu.make_async_copy(
                    scal_far.at[part], scal_ref.at[part], sems.at[2 * piece + 1]
                ),
            ]
        )
        for copy in fetches[-1]:
            copy.start()
    for copy in fetches[0]:
        copy.wait()
    for piece in range(pieces):
        for copy in fetches[piece + 1] if piece + 1 < pieces else ():
            copy.wait()
        lax.fori_loop(piece * size, (piece + 1) * size, one_row, 0)


def wide_row(ref, f, y, tiles_x, depth_z):
    return jnp.concatenate(
        [ref[at_row(y, x, f, tiles_x, depth_z), :] for x in range(tiles_x)], axis=1
    )


def packed_rows(rows_y, depth_z, n_wide):
    cells = rows_y // 2 * depth_z
    row = cells + depth_z // 2
    plane = row + rows_y // 2
    return cells, row, plane, plane + n_wide, plane + n_wide + 8


partners = (4, 5, 2, 3, 6, 7, 1, 0)


def by_partner(ref, parts):
    mine = lax.axis_index("grp")
    for d, part in zip(partners, parts):
        part[...] = ref[jnp.bitwise_xor(mine, d)]


def from_partner(parts, ref):
    mine = lax.axis_index("grp")
    for d, part in zip(partners, parts):
        ref[jnp.bitwise_xor(mine, d)] = part[...]


def exchanged(parts):
    count = len(parts)
    return [
        part if d == 0 else lax.ppermute(part, "grp", [(i, i ^ d) for i in range(count)])
        for d, part in zip(partners, parts)
    ]


def halves(one, two, first_half):
    even = jnp.where(first_half, one, pltpu.roll(two, lanes // 2, 1))
    odd = jnp.where(first_half, pltpu.roll(one, lanes // 2, 1), two)
    return even, odd


def times_x(value, high_ref, low_ref):
    high, low = split_two(value)
    return dot(high, high_ref[...]) + dot(low, high_ref[...]) + dot(high, low_ref[...])


def divergence_part(forced_ref, div, sums, shape):
    rows_y, depth_z, length_x = shape
    tiles_x = length_x // lanes
    rows = rows_y * depth_z
    level = iota((depth_z, length_x), 0)
    sums[...] = jnp.zeros_like(sums)

    def one_row(y, carry):
        after = jnp.minimum(y + 1, rows_y - 1)
        along = wide_row(forced_ref, 0, y, tiles_x, depth_z)
        second = wide_row(forced_ref, 1, y, tiles_x, depth_z)
        third = wide_row(forced_ref, 2, y, tiles_x, depth_z)
        north = wide_row(forced_ref, 1, after, tiles_x, depth_z)
        north = jnp.where(y == rows_y - 1, 0.0, north)
        upper = jnp.where(level == depth_z - 1, 0.0, pltpu.roll(third, depth_z - 1, 0))
        total = pltpu.roll(along, length_x - 1, 1) - along + (north - second) + (upper - third)
        div[pl.ds(pl.multiple_of(y * depth_z, depth_z), depth_z), :] = total
        div[pl.ds(rows + depth_z + y, 1), :] = third[0:1, :]
        folded = sum(second[:, x * lanes : (x + 1) * lanes] for x in range(tiles_x))
        sums[pl.ds(y, 1), :] = jnp.sum(folded, axis=0, keepdims=True)
        return carry

    loop(0, rows_y, one_row, 0, 2)
    div[rows : rows + depth_z, :] = wide_row(forced_ref, 1, 0, tiles_x, depth_z)


def first_body(shape, *refs):
    vel_far, scal_far, ylo, yhi, zlo, zhi, recv_ref, high_ref, low_ref, far_ref, *rest = refs
    out_refs, rest = rest[:-14], rest[-14:]
    vel_ref, scal_ref, sems, star_ref, forced_ref, out_ref, *rest = rest
    force, samp, table, div, modes, index, sem, far_sem = rest
    rows_y, depth_z, length_x = shape
    n_grp = out_ref.shape[0]
    n_wide = recv_ref.shape[0] // n_grp
    rows = rows_y * depth_z
    tiles_x = length_x // lanes
    stencil_part(
        vel_far, scal_far, ylo, yhi, zlo, zhi, vel_ref, scal_ref, forced_ref, star_ref, sems
    )
    marker_part(recv_ref, star_ref, forced_ref, force, samp, table, index, sem, tiles_x, depth_z)
    keep = pltpu.make_async_copy(forced_ref, far_ref, far_sem)
    keep.start()
    divergence_part(forced_ref, div, samp, (rows_y, depth_z, length_x))
    chunk = div.shape[0] // 4
    for start in range(0, 4 * chunk, chunk):
        modes[start : start + chunk, :] = times_x(div[start : start + chunk, :], high_ref, low_ref)
    row, plane, forces, sums_row, end = packed_rows(rows_y, depth_z, n_wide)

    def send(front, back, size, place):
        first_half = iota((size, lanes), 1) < lanes // 2
        for j in range(n_grp // 2):
            one = modes[pl.ds(front, size), j * lanes : (j + 1) * lanes]
            two = modes[pl.ds(back, size), j * lanes : (j + 1) * lanes]
            even, odd = halves(one, two, first_half)
            out_ref[2 * j, pl.ds(place, size), :] = even
            out_ref[2 * j + 1, pl.ds(place, size), :] = odd

    def shuffle(y, carry):
        front = pl.multiple_of(y * depth_z, depth_z)
        back = pl.multiple_of((y + rows_y // 2) * depth_z, depth_z)
        send(front, back, depth_z, front)
        return carry

    loop(0, rows_y // 2, shuffle, 0, 4)
    send(rows, rows + depth_z // 2, depth_z // 2, row)
    send(rows + depth_z, rows + depth_z + rows_y // 2, rows_y // 2, plane)
    total = jnp.broadcast_to(jnp.sum(samp[...].T, axis=0, keepdims=True), (end - sums_row, lanes))
    for g in range(n_grp):
        out_ref[g, forces:sums_row, :] = force[pl.ds(g, n_wide, stride=n_grp), :]
        out_ref[g, sums_row:end, :] = total
    by_partner(out_ref, out_refs)
    keep.wait()


def times_z(value, high_ref, low_ref):
    high, low = split_two(value)
    return dot(high_ref[...], high) + dot(high_ref[...], low) + dot(low_ref[...], high)


def forward_z_body(rows_y, *refs):
    recv_refs, refs = refs[:-7], refs[-7:]
    high_ref, low_ref, table_ref, coef_ref, ends_ref, small_ref, recv_ref = refs
    n_grp = recv_ref.shape[0]
    from_partner(recv_refs, recv_ref)
    n_wide = small_ref.shape[0]
    steps, full_z, _ = coef_ref.shape
    depth_z = full_z // n_grp
    row, plane, forces, sums_row, end = packed_rows(rows_y, depth_z, n_wide)
    root = table_ref[0]
    last = iota((n_grp, depth_z, lanes), 1) == depth_z - 1
    first_half = iota((full_z, lanes), 1) < lanes // 2

    def cells_of(step):
        value = recv_ref[:, pl.ds(pl.multiple_of(step * depth_z, depth_z), depth_z), :]
        edge = recv_ref[:, pl.ds(plane + step, 1), :]
        edge = jnp.concatenate([edge[1:], edge[:1]], axis=0)
        value = value + jnp.where(last, jnp.broadcast_to(edge, value.shape), 0.0)
        return value.reshape(full_z, lanes)

    def one_pair(pair, total):
        value = jnp.concatenate([cells_of(2 * pair), cells_of(2 * pair + 1)], axis=1)
        found = times_z(value, high_ref, low_ref)
        coef_ref[2 * pair] = found[:, :lanes]
        coef_ref[2 * pair + 1] = found[:, lanes:]
        return found[:, lanes:] + root * (found[:, :lanes] + root * total)

    packed = recv_ref[:, row:plane, :]
    other = jnp.stack([pltpu.roll(packed[g], lanes // 2, 1) for g in range(n_grp)], axis=0)
    extra = jnp.concatenate([packed, other], axis=1).reshape(full_z, lanes)
    extra = jnp.where(first_half, times_z(extra, high_ref, low_ref), 0.0)
    ends_ref[2] = extra
    up = loop(0, steps // 2, one_pair, extra, 3)
    down = loop(
        0,
        steps,
        lambda i, total: coef_ref[steps - 1 - i] + root * total,
        jnp.zeros((full_z, lanes), f32),
        2,
    )
    down = root * down
    ends_ref[0] = up
    ends_ref[1] = down
    over = table_ref[1]
    up_other = pltpu.roll(up, lanes // 2, 1)
    down_other = pltpu.roll(down, lanes // 2, 1)
    up = jnp.where(first_half, up_other + over * up, up + over * up_other)
    down = jnp.where(first_half, down + over * down_other, down_other + over * down)
    down = down + extra + pltpu.roll(extra, lanes // 2, 1)
    upper = full_z // 2
    share = upper // n_wide
    for k, value in enumerate((up, down)):
        value = jnp.where(first_half[:upper], value[:upper], value[upper:])
        for i in range(n_wide):
            small_ref[i, k * share : (k + 1) * share, :] = value[i * share : (i + 1) * share]
    sums = sum(recv_ref[g, sums_row:end, :] for g in range(n_grp))
    for i in range(n_wide):
        for g in range(n_grp):
            place = 2 * share + g
            small_ref[i, place : place + 1, :] = recv_ref[g, forces + i : forces + i + 1, :]
        small_ref[i, 2 * share + n_grp : 2 * share + n_grp + 8, :] = sums


def widen(small):
    first_half = iota(small.shape, 1) < lanes // 2
    other = pltpu.roll(small, lanes // 2, 1)
    return jnp.concatenate(
        [jnp.where(first_half, small, other), jnp.where(first_half, other, small)], axis=0
    )


def backward_z_body(
    rows_y, coef_ref, ends_ref, small_ref, table_ref, high_ref, low_ref, *rest
):
    out_refs, rest = rest[:-3], rest[-3:]
    out_ref, ups, small = rest
    n_grp = out_ref.shape[0]
    steps, full_z, _ = coef_ref.shape
    depth_z = full_z // n_grp
    row, plane, _, _, _ = packed_rows(rows_y, depth_z, small_ref.shape[0])
    root, over, gain = table_ref[0], table_ref[1], table_ref[2]
    first_half = iota((full_z, lanes), 1) < lanes // 2
    share = small_ref.shape[1] // 2
    for i in range(small_ref.shape[0]):
        for k in range(2):
            small[k, i * share : (i + 1) * share] = small_ref[i, k * share : (k + 1) * share]
    up_in = widen(small[0])
    down_in = widen(small[1])
    up_start = jnp.where(
        first_half,
        up_in + ends_ref[2],
        pltpu.roll(ends_ref[0], lanes // 2, 1) + over * up_in,
    )
    down = jnp.where(
        first_half, pltpu.roll(ends_ref[1], lanes // 2, 1) + over * down_in, down_in
    )

    def rising(step, total):
        total = coef_ref[step] + root * total
        ups[step] = total
        return total

    loop(0, steps, rising, up_start, 2)

    def falling(i, total):
        pair = steps // 2 - 1 - i
        second = gain * (ups[2 * pair + 1] + total)
        total = root * (coef_ref[2 * pair + 1] + total)
        first = gain * (ups[2 * pair] + total)
        total = root * (coef_ref[2 * pair] + total)
        found = times_z(jnp.concatenate([first, second], axis=1), high_ref, low_ref)
        for j in range(2):
            step = 2 * pair + j
            value = found[:, j * lanes : (j + 1) * lanes]
            start = pl.multiple_of(step * depth_z, depth_z)
            out_ref[:, pl.ds(start, depth_z), :] = value.reshape(n_grp, depth_z, lanes)
            for g in range(n_grp):
                before = (g * depth_z - 1) % full_z
                out_ref[g, pl.ds(plane + step, 1), :] = value[before : before + 1, :]
        return total

    down = loop(0, steps // 2, falling, down, 3)
    extra = times_z(gain * (up_start + down), high_ref, low_ref)
    half = depth_z // 2
    for g in range(n_grp):
        start = g * depth_z
        out_ref[g, row:plane, :] = jnp.where(
            first_half[:half],
            extra[start : start + half],
            pltpu.roll(extra[start + half : start + depth_z], lanes // 2, 1),
        )
    by_partner(out_ref, out_refs)


def last_body(far_ref, mean_ref, high_ref, low_ref, *refs):
    recv_refs, refs = refs[:-10], refs[-10:]
    vel_far, scal_far, vel_ref, scal_ref, recv_ref, forced_ref, modes, press_ref, sem, sems = refs
    fetch = pltpu.make_async_copy(far_ref, forced_ref, sem)
    fetch.start()
    from_partner(recv_refs, recv_ref)
    n_grp = recv_ref.shape[0]
    _, rows_y, depth_z, length_x = vel_ref.shape
    rows = rows_y * depth_z
    tiles_x = length_x // lanes
    row, plane, _, _, _ = packed_rows(rows_y, depth_z, 0)

    def take(front, back, size, place):
        first_half = iota((size, lanes), 1) < lanes // 2
        for j in range(n_grp // 2):
            even = recv_ref[2 * j, pl.ds(place, size), :]
            odd = recv_ref[2 * j + 1, pl.ds(place, size), :]
            one, two = halves(even, odd, first_half)
            modes[pl.ds(front, size), j * lanes : (j + 1) * lanes] = one
            modes[pl.ds(back, size), j * lanes : (j + 1) * lanes] = two

    def shuffle(y, carry):
        front = pl.multiple_of(y * depth_z, depth_z)
        back = pl.multiple_of((y + rows_y // 2) * depth_z, depth_z)
        take(front, back, depth_z, front)
        return carry

    loop(0, rows_y // 2, shuffle, 0, 4)
    take(rows, rows + depth_z // 2, depth_z // 2, row)
    take(rows + depth_z, rows + depth_z + rows_y // 2, rows_y // 2, plane)
    chunk = modes.shape[0] // 4
    for start in range(0, 4 * chunk, chunk):
        press_ref[start : start + chunk, :] = times_x(
            modes[start : start + chunk, :], high_ref, low_ref
        )
    level = iota((depth_z, length_x), 0)

    def one_row(y, carry):
        start = pl.multiple_of(y * depth_z, depth_z)
        before = pl.multiple_of(jnp.where(y == 0, rows, start - depth_z), depth_z)
        press = press_ref[pl.ds(start, depth_z), :]
        south = press_ref[pl.ds(before, depth_z), :]
        below = jnp.broadcast_to(press_ref[pl.ds(rows + depth_z + y, 1), :], press.shape)
        lower = jnp.where(level == 0, below, pltpu.roll(press, 1, 0))
        west = pltpu.roll(press, 1, 1)
        mean = mean_ref[pl.ds(y, 1), :]
        mean = jnp.concatenate([mean] * tiles_x, axis=1)
        vel_ref[0, y] = wide_row(forced_ref, 0, y, tiles_x, depth_z) - (press - west)
        vel_ref[1, y] = wide_row(forced_ref, 1, y, tiles_x, depth_z) - (press - south) - mean
        vel_ref[2, y] = wide_row(forced_ref, 2, y, tiles_x, depth_z) - (press - lower)
        scal_ref[y] = wide_row(forced_ref, 3, y, tiles_x, depth_z)
        return carry

    fetch.wait()
    pieces = sems.shape[0] // 2
    size = rows_y // pieces
    copies = []
    for piece in range(pieces):
        loop(piece * size, (piece + 1) * size, one_row, 0, 2)
        part = pl.ds(piece * size, size)
        copies += [
            pltpu.make_async_copy(
                vel_ref.at[:, part], vel_far.at[:, part], sems.at[2 * piece]
            ),
            pltpu.make_async_copy(
                scal_ref.at[part], scal_far.at[part], sems.at[2 * piece + 1]
            ),
        ]
        copies[-2].start()
        copies[-1].start()
    for copy in copies:
        copy.wait()


def ring_body(recv_ref, table_ref, out_ref):
    count, size, _ = out_ref.shape
    rising = iota((size, lanes), 0) < size // 2
    ends = [
        jnp.where(rising, recv_ref[i, 0:size, :], recv_ref[count - 1 - i, 0:size, :])
        for i in range(count)
    ]
    step, whole = table_ref[0], table_ref[1]
    total = ends[0]
    for i in range(1, count):
        total = ends[i] + step * total
    total = whole * total
    reached = []
    for i in range(count):
        reached.append(total)
        total = ends[i] + step * total
    for i in range(count):
        out_ref[i] = jnp.where(rising, reached[i], reached[count - 1 - i])


def per_device(
    tables, velocity, scalar, marker_owner, marker_tile, marker_offset, marker_target, marker_eta
):
    _, rows_y, depth_z, length_x = velocity.shape
    n_wide = lax.axis_size("wide")
    n_grp = lax.axis_size("grp")
    owners = n_wide * n_grp
    full_z = depth_z * n_grp
    rows = rows_y * depth_z
    tiles_x = length_x // lanes
    held = marker_owner.shape[0]
    x_high, x_low, xt_high, xt_low, fz_high, fz_low, bz_high, bz_low, full, small_table = tables
    my_grp = lax.axis_index("grp")
    my_wide = lax.axis_index("wide")
    full = lax.dynamic_index_in_dim(full, my_grp, 0, keepdims=False)
    small_table = lax.dynamic_slice(
        small_table, (my_grp, my_wide, 0, 0, 0), (1, 1) + small_table.shape[2:]
    )[0, 0]

    owner = marker_owner[None, :]
    send, rank, y_first, y_last, z_first, z_last = call(
        pack_body,
        [((owners, 2 * lanes), f32), ((1, held), jnp.int32)]
        + [((4, depth_z, length_x), f32)] * 2
        + [((4, rows_y, length_x), f32)] * 2,
        [
            owner,
            marker_tile[None, :],
            marker_offset[None, :],
            marker_target,
            marker_eta[None, :],
            velocity,
            scalar,
        ],
        [
            pltpu.VMEM((1, held), jnp.int32),
            pltpu.VMEM((1, held), jnp.int32),
            pltpu.VMEM((1, held), jnp.int32),
            pltpu.VMEM((4, held), f32),
            pltpu.VMEM((1, held), f32),
            pltpu.VMEM(velocity.shape, f32),
            pltpu.VMEM(scalar.shape, f32),
            pltpu.SemaphoreType.DMA((7,)),
        ],
        name="pack",
        room=58,
        far_in=range(7),
    )
    z_low = passed_along(z_last, "grp", 1)
    z_high = passed_along(z_first, "grp", -1)
    y_low = passed_along(y_last, "wide", 1)
    y_high = passed_along(y_first, "wide", -1)
    recv = lax.all_to_all(send, ("wide", "grp"), split_axis=0, concat_axis=0, tiled=True)
    flat = 4 * tiles_x * rows
    sent_rows = packed_rows(rows_y, depth_z, n_wide)[-1]
    back_rows = packed_rows(rows_y, depth_z, n_wide)[2]
    with_edges = rows + depth_z + rows_y
    forced, *chunks = call(
        functools.partial(first_body, scalar.shape),
        [((flat, lanes), f32)] + [((sent_rows, lanes), f32)] * n_grp,
        [velocity, scalar, y_low, y_high, z_low, z_high, recv, x_high, x_low],
        [
            pltpu.VMEM(velocity.shape, f32),
            pltpu.VMEM(scalar.shape, f32),
            pltpu.SemaphoreType.DMA((8,)),
            pltpu.VMEM((flat, lanes), f32),
            pltpu.VMEM((flat, lanes), f32),
            pltpu.VMEM((n_grp, sent_rows, lanes), f32),
            pltpu.VMEM((owners, lanes), f32),
            pltpu.VMEM((owners, lanes), f32),
            pltpu.VMEM((owners, lanes), jnp.int32),
            pltpu.VMEM((with_edges, length_x), f32),
            pltpu.VMEM((with_edges, length_x), f32),
            pltpu.SMEM((owners, lanes), jnp.int32),
            pltpu.SemaphoreType.DMA(()),
            pltpu.SemaphoreType.DMA(()),
        ],
        name="first",
        room=58,
        micros=40,
        far_in=(0, 1),
        far_out=(0,),
    )
    chunks = exchanged(chunks)
    ends_size = full_z // n_wide
    coef, ends, small = call(
        functools.partial(forward_z_body, rows_y),
        [
            ((rows_y // 2, full_z, lanes), f32),
            ((3, full_z, lanes), f32),
            ((n_wide, ends_size + n_grp + 8, lanes), f32),
        ],
        [*chunks, fz_high, fz_low, full],
        [
            pltpu.VMEM((n_grp, sent_rows, lanes), f32),
        ],
        name="forward_z",
    )
    small = lax.all_to_all(small, "wide", split_axis=0, concat_axis=0, tiled=True)
    (reach,) = call(
        ring_body, [((n_wide, ends_size, lanes), f32)], [small, small_table], name="ring"
    )
    reach = lax.all_to_all(reach, "wide", split_axis=0, concat_axis=0, tiled=True)
    place = (jnp.arange(lanes, dtype=jnp.int32) - my_wide)[None, :]
    marker_force, mine = call(
        functools.partial(unpack_body, n_grp, n_wide * rows_y, length_x * depth_z * n_grp),
        [((4, held), f32), ((lanes, lanes), f32)],
        [owner, rank, small, place],
        name="unpack",
    )
    chunks = call(
        functools.partial(backward_z_body, rows_y),
        [((back_rows, lanes), f32)] * n_grp,
        [coef, ends, reach, full, bz_high, bz_low],
        [
            pltpu.VMEM((n_grp, back_rows, lanes), f32),
            pltpu.VMEM((rows_y // 2, full_z, lanes), f32),
            pltpu.VMEM((2, full_z // 2, lanes), f32),
        ],
        name="backward_z",
    )
    chunks = exchanged(chunks)
    velocity_out, scalar_out = call(
        last_body,
        [(velocity.shape, f32), (scalar.shape, f32)],
        [forced, mine, xt_high, xt_low, *chunks],
        [
            pltpu.VMEM(velocity.shape, f32),
            pltpu.VMEM(scalar.shape, f32),
            pltpu.VMEM((n_grp, back_rows, lanes), f32),
            pltpu.VMEM((flat, lanes), f32),
            pltpu.VMEM((with_edges, length_x), f32),
            pltpu.VMEM((with_edges, length_x), f32),
            pltpu.SemaphoreType.DMA(()),
            pltpu.SemaphoreType.DMA((8,)),
        ],
        name="last",
        room=54,
        far_in=(0,),
        far_out=(0, 1),
    )
    return velocity_out, scalar_out, marker_force


def solution(mesh):
    n_wide, n_grp = mesh.shape["wide"], mesh.shape["grp"]
    rows_y, full_z, length_x = 48, 128, 512
    basis_x, squares_x = real_basis(length_x)
    basis_z, squares_z = real_basis(full_z)
    parts = (
        two_parts(basis_x)
        + two_parts(basis_x.T)
        + two_parts(basis_z.T)
        + two_parts(basis_z)
        + decay_tables(squares_x, squares_z, n_grp, n_wide, rows_y)
    )

    def whole(*args):
        tables = tuple(jnp.asarray(part) for part in parts)
        return per_device(tables, *args)

    return jax.shard_map(
        whole,
        mesh=mesh,
        in_specs=(
            P(None, "wide", "grp", None),
            P("wide", "grp", None),
            P(("wide", "grp")),
            P(("wide", "grp")),
            P(("wide", "grp")),
            P(None, ("wide", "grp")),
            P(("wide", "grp")),
        ),
        out_specs=(P(None, "wide", "grp", None), P("wide", "grp", None), P(None, ("wide", "grp"))),
        check_vma=False,
    )
```

```python
import functools
import math

import jax
import jax.numpy as jnp
import ml_dtypes
import numpy as np
from jax import lax
from jax.experimental import pallas as pl
from jax.experimental.pallas import tpu as pltpu
from jax.sharding import PartitionSpec as P

time_step = 0.1
viscosity = 0.4
diffusivity = 0.25
f32 = jnp.float32
bf16 = jnp.bfloat16
lanes = 128
slots = 32
vmem = pl.BlockSpec(memory_space=pltpu.VMEM)
hbm = pl.BlockSpec(memory_space=pltpu.HBM)


def iota(shape, dim):
    return lax.broadcasted_iota(jnp.int32, shape, dim)


def call(body, out, args, scratch=(), name=None, micros=0, far_in=(), far_out=(), room=0):
    shapes = [jax.ShapeDtypeStruct(s, d) for s, d in out]
    moved = sum(a.size * a.dtype.itemsize for a in args)
    moved += sum(s.size * s.dtype.itemsize for s in shapes)
    near = [a for i, a in enumerate(args) if i not in far_in]
    near += [s for i, s in enumerate(shapes) if i not in far_out]
    held = sum(a.size * a.dtype.itemsize for a in near)
    held += sum(math.prod(s.shape) * 4 for s in scratch if s.shape)
    moved = max(moved, micros * 3000000)
    return pl.pallas_call(
        body,
        out_shape=shapes,
        in_specs=[hbm if i in far_in else vmem for i in range(len(args))],
        out_specs=[hbm if i in far_out else vmem for i in range(len(out))],
        scratch_shapes=list(scratch),
        compiler_params=pltpu.CompilerParams(vmem_limit_bytes=max(held + 6 * 2**20, room * 2**20)),
        cost_estimate=pl.CostEstimate(flops=0, bytes_accessed=moved, transcendentals=0),
        name=name,
    )(*args)


def loop(low, high, body, init, by):
    def several(turn, carry):
        for i in range(by):
            carry = body(low + turn * by + i, carry)
        return carry

    return lax.fori_loop(0, (high - low) // by, several, init)


def passed_along(value, axis, steps):
    count = lax.axis_size(axis)
    return lax.ppermute(value, axis, [(i, (i + steps) % count) for i in range(count)])


def real_basis(length):
    place = np.arange(length)
    columns, squares = [], []
    for k in range(length // 2 + 1):
        angle = 2.0 * np.pi * ((k * place) % length) / length
        scale = math.sqrt((1.0 if k in (0, length // 2) else 2.0) / length)
        square = 4.0 * math.sin(math.pi * k / length) ** 2
        columns.append(scale * np.cos(angle))
        squares.append(square)
        if k not in (0, length // 2):
            columns.append(scale * np.sin(angle))
            squares.append(square)
    return np.stack(columns, axis=1), np.array(squares)


def two_parts(table):
    high = table.astype(np.float32).astype(ml_dtypes.bfloat16)
    low = (table - high.astype(np.float64)).astype(np.float32).astype(ml_dtypes.bfloat16)
    return high, low


def decay_tables(squares_x, squares_z, n_grp, n_wide, rows_y):
    full_y = n_wide * rows_y
    local = squares_x.shape[0] // n_grp
    square = squares_z[None, :, None] + squares_x.reshape(n_grp, 1, local)
    mean_mode = square == 0.0
    safe = np.where(mean_mode, 1.0, square)
    root = 1.0 / (1.0 + safe / 2.0 + np.sqrt(safe + safe * safe / 4.0))
    root = np.where(mean_mode, 0.0, root)
    gain = np.where(mean_mode, 0.0, -root / (1.0 - root * root))
    half = rows_y // 2
    full = np.stack([root, root**half, gain], axis=1)
    full = np.concatenate([full, full], axis=3)
    device = root**rows_y
    small = np.stack([device, 1.0 / (1.0 - root**full_y)], axis=1)
    upper = small.shape[2] // 2
    small = np.concatenate([small[:, :, :upper], small[:, :, upper:]], axis=3)
    share = upper // n_wide
    small = small.reshape(n_grp, 2, n_wide, share, 2 * local).transpose(0, 2, 1, 3, 4)
    small = np.concatenate([small, small], axis=3)
    return full.astype(np.float32), small.astype(np.float32)


def split_two(value):
    high = value.astype(bf16)
    return high, (value - high.astype(f32)).astype(bf16)


def split_three(value):
    high = value.astype(bf16)
    rest = value - high.astype(f32)
    middle = rest.astype(bf16)
    return high, middle, (rest - middle.astype(f32)).astype(bf16)


def dot(left, right, dims=((1,), (0,))):
    return lax.dot_general(left, right, (dims, ((), ())), preferred_element_type=f32)


def pack_body(*refs):
    far, near, sems = refs[:7], refs[13:20], refs[20]
    send_ref, rank_ref, y_first, y_last, z_first, z_last = refs[7:13]
    owner_ref, tile_ref, offset_ref, target_ref, eta_ref, vel_ref, scal_ref = near
    copies = [pltpu.make_async_copy(a, b, sems.at[i]) for i, (a, b) in enumerate(zip(far, near))]
    for copy in copies:
        copy.start()
    for copy in copies[:5]:
        copy.wait()
    pack_markers(owner_ref, tile_ref, offset_ref, target_ref, eta_ref, send_ref, rank_ref)
    for copy in copies[5:]:
        copy.wait()
    rows_y, depth_z, _ = scal_ref.shape

    def edges(y, carry):
        for z, out in ((0, z_first), (depth_z - 1, z_last)):
            for f in range(3):
                out[f, pl.ds(y, 1), :] = vel_ref[f, y, z : z + 1, :]
            out[3, pl.ds(y, 1), :] = scal_ref[y, z : z + 1, :]
        return carry

    loop(0, rows_y, edges, 0, 8)
    for y, out in ((0, y_first), (rows_y - 1, y_last)):
        for f in range(3):
            out[f] = vel_ref[f, y]
        out[3] = scal_ref[y]


def pack_markers(owner_ref, tile_ref, offset_ref, target_ref, eta_ref, send_ref, rank_ref):
    owners = send_ref.shape[0]
    held = owner_ref.shape[1]
    onehot = owner_ref[...] == iota((owners, held), 0)
    onehot = jnp.where(onehot, 1.0, 0.0)
    upto = jnp.where(iota((lanes, lanes), 0) <= iota((lanes, lanes), 1), 1.0, 0.0).astype(bf16)
    carry = jnp.zeros((owners, 1), f32)
    ranks = []
    for start in range(0, held, lanes):
        piece = onehot[:, start : start + lanes]
        running = dot(piece.astype(bf16), upto) + carry
        ranks.append(jnp.sum(running * piece, axis=0, keepdims=True) - 1.0)
        carry = carry + jnp.sum(piece, axis=1, keepdims=True)
    rank = jnp.concatenate(ranks, axis=1).astype(jnp.int32)
    rank_ref[...] = rank
    chosen = rank == iota((slots, held), 0)
    cell = (tile_ref[...] * lanes + offset_ref[...]).astype(f32)
    values = [target_ref[k : k + 1, :] for k in range(4)] + [eta_ref[...], cell]
    onehot = onehot.astype(bf16)
    total = jnp.zeros((owners, 6 * slots), f32)
    for part in range(3):
        rows = [
            jnp.where(chosen, split_three(v)[part].astype(f32), 0.0).astype(bf16) for v in values
        ]
        total = total + dot(onehot, jnp.concatenate(rows, axis=0), ((1,), (1,)))
    column = iota((owners, 2 * lanes), 1)
    slot = column - 5 * slots
    spare = (slot >= 0) & (slot < slots) & (slot.astype(f32) >= carry)
    total = jnp.concatenate([total, jnp.zeros((owners, 2 * lanes - 6 * slots), f32)], axis=1)
    send_ref[:, 0, :] = total + jnp.where(spare, (slot * lanes).astype(f32), 0.0)


def unpack_body(
    n_grp, all_rows, row_cells, owner_ref, rank_ref, back_ref, place_ref, force_ref, mean_ref
):
    size = back_ref.shape[1] // 3
    owners = back_ref.shape[0] * n_grp
    held = owner_ref.shape[1]
    onehot = jnp.where(owner_ref[...] == iota((owners, held), 0), 1.0, 0.0).astype(bf16)
    sums = back_ref[:, 2 * size, :]
    sums = jnp.concatenate([sums, jnp.zeros((lanes - sums.shape[0], lanes), f32)], axis=0).T
    mine = jnp.where(place_ref[...] == 0, sums, 0.0)
    mean = jnp.sum(jnp.sum(sums, axis=1, keepdims=True), axis=0, keepdims=True)
    mine = jnp.sum(mine, axis=1, keepdims=True) * (1.0 / row_cells)
    mean_ref[...] = jnp.broadcast_to(mine - mean * (1.0 / (all_rows * row_cells)), mean_ref.shape)
    back = back_ref[:, size : 2 * size, :].reshape(owners, lanes).T
    spread = sum(dot(part, onehot) for part in split_three(back))
    chosen = rank_ref[...] == iota((slots, held), 0)
    for k in range(4):
        piece = jnp.where(chosen, spread[k * slots : (k + 1) * slots], 0.0)
        force_ref[k : k + 1, :] = jnp.sum(piece, axis=0, keepdims=True)


def swap_groups(value):
    row = iota(value.shape, 0) & 3
    group = lax.shift_right_logical(iota(value.shape, 1), 5)
    count = value.shape[0]
    out = value
    for k in (1, 2, 3):
        moved = pltpu.roll(value, 32 * k, 1)
        moved = jnp.where(
            row + k < 4, pltpu.roll(moved, count - k, 0), pltpu.roll(moved, 4 - k, 0)
        )
        out = jnp.where(((group - row) & 3) == k, moved, out)
    return out


def marker_part(recv_ref, star_ref, out_ref, force_ref, samp, table, index, sem, tiles_x, depth_z):
    sources = recv_ref.shape[0]
    wide_lane = iota((sources, lanes), 1)
    second = recv_ref[:, 0, lanes : 2 * lanes]
    cell = pltpu.roll(second.astype(jnp.int32), lanes - 32, 1)
    tile = lax.shift_right_logical(cell, 7)
    shift_x = tiles_x.bit_length() - 1
    shift_z = shift_x + depth_z.bit_length() - 1
    row = lax.shift_right_logical(tile, shift_z) * tiles_x + (tile & (tiles_x - 1))
    row = row * depth_z + (lax.shift_right_logical(tile, shift_x) & (depth_z - 1))
    spot = (iota((sources, lanes), 0) & 3) * 32 + (wide_lane & 31)
    there = (spot - cell) & (lanes - 1)
    back = (cell - spot) & (lanes - 1)
    table[...] = jnp.where(
        wide_lane < 32,
        4 * row,
        jnp.where(wide_lane < 64, pltpu.roll(there, 32, 1), pltpu.roll(back, 64, 1)),
    )
    copy = pltpu.make_async_copy(table, index, sem)
    copy.start()
    copy.wait()
    lane = iota((4, lanes), 1)

    def at(place):
        return pl.ds(pl.multiple_of(place, 4), 4)

    eta = jnp.where(wide_lane < 32, second, 0.0)
    eta = eta + pltpu.roll(eta, 32, 1)
    eta = eta + pltpu.roll(eta, 64, 1)
    force_ref[...] = swap_groups(eta)
    samp[...] = swap_groups(recv_ref[:, 0, 0:lanes])

    def rows_of(batch):
        return pl.ds(pl.multiple_of(4 * batch, 4), 4)

    def look(source, q, r, found):
        value = star_ref[at(index[source, r]), :]
        value = pltpu.roll(value, index[source, 32 + r], 1)
        return jnp.where(lane == 32 * q + r, value, found)

    def force_of(batch, found):
        force = force_ref[rows_of(batch), :] * (samp[rows_of(batch), :] - found)
        samp[rows_of(batch), :] = force
        return force

    def add(source, q, first, mine):
        places = [index[source, first + j] for j in range(2)]
        values = [out_ref[at(place), :] for place in places]
        terms = []
        for j in range(2):
            only = jnp.where(lane == 32 * q + first + j, mine, 0.0)
            terms.append(pltpu.roll(only, index[source, 64 + first + j], 1))
        values[0] = values[0] + terms[0]
        values[1] = jnp.where(places[0] == places[1], values[0], values[1]) + terms[1]
        for j in range(2):
            out_ref[at(places[j]), :] = values[j]

    def both(batch, mine):
        found = jnp.zeros((4, lanes), f32)
        for q in range(4):
            source = 4 * batch + q
            for first in range(0, slots, 4):
                for r in range(first, first + 4):
                    found = look(source, q, r, found)
                for r in (first, first + 2):
                    add(source - 4, q, r, mine)
        return force_of(batch, found)

    found = jnp.zeros((4, lanes), f32)
    for q in range(4):
        for r in range(slots):
            found = look(q, q, r, found)
    mine = lax.fori_loop(1, sources // 4, both, force_of(0, found))
    for q in range(4):
        for r in range(0, slots, 2):
            add(sources - 4 + q, q, r, mine)
    force_ref[...] = swap_groups(samp[...])


def at_row(y, x, f, tiles_x, depth_z):
    return pl.ds((y * tiles_x + x) * (4 * depth_z) + f, depth_z, stride=4)


def stencil_part(
    vel_far, scal_far, ylo_ref, yhi_ref, zlo_ref, zhi_ref, vel_ref, scal_ref, out_ref, same_ref, sems
):
    _, rows_y, depth_z, length_x = vel_ref.shape
    tiles_x = length_x // lanes
    level = iota((depth_z, length_x), 0)

    def one_row(y, carry):
        at_low = y == 0
        at_high = y == rows_y - 1
        below = jnp.maximum(y - 1, 0)
        above = jnp.minimum(y + 1, rows_y - 1)
        flow = [vel_ref[f, y] for f in range(3)]
        for f in range(4):
            if f < 3:
                center = flow[f]
                low, high = vel_ref[f, below], vel_ref[f, above]
            else:
                center = scal_ref[y]
                low, high = scal_ref[below], scal_ref[above]
            south = jnp.where(at_low, ylo_ref[f], low)
            north = jnp.where(at_high, yhi_ref[f], high)
            east = pltpu.roll(center, length_x - 1, 1)
            west = pltpu.roll(center, 1, 1)
            top = jnp.broadcast_to(zhi_ref[f, pl.ds(y, 1), :], center.shape)
            bottom = jnp.broadcast_to(zlo_ref[f, pl.ds(y, 1), :], center.shape)
            upper = jnp.where(level == depth_z - 1, top, pltpu.roll(center, depth_z - 1, 0))
            lower = jnp.where(level == 0, bottom, pltpu.roll(center, 1, 0))
            transport = (
                flow[0] * (east - west) + flow[1] * (north - south) + flow[2] * (upper - lower)
            )
            around = east + west + north + south + upper + lower
            coeff = viscosity if f < 3 else diffusivity
            star = (
                center * (1.0 - 6.0 * time_step * coeff)
                + (time_step * coeff) * around
                - (0.5 * time_step) * transport
            )
            for x in range(tiles_x):
                place = at_row(y, x, f, tiles_x, depth_z)
                out_ref[place, :] = star[:, x * lanes : (x + 1) * lanes]
                same_ref[place, :] = star[:, x * lanes : (x + 1) * lanes]
        return carry

    pieces = sems.shape[0] // 2
    size = rows_y // pieces
    fetches = []
    for piece in range(pieces):
        part = pl.ds(piece * size, size)
        fetches.append(
            [
                pltpu.make_async_copy(
                    vel_far.at[:, part], vel_ref.at[:, part], sems.at[2 * piece]
                ),
                pltpu.make_async_copy(
                    scal_far.at[part], scal_ref.at[part], sems.at[2 * piece + 1]
                ),
            ]
        )
        for copy in fetches[-1]:
            copy.start()
    for copy in fetches[0]:
        copy.wait()
    for piece in range(pieces):
        for copy in fetches[piece + 1] if piece + 1 < pieces else ():
            copy.wait()
        loop(piece * size, (piece + 1) * size, one_row, 0, 2)


def wide_row(ref, f, y, tiles_x, depth_z):
    return jnp.concatenate(
        [ref[at_row(y, x, f, tiles_x, depth_z), :] for x in range(tiles_x)], axis=1
    )


def packed_rows(rows_y, depth_z, n_wide):
    cells = rows_y // 2 * depth_z
    row = cells + depth_z // 2
    plane = row + rows_y // 2
    return cells, row, plane, plane + n_wide, plane + n_wide + 8


partners = (4, 5, 2, 3, 6, 7, 1, 0)


def by_partner(ref, parts):
    mine = lax.axis_index("grp")
    for d, part in zip(partners, parts):
        part[...] = ref[jnp.bitwise_xor(mine, d)]


def from_partner(parts, ref):
    mine = lax.axis_index("grp")
    for d, part in zip(partners, parts):
        ref[jnp.bitwise_xor(mine, d)] = part[...]


def exchanged(parts):
    count = len(parts)
    return [
        part if d == 0 else lax.ppermute(part, "grp", [(i, i ^ d) for i in range(count)])
        for d, part in zip(partners, parts)
    ]


def halves(one, two, first_half):
    even = jnp.where(first_half, one, pltpu.roll(two, lanes // 2, 1))
    odd = jnp.where(first_half, pltpu.roll(one, lanes // 2, 1), two)
    return even, odd


def times_x(value, high_ref, low_ref):
    high, low = split_two(value)
    return dot(high, high_ref[...]) + dot(low, high_ref[...]) + dot(high, low_ref[...])


def divergence_part(forced_ref, div, sums, shape):
    rows_y, depth_z, length_x = shape
    tiles_x = length_x // lanes
    rows = rows_y * depth_z
    level = iota((depth_z, length_x), 0)
    sums[...] = jnp.zeros_like(sums)

    def one_row(y, carry):
        after = jnp.minimum(y + 1, rows_y - 1)
        along = wide_row(forced_ref, 0, y, tiles_x, depth_z)
        second = wide_row(forced_ref, 1, y, tiles_x, depth_z)
        third = wide_row(forced_ref, 2, y, tiles_x, depth_z)
        north = wide_row(forced_ref, 1, after, tiles_x, depth_z)
        north = jnp.where(y == rows_y - 1, 0.0, north)
        upper = jnp.where(level == depth_z - 1, 0.0, pltpu.roll(third, depth_z - 1, 0))
        total = pltpu.roll(along, length_x - 1, 1) - along + (north - second) + (upper - third)
        div[pl.ds(pl.multiple_of(y * depth_z, depth_z), depth_z), :] = total
        div[pl.ds(rows + depth_z + y, 1), :] = third[0:1, :]
        folded = sum(second[:, x * lanes : (x + 1) * lanes] for x in range(tiles_x))
        sums[pl.ds(y, 1), :] = jnp.sum(folded, axis=0, keepdims=True)
        return carry

    loop(0, rows_y, one_row, 0, 4)
    div[rows : rows + depth_z, :] = wide_row(forced_ref, 1, 0, tiles_x, depth_z)


def first_body(shape, *refs):
    vel_far, scal_far, ylo, yhi, zlo, zhi, recv_ref, high_ref, low_ref, far_ref, *rest = refs
    out_refs, rest = rest[:-14], rest[-14:]
    vel_ref, scal_ref, sems, star_ref, forced_ref, out_ref, *rest = rest
    force, samp, table, div, modes, index, sem, far_sem = rest
    rows_y, depth_z, length_x = shape
    n_grp = out_ref.shape[0]
    n_wide = recv_ref.shape[0] // n_grp
    rows = rows_y * depth_z
    tiles_x = length_x // lanes
    stencil_part(
        vel_far, scal_far, ylo, yhi, zlo, zhi, vel_ref, scal_ref, forced_ref, star_ref, sems
    )
    marker_part(recv_ref, star_ref, forced_ref, force, samp, table, index, sem, tiles_x, depth_z)
    keep = pltpu.make_async_copy(forced_ref, far_ref, far_sem)
    keep.start()
    divergence_part(forced_ref, div, samp, (rows_y, depth_z, length_x))
    chunk = div.shape[0] // 4
    for start in range(0, 4 * chunk, chunk):
        modes[start : start + chunk, :] = times_x(div[start : start + chunk, :], high_ref, low_ref)
    row, plane, forces, sums_row, end = packed_rows(rows_y, depth_z, n_wide)

    def send(front, back, size, place):
        first_half = iota((size, lanes), 1) < lanes // 2
        for j in range(n_grp // 2):
            one = modes[pl.ds(front, size), j * lanes : (j + 1) * lanes]
            two = modes[pl.ds(back, size), j * lanes : (j + 1) * lanes]
            even, odd = halves(one, two, first_half)
            out_ref[2 * j, pl.ds(place, size), :] = even
            out_ref[2 * j + 1, pl.ds(place, size), :] = odd

    def shuffle(y, carry):
        front = pl.multiple_of(y * depth_z, depth_z)
        back = pl.multiple_of((y + rows_y // 2) * depth_z, depth_z)
        send(front, back, depth_z, front)
        return carry

    loop(0, rows_y // 2, shuffle, 0, 4)
    send(rows, rows + depth_z // 2, depth_z // 2, row)
    send(rows + depth_z, rows + depth_z + rows_y // 2, rows_y // 2, plane)
    total = jnp.broadcast_to(jnp.sum(samp[...].T, axis=0, keepdims=True), (end - sums_row, lanes))
    for g in range(n_grp):
        out_ref[g, forces:sums_row, :] = force[pl.ds(g, n_wide, stride=n_grp), :]
        out_ref[g, sums_row:end, :] = total
    by_partner(out_ref, out_refs)
    keep.wait()


def times_z(value, high_ref, low_ref):
    high, low = split_two(value)
    return dot(high_ref[...], high) + dot(high_ref[...], low) + dot(low_ref[...], high)


def forward_z_body(rows_y, *refs):
    recv_refs, refs = refs[:-7], refs[-7:]
    high_ref, low_ref, table_ref, coef_ref, ends_ref, small_ref, recv_ref = refs
    n_grp = recv_ref.shape[0]
    from_partner(recv_refs, recv_ref)
    n_wide = small_ref.shape[0]
    steps, full_z, _ = coef_ref.shape
    depth_z = full_z // n_grp
    row, plane, forces, sums_row, end = packed_rows(rows_y, depth_z, n_wide)
    root = table_ref[0]
    last = iota((n_grp, depth_z, lanes), 1) == depth_z - 1
    first_half = iota((full_z, lanes), 1) < lanes // 2

    def cells_of(step):
        value = recv_ref[:, pl.ds(pl.multiple_of(step * depth_z, depth_z), depth_z), :]
        edge = recv_ref[:, pl.ds(plane + step, 1), :]
        edge = jnp.concatenate([edge[1:], edge[:1]], axis=0)
        value = value + jnp.where(last, jnp.broadcast_to(edge, value.shape), 0.0)
        return value.reshape(full_z, lanes)

    def one_pair(pair, total):
        value = jnp.concatenate([cells_of(2 * pair), cells_of(2 * pair + 1)], axis=1)
        found = times_z(value, high_ref, low_ref)
        coef_ref[2 * pair] = found[:, :lanes]
        coef_ref[2 * pair + 1] = found[:, lanes:]
        return found[:, lanes:] + root * (found[:, :lanes] + root * total)

    packed = recv_ref[:, row:plane, :]
    other = jnp.stack([pltpu.roll(packed[g], lanes // 2, 1) for g in range(n_grp)], axis=0)
    extra = jnp.concatenate([packed, other], axis=1).reshape(full_z, lanes)
    extra = jnp.where(first_half, times_z(extra, high_ref, low_ref), 0.0)
    ends_ref[2] = extra
    up = loop(0, steps // 2, one_pair, extra, 4)
    down = loop(
        0,
        steps,
        lambda i, total: coef_ref[steps - 1 - i] + root * total,
        jnp.zeros((full_z, lanes), f32),
        4,
    )
    down = root * down
    ends_ref[0] = up
    ends_ref[1] = down
    over = table_ref[1]
    up_other = pltpu.roll(up, lanes // 2, 1)
    down_other = pltpu.roll(down, lanes // 2, 1)
    up = jnp.where(first_half, up_other + over * up, up + over * up_other)
    down = jnp.where(first_half, down + over * down_other, down_other + over * down)
    down = down + extra + pltpu.roll(extra, lanes // 2, 1)
    upper = full_z // 2
    share = upper // n_wide
    for k, value in enumerate((up, down)):
        value = jnp.where(first_half[:upper], value[:upper], value[upper:])
        for i in range(n_wide):
            small_ref[i, k * share : (k + 1) * share, :] = value[i * share : (i + 1) * share]
    sums = sum(recv_ref[g, sums_row:end, :] for g in range(n_grp))
    for i in range(n_wide):
        for g in range(n_grp):
            place = 2 * share + g
            small_ref[i, place : place + 1, :] = recv_ref[g, forces + i : forces + i + 1, :]
        small_ref[i, 2 * share + n_grp : 2 * share + n_grp + 8, :] = sums


def widen(small):
    first_half = iota(small.shape, 1) < lanes // 2
    other = pltpu.roll(small, lanes // 2, 1)
    return jnp.concatenate(
        [jnp.where(first_half, small, other), jnp.where(first_half, other, small)], axis=0
    )


def backward_z_body(
    rows_y, coef_ref, ends_ref, small_ref, table_ref, high_ref, low_ref, *rest
):
    out_refs, rest = rest[:-3], rest[-3:]
    out_ref, ups, small = rest
    n_grp = out_ref.shape[0]
    steps, full_z, _ = coef_ref.shape
    depth_z = full_z // n_grp
    row, plane, _, _, _ = packed_rows(rows_y, depth_z, small_ref.shape[0])
    root, over, gain = table_ref[0], table_ref[1], table_ref[2]
    first_half = iota((full_z, lanes), 1) < lanes // 2
    share = small_ref.shape[1] // 2
    for i in range(small_ref.shape[0]):
        for k in range(2):
            small[k, i * share : (i + 1) * share] = small_ref[i, k * share : (k + 1) * share]
    up_in = widen(small[0])
    down_in = widen(small[1])
    up_start = jnp.where(
        first_half,
        up_in + ends_ref[2],
        pltpu.roll(ends_ref[0], lanes // 2, 1) + over * up_in,
    )
    down = jnp.where(
        first_half, pltpu.roll(ends_ref[1], lanes // 2, 1) + over * down_in, down_in
    )

    def rising(step, total):
        total = coef_ref[step] + root * total
        ups[step] = total
        return total

    loop(0, steps, rising, up_start, 4)

    def falling(i, total):
        pair = steps // 2 - 1 - i
        second = gain * (ups[2 * pair + 1] + total)
        total = root * (coef_ref[2 * pair + 1] + total)
        first = gain * (ups[2 * pair] + total)
        total = root * (coef_ref[2 * pair] + total)
        found = times_z(jnp.concatenate([first, second], axis=1), high_ref, low_ref)
        for j in range(2):
            step = 2 * pair + j
            value = found[:, j * lanes : (j + 1) * lanes]
            start = pl.multiple_of(step * depth_z, depth_z)
            out_ref[:, pl.ds(start, depth_z), :] = value.reshape(n_grp, depth_z, lanes)
            for g in range(n_grp):
                before = (g * depth_z - 1) % full_z
                out_ref[g, pl.ds(plane + step, 1), :] = value[before : before + 1, :]
        return total

    down = loop(0, steps // 2, falling, down, 4)
    extra = times_z(gain * (up_start + down), high_ref, low_ref)
    half = depth_z // 2
    for g in range(n_grp):
        start = g * depth_z
        out_ref[g, row:plane, :] = jnp.where(
            first_half[:half],
            extra[start : start + half],
            pltpu.roll(extra[start + half : start + depth_z], lanes // 2, 1),
        )
    by_partner(out_ref, out_refs)


def last_body(far_ref, mean_ref, high_ref, low_ref, *refs):
    recv_refs, refs = refs[:-10], refs[-10:]
    vel_far, scal_far, vel_ref, scal_ref, recv_ref, forced_ref, modes, press_ref, sem, sems = refs
    fetch = pltpu.make_async_copy(far_ref, forced_ref, sem)
    fetch.start()
    from_partner(recv_refs, recv_ref)
    n_grp = recv_ref.shape[0]
    _, rows_y, depth_z, length_x = vel_ref.shape
    rows = rows_y * depth_z
    tiles_x = length_x // lanes
    row, plane, _, _, _ = packed_rows(rows_y, depth_z, 0)

    def take(front, back, size, place):
        first_half = iota((size, lanes), 1) < lanes // 2
        for j in range(n_grp // 2):
            even = recv_ref[2 * j, pl.ds(place, size), :]
            odd = recv_ref[2 * j + 1, pl.ds(place, size), :]
            one, two = halves(even, odd, first_half)
            modes[pl.ds(front, size), j * lanes : (j + 1) * lanes] = one
            modes[pl.ds(back, size), j * lanes : (j + 1) * lanes] = two

    def shuffle(y, carry):
        front = pl.multiple_of(y * depth_z, depth_z)
        back = pl.multiple_of((y + rows_y // 2) * depth_z, depth_z)
        take(front, back, depth_z, front)
        return carry

    loop(0, rows_y // 2, shuffle, 0, 4)
    take(rows, rows + depth_z // 2, depth_z // 2, row)
    take(rows + depth_z, rows + depth_z + rows_y // 2, rows_y // 2, plane)
    chunk = modes.shape[0] // 4
    for start in range(0, 4 * chunk, chunk):
        press_ref[start : start + chunk, :] = times_x(
            modes[start : start + chunk, :], high_ref, low_ref
        )
    level = iota((depth_z, length_x), 0)

    def one_row(y, carry):
        start = pl.multiple_of(y * depth_z, depth_z)
        before = pl.multiple_of(jnp.where(y == 0, rows, start - depth_z), depth_z)
        press = press_ref[pl.ds(start, depth_z), :]
        south = press_ref[pl.ds(before, depth_z), :]
        below = jnp.broadcast_to(press_ref[pl.ds(rows + depth_z + y, 1), :], press.shape)
        lower = jnp.where(level == 0, below, pltpu.roll(press, 1, 0))
        west = pltpu.roll(press, 1, 1)
        mean = mean_ref[pl.ds(y, 1), :]
        mean = jnp.concatenate([mean] * tiles_x, axis=1)
        vel_ref[0, y] = wide_row(forced_ref, 0, y, tiles_x, depth_z) - (press - west)
        vel_ref[1, y] = wide_row(forced_ref, 1, y, tiles_x, depth_z) - (press - south) - mean
        vel_ref[2, y] = wide_row(forced_ref, 2, y, tiles_x, depth_z) - (press - lower)
        scal_ref[y] = wide_row(forced_ref, 3, y, tiles_x, depth_z)
        return carry

    fetch.wait()
    pieces = sems.shape[0] // 2
    size = rows_y // pieces
    copies = []
    for piece in range(pieces):
        loop(piece * size, (piece + 1) * size, one_row, 0, 4)
        part = pl.ds(piece * size, size)
        copies += [
            pltpu.make_async_copy(
                vel_ref.at[:, part], vel_far.at[:, part], sems.at[2 * piece]
            ),
            pltpu.make_async_copy(
                scal_ref.at[part], scal_far.at[part], sems.at[2 * piece + 1]
            ),
        ]
        copies[-2].start()
        copies[-1].start()
    for copy in copies:
        copy.wait()


def ring_body(recv_ref, table_ref, out_ref):
    count, size, _ = out_ref.shape
    rising = iota((size, lanes), 0) < size // 2
    ends = [
        jnp.where(rising, recv_ref[i, 0:size, :], recv_ref[count - 1 - i, 0:size, :])
        for i in range(count)
    ]
    step, whole = table_ref[0], table_ref[1]
    total = ends[0]
    for i in range(1, count):
        total = ends[i] + step * total
    total = whole * total
    reached = []
    for i in range(count):
        reached.append(total)
        total = ends[i] + step * total
    for i in range(count):
        out_ref[i] = jnp.where(rising, reached[i], reached[count - 1 - i])


def per_device(
    tables, velocity, scalar, marker_owner, marker_tile, marker_offset, marker_target, marker_eta
):
    _, rows_y, depth_z, length_x = velocity.shape
    n_wide = lax.axis_size("wide")
    n_grp = lax.axis_size("grp")
    owners = n_wide * n_grp
    full_z = depth_z * n_grp
    rows = rows_y * depth_z
    tiles_x = length_x // lanes
    held = marker_owner.shape[0]
    x_high, x_low, xt_high, xt_low, fz_high, fz_low, bz_high, bz_low, full, small_table = tables
    my_grp = lax.axis_index("grp")
    my_wide = lax.axis_index("wide")
    full = lax.dynamic_index_in_dim(full, my_grp, 0, keepdims=False)
    small_table = lax.dynamic_slice(
        small_table, (my_grp, my_wide, 0, 0, 0), (1, 1) + small_table.shape[2:]
    )[0, 0]

    owner = marker_owner[None, :]
    send, rank, y_first, y_last, z_first, z_last = call(
        pack_body,
        [((owners, 1, 2 * lanes), f32), ((1, held), jnp.int32)]
        + [((4, depth_z, length_x), f32)] * 2
        + [((4, rows_y, length_x), f32)] * 2,
        [
            owner,
            marker_tile[None, :],
            marker_offset[None, :],
            marker_target,
            marker_eta[None, :],
            velocity,
            scalar,
        ],
        [
            pltpu.VMEM((1, held), jnp.int32),
            pltpu.VMEM((1, held), jnp.int32),
            pltpu.VMEM((1, held), jnp.int32),
            pltpu.VMEM((4, held), f32),
            pltpu.VMEM((1, held), f32),
            pltpu.VMEM(velocity.shape, f32),
            pltpu.VMEM(scalar.shape, f32),
            pltpu.SemaphoreType.DMA((7,)),
        ],
        name="pack",
        room=58,
        far_in=range(7),
    )
    z_low = passed_along(z_last, "grp", 1)
    z_high = passed_along(z_first, "grp", -1)
    y_low = passed_along(y_last, "wide", 1)
    y_high = passed_along(y_first, "wide", -1)
    recv = lax.all_to_all(send, ("wide", "grp"), split_axis=0, concat_axis=0, tiled=True)
    flat = 4 * tiles_x * rows
    sent_rows = packed_rows(rows_y, depth_z, n_wide)[-1]
    back_rows = packed_rows(rows_y, depth_z, n_wide)[2]
    with_edges = rows + depth_z + rows_y
    forced, *chunks = call(
        functools.partial(first_body, scalar.shape),
        [((flat, lanes), f32)] + [((sent_rows, lanes), f32)] * n_grp,
        [velocity, scalar, y_low, y_high, z_low, z_high, recv, x_high, x_low],
        [
            pltpu.VMEM(velocity.shape, f32),
            pltpu.VMEM(scalar.shape, f32),
            pltpu.SemaphoreType.DMA((8,)),
            pltpu.VMEM((flat, lanes), f32),
            pltpu.VMEM((flat, lanes), f32),
            pltpu.VMEM((n_grp, sent_rows, lanes), f32),
            pltpu.VMEM((owners, lanes), f32),
            pltpu.VMEM((owners, lanes), f32),
            pltpu.VMEM((owners, lanes), jnp.int32),
            pltpu.VMEM((with_edges, length_x), f32),
            pltpu.VMEM((with_edges, length_x), f32),
            pltpu.SMEM((owners, lanes), jnp.int32),
            pltpu.SemaphoreType.DMA(()),
            pltpu.SemaphoreType.DMA(()),
        ],
        name="first",
        room=50,
        micros=40,
        far_in=(0, 1),
        far_out=(0,),
    )
    chunks = exchanged(chunks)
    ends_size = full_z // n_wide
    coef, ends, small = call(
        functools.partial(forward_z_body, rows_y),
        [
            ((rows_y // 2, full_z, lanes), f32),
            ((3, full_z, lanes), f32),
            ((n_wide, ends_size + n_grp + 8, lanes), f32),
        ],
        [*chunks, fz_high, fz_low, full],
        [
            pltpu.VMEM((n_grp, sent_rows, lanes), f32),
        ],
        name="forward_z",
    )
    small = lax.all_to_all(small, "wide", split_axis=0, concat_axis=0, tiled=True)
    (reach,) = call(
        ring_body, [((n_wide, ends_size, lanes), f32)], [small, small_table], name="ring"
    )
    reach = lax.all_to_all(reach, "wide", split_axis=0, concat_axis=0, tiled=True)
    place = (jnp.arange(lanes, dtype=jnp.int32) - my_wide)[None, :]
    marker_force, mine = call(
        functools.partial(unpack_body, n_grp, n_wide * rows_y, length_x * depth_z * n_grp),
        [((4, held), f32), ((lanes, lanes), f32)],
        [owner, rank, small, place],
        name="unpack",
    )
    chunks = call(
        functools.partial(backward_z_body, rows_y),
        [((back_rows, lanes), f32)] * n_grp,
        [coef, ends, reach, full, bz_high, bz_low],
        [
            pltpu.VMEM((n_grp, back_rows, lanes), f32),
            pltpu.VMEM((rows_y // 2, full_z, lanes), f32),
            pltpu.VMEM((2, full_z // 2, lanes), f32),
        ],
        name="backward_z",
    )
    chunks = exchanged(chunks)
    velocity_out, scalar_out = call(
        last_body,
        [(velocity.shape, f32), (scalar.shape, f32)],
        [forced, mine, xt_high, xt_low, *chunks],
        [
            pltpu.VMEM(velocity.shape, f32),
            pltpu.VMEM(scalar.shape, f32),
            pltpu.VMEM((n_grp, back_rows, lanes), f32),
            pltpu.VMEM((flat, lanes), f32),
            pltpu.VMEM((with_edges, length_x), f32),
            pltpu.VMEM((with_edges, length_x), f32),
            pltpu.SemaphoreType.DMA(()),
            pltpu.SemaphoreType.DMA((8,)),
        ],
        name="last",
        room=54,
        far_in=(0,),
        far_out=(0, 1),
    )
    return velocity_out, scalar_out, marker_force


def solution(mesh):
    n_wide, n_grp = mesh.shape["wide"], mesh.shape["grp"]
    rows_y, full_z, length_x = 48, 128, 512
    basis_x, squares_x = real_basis(length_x)
    basis_z, squares_z = real_basis(full_z)
    parts = (
        two_parts(basis_x)
        + two_parts(basis_x.T)
        + two_parts(basis_z.T)
        + two_parts(basis_z)
        + decay_tables(squares_x, squares_z, n_grp, n_wide, rows_y)
    )

    def whole(*args):
        tables = tuple(jnp.asarray(part) for part in parts)
        return per_device(tables, *args)

    return jax.shard_map(
        whole,
        mesh=mesh,
        in_specs=(
            P(None, "wide", "grp", None),
            P("wide", "grp", None),
            P(("wide", "grp")),
            P(("wide", "grp")),
            P(("wide", "grp")),
            P(None, ("wide", "grp")),
            P(("wide", "grp")),
        ),
        out_specs=(P(None, "wide", "grp", None), P("wide", "grp", None), P(None, ("wide", "grp"))),
        check_vma=False,
    )
```

```python
import functools
import math

import jax
import jax.numpy as jnp
import ml_dtypes
import numpy as np
from jax import lax
from jax.experimental import pallas as pl
from jax.experimental.pallas import tpu as pltpu
from jax.sharding import PartitionSpec as P

time_step = 0.1
viscosity = 0.4
diffusivity = 0.25
f32 = jnp.float32
bf16 = jnp.bfloat16
lanes = 128
slots = 32
vmem = pl.BlockSpec(memory_space=pltpu.VMEM)
hbm = pl.BlockSpec(memory_space=pltpu.HBM)


def iota(shape, dim):
    return lax.broadcasted_iota(jnp.int32, shape, dim)


def call(body, out, args, scratch=(), name=None, micros=0, far_in=(), far_out=(), room=0):
    shapes = [jax.ShapeDtypeStruct(s, d) for s, d in out]
    moved = sum(a.size * a.dtype.itemsize for a in args)
    moved += sum(s.size * s.dtype.itemsize for s in shapes)
    near = [a for i, a in enumerate(args) if i not in far_in]
    near += [s for i, s in enumerate(shapes) if i not in far_out]
    held = sum(a.size * a.dtype.itemsize for a in near)
    held += sum(math.prod(s.shape) * 4 for s in scratch if s.shape)
    moved = max(moved, micros * 3000000)
    return pl.pallas_call(
        body,
        out_shape=shapes,
        in_specs=[hbm if i in far_in else vmem for i in range(len(args))],
        out_specs=[hbm if i in far_out else vmem for i in range(len(out))],
        scratch_shapes=list(scratch),
        compiler_params=pltpu.CompilerParams(vmem_limit_bytes=max(held + 6 * 2**20, room * 2**20)),
        cost_estimate=pl.CostEstimate(flops=0, bytes_accessed=moved, transcendentals=0),
        name=name,
    )(*args)


def loop(low, high, body, init, by):
    def several(turn, carry):
        for i in range(by):
            carry = body(low + turn * by + i, carry)
        return carry

    return lax.fori_loop(0, (high - low) // by, several, init)


def passed_along(value, axis, steps):
    count = lax.axis_size(axis)
    return lax.ppermute(value, axis, [(i, (i + steps) % count) for i in range(count)])


def real_basis(length):
    place = np.arange(length)
    columns, squares = [], []
    for k in range(length // 2 + 1):
        angle = 2.0 * np.pi * ((k * place) % length) / length
        scale = math.sqrt((1.0 if k in (0, length // 2) else 2.0) / length)
        square = 4.0 * math.sin(math.pi * k / length) ** 2
        columns.append(scale * np.cos(angle))
        squares.append(square)
        if k not in (0, length // 2):
            columns.append(scale * np.sin(angle))
            squares.append(square)
    return np.stack(columns, axis=1), np.array(squares)


def two_parts(table):
    high = table.astype(np.float32).astype(ml_dtypes.bfloat16)
    low = (table - high.astype(np.float64)).astype(np.float32).astype(ml_dtypes.bfloat16)
    return high, low


def decay_tables(squares_x, squares_z, n_grp, n_wide, rows_y):
    full_y = n_wide * rows_y
    local = squares_x.shape[0] // n_grp
    square = squares_z[None, :, None] + squares_x.reshape(n_grp, 1, local)
    mean_mode = square == 0.0
    safe = np.where(mean_mode, 1.0, square)
    root = 1.0 / (1.0 + safe / 2.0 + np.sqrt(safe + safe * safe / 4.0))
    root = np.where(mean_mode, 0.0, root)
    gain = np.where(mean_mode, 0.0, -root / (1.0 - root * root))
    half = rows_y // 2
    full = np.stack([root, root**half, gain], axis=1)
    full = np.concatenate([full, full], axis=3)
    device = root**rows_y
    small = np.stack([device, 1.0 / (1.0 - root**full_y)], axis=1)
    upper = small.shape[2] // 2
    small = np.concatenate([small[:, :, :upper], small[:, :, upper:]], axis=3)
    share = upper // n_wide
    small = small.reshape(n_grp, 2, n_wide, share, 2 * local).transpose(0, 2, 1, 3, 4)
    small = np.concatenate([small, small], axis=3)
    return full.astype(np.float32), small.astype(np.float32)


def split_two(value):
    high = value.astype(bf16)
    return high, (value - high.astype(f32)).astype(bf16)


def split_three(value):
    high = value.astype(bf16)
    rest = value - high.astype(f32)
    middle = rest.astype(bf16)
    return high, middle, (rest - middle.astype(f32)).astype(bf16)


def dot(left, right, dims=((1,), (0,))):
    return lax.dot_general(left, right, (dims, ((), ())), preferred_element_type=f32)


def pack_body(*refs):
    far, near, sems = refs[:7], refs[13:18], refs[18]
    send_ref, rank_ref, y_first, y_last, z_first, z_last = refs[7:13]
    vel_far, scal_far = far[5:]
    rows_y, depth_z, _ = scal_far.shape
    pairs = list(zip(far[:5], near))
    for y, out in ((0, y_first), (rows_y - 1, y_last)):
        pairs += [(vel_far.at[:, y], out.at[0:3]), (scal_far.at[y], out.at[3])]
    for z, out in ((0, z_first), (depth_z - 1, z_last)):
        pairs += [(vel_far.at[:, :, z, :], out.at[0:3]), (scal_far.at[:, z, :], out.at[3])]
    copies = [pltpu.make_async_copy(a, b, sems.at[i]) for i, (a, b) in enumerate(pairs)]
    for copy in copies[5:] + copies[:5]:
        copy.start()
    for copy in copies[:5]:
        copy.wait()
    pack_markers(*near, send_ref, rank_ref)
    for copy in copies[5:]:
        copy.wait()


def pack_markers(owner_ref, tile_ref, offset_ref, target_ref, eta_ref, send_ref, rank_ref):
    owners = send_ref.shape[0]
    held = owner_ref.shape[1]
    onehot = owner_ref[...] == iota((owners, held), 0)
    onehot = jnp.where(onehot, 1.0, 0.0)
    upto = jnp.where(iota((lanes, lanes), 0) <= iota((lanes, lanes), 1), 1.0, 0.0).astype(bf16)
    carry = jnp.zeros((owners, 1), f32)
    ranks = []
    for start in range(0, held, lanes):
        piece = onehot[:, start : start + lanes]
        running = dot(piece.astype(bf16), upto) + carry
        ranks.append(jnp.sum(running * piece, axis=0, keepdims=True) - 1.0)
        carry = carry + jnp.sum(piece, axis=1, keepdims=True)
    rank = jnp.concatenate(ranks, axis=1).astype(jnp.int32)
    rank_ref[...] = rank
    chosen = rank == iota((slots, held), 0)
    cell = (tile_ref[...] * lanes + offset_ref[...]).astype(f32)
    values = [target_ref[k : k + 1, :] for k in range(4)] + [eta_ref[...], cell]
    onehot = onehot.astype(bf16)
    total = jnp.zeros((owners, 6 * slots), f32)
    for part in range(3):
        rows = [
            jnp.where(chosen, split_three(v)[part].astype(f32), 0.0).astype(bf16) for v in values
        ]
        total = total + dot(onehot, jnp.concatenate(rows, axis=0), ((1,), (1,)))
    column = iota((owners, 2 * lanes), 1)
    slot = column - 5 * slots
    spare = (slot >= 0) & (slot < slots) & (slot.astype(f32) >= carry)
    total = jnp.concatenate([total, jnp.zeros((owners, 2 * lanes - 6 * slots), f32)], axis=1)
    send_ref[:, 0, :] = total + jnp.where(spare, (slot * lanes).astype(f32), 0.0)


def unpack_body(
    n_grp, all_rows, row_cells, owner_ref, rank_ref, back_ref, place_ref, force_ref, mean_ref
):
    size = back_ref.shape[1] // 3
    owners = back_ref.shape[0] * n_grp
    held = owner_ref.shape[1]
    onehot = jnp.where(owner_ref[...] == iota((owners, held), 0), 1.0, 0.0).astype(bf16)
    sums = back_ref[:, 2 * size, :]
    sums = jnp.concatenate([sums, jnp.zeros((lanes - sums.shape[0], lanes), f32)], axis=0).T
    mine = jnp.where(place_ref[...] == 0, sums, 0.0)
    mean = jnp.sum(jnp.sum(sums, axis=1, keepdims=True), axis=0, keepdims=True)
    mine = jnp.sum(mine, axis=1, keepdims=True) * (1.0 / row_cells)
    mean_ref[...] = jnp.broadcast_to(mine - mean * (1.0 / (all_rows * row_cells)), mean_ref.shape)
    back = back_ref[:, size : 2 * size, :].reshape(owners, lanes).T
    spread = sum(dot(part, onehot) for part in split_three(back))
    chosen = rank_ref[...] == iota((slots, held), 0)
    for k in range(4):
        piece = jnp.where(chosen, spread[k * slots : (k + 1) * slots], 0.0)
        force_ref[k : k + 1, :] = jnp.sum(piece, axis=0, keepdims=True)


def swap_groups(value):
    row = iota(value.shape, 0) & 3
    group = lax.shift_right_logical(iota(value.shape, 1), 5)
    count = value.shape[0]
    out = value
    for k in (1, 2, 3):
        moved = pltpu.roll(value, 32 * k, 1)
        moved = jnp.where(
            row + k < 4, pltpu.roll(moved, count - k, 0), pltpu.roll(moved, 4 - k, 0)
        )
        out = jnp.where(((group - row) & 3) == k, moved, out)
    return out


def marker_part(recv_ref, star_ref, out_ref, force_ref, samp, table, index, sem, tiles_x, depth_z):
    sources = recv_ref.shape[0]
    wide_lane = iota((sources, lanes), 1)
    second = recv_ref[:, 0, lanes : 2 * lanes]
    cell = pltpu.roll(second.astype(jnp.int32), lanes - 32, 1)
    tile = lax.shift_right_logical(cell, 7)
    shift_x = tiles_x.bit_length() - 1
    shift_z = shift_x + depth_z.bit_length() - 1
    row = lax.shift_right_logical(tile, shift_z) * tiles_x + (tile & (tiles_x - 1))
    row = row * depth_z + (lax.shift_right_logical(tile, shift_x) & (depth_z - 1))
    spot = (iota((sources, lanes), 0) & 3) * 32 + (wide_lane & 31)
    there = (spot - cell) & (lanes - 1)
    back = (cell - spot) & (lanes - 1)
    table[...] = jnp.where(
        wide_lane < 32,
        4 * row,
        jnp.where(wide_lane < 64, pltpu.roll(there, 32, 1), pltpu.roll(back, 64, 1)),
    )
    copy = pltpu.make_async_copy(table, index, sem)
    copy.start()
    copy.wait()
    lane = iota((4, lanes), 1)

    def at(place):
        return pl.ds(pl.multiple_of(place, 4), 4)

    eta = jnp.where(wide_lane < 32, second, 0.0)
    eta = eta + pltpu.roll(eta, 32, 1)
    eta = eta + pltpu.roll(eta, 64, 1)
    force_ref[...] = swap_groups(eta)
    samp[...] = swap_groups(recv_ref[:, 0, 0:lanes])

    def rows_of(batch):
        return pl.ds(pl.multiple_of(4 * batch, 4), 4)

    def look(source, q, r, found):
        value = star_ref[at(index[source, r]), :]
        value = pltpu.roll(value, index[source, 32 + r], 1)
        return jnp.where(lane == 32 * q + r, value, found)

    def force_of(batch, found):
        force = force_ref[rows_of(batch), :] * (samp[rows_of(batch), :] - found)
        samp[rows_of(batch), :] = force
        return force

    def add(source, q, first, mine):
        places = [index[source, first + j] for j in range(2)]
        values = [out_ref[at(place), :] for place in places]
        terms = []
        for j in range(2):
            only = jnp.where(lane == 32 * q + first + j, mine, 0.0)
            terms.append(pltpu.roll(only, index[source, 64 + first + j], 1))
        values[0] = values[0] + terms[0]
        values[1] = jnp.where(places[0] == places[1], values[0], values[1]) + terms[1]
        for j in range(2):
            out_ref[at(places[j]), :] = values[j]

    def both(batch, mine):
        found = jnp.zeros((4, lanes), f32)
        for q in range(4):
            source = 4 * batch + q
            for first in range(0, slots, 4):
                for r in range(first, first + 4):
                    found = look(source, q, r, found)
                for r in (first, first + 2):
                    add(source - 4, q, r, mine)
        return force_of(batch, found)

    found = jnp.zeros((4, lanes), f32)
    for q in range(4):
        for r in range(slots):
            found = look(q, q, r, found)
    mine = lax.fori_loop(1, sources // 4, both, force_of(0, found))
    for q in range(4):
        for r in range(0, slots, 2):
            add(sources - 4 + q, q, r, mine)
    force_ref[...] = swap_groups(samp[...])


def at_row(y, x, f, tiles_x, depth_z):
    return pl.ds((y * tiles_x + x) * (4 * depth_z) + f, depth_z, stride=4)


def stencil_part(
    vel_far, scal_far, ylo_ref, yhi_ref, zlo_ref, zhi_ref, vel_ref, scal_ref, out_ref, same_ref, sems
):
    _, rows_y, depth_z, length_x = vel_ref.shape
    tiles_x = length_x // lanes
    level = iota((depth_z, length_x), 0)

    def one_row(y, carry):
        at_low = y == 0
        at_high = y == rows_y - 1
        below = jnp.maximum(y - 1, 0)
        above = jnp.minimum(y + 1, rows_y - 1)
        flow = [vel_ref[f, y] for f in range(3)]
        for f in range(4):
            if f < 3:
                center = flow[f]
                low, high = vel_ref[f, below], vel_ref[f, above]
            else:
                center = scal_ref[y]
                low, high = scal_ref[below], scal_ref[above]
            south = jnp.where(at_low, ylo_ref[f], low)
            north = jnp.where(at_high, yhi_ref[f], high)
            east = pltpu.roll(center, length_x - 1, 1)
            west = pltpu.roll(center, 1, 1)
            top = jnp.broadcast_to(zhi_ref[f, pl.ds(y, 1), :], center.shape)
            bottom = jnp.broadcast_to(zlo_ref[f, pl.ds(y, 1), :], center.shape)
            upper = jnp.where(level == depth_z - 1, top, pltpu.roll(center, depth_z - 1, 0))
            lower = jnp.where(level == 0, bottom, pltpu.roll(center, 1, 0))
            transport = (
                flow[0] * (east - west) + flow[1] * (north - south) + flow[2] * (upper - lower)
            )
            around = east + west + north + south + upper + lower
            coeff = viscosity if f < 3 else diffusivity
            star = (
                center * (1.0 - 6.0 * time_step * coeff)
                + (time_step * coeff) * around
                - (0.5 * time_step) * transport
            )
            for x in range(tiles_x):
                place = at_row(y, x, f, tiles_x, depth_z)
                out_ref[place, :] = star[:, x * lanes : (x + 1) * lanes]
                same_ref[place, :] = star[:, x * lanes : (x + 1) * lanes]
        return carry

    pieces = sems.shape[0] // 2
    size = rows_y // pieces
    fetches = []
    for piece in range(pieces):
        part = pl.ds(piece * size, size)
        fetches.append(
            [
                pltpu.make_async_copy(
                    vel_far.at[:, part], vel_ref.at[:, part], sems.at[2 * piece]
                ),
                pltpu.make_async_copy(
                    scal_far.at[part], scal_ref.at[part], sems.at[2 * piece + 1]
                ),
            ]
        )
        for copy in fetches[-1]:
            copy.start()
    for copy in fetches[0]:
        copy.wait()
    for piece in range(pieces):
        for copy in fetches[piece + 1] if piece + 1 < pieces else ():
            copy.wait()
        loop(piece * size, (piece + 1) * size, one_row, 0, 3)


def wide_row(ref, f, y, tiles_x, depth_z):
    return jnp.concatenate(
        [ref[at_row(y, x, f, tiles_x, depth_z), :] for x in range(tiles_x)], axis=1
    )


def packed_rows(rows_y, depth_z, n_wide):
    cells = rows_y // 2 * depth_z
    row = cells + depth_z // 2
    plane = row + rows_y // 2
    return cells, row, plane, plane + n_wide, plane + n_wide + 8


partners = (4, 5, 2, 3, 6, 7, 1, 0)


def by_partner(ref, parts):
    mine = lax.axis_index("grp")
    for d, part in zip(partners, parts):
        part[...] = ref[jnp.bitwise_xor(mine, d)]


def from_partner(parts, ref):
    mine = lax.axis_index("grp")
    for d, part in zip(partners, parts):
        ref[jnp.bitwise_xor(mine, d)] = part[...]


def exchanged(parts):
    count = len(parts)
    return [
        part if d == 0 else lax.ppermute(part, "grp", [(i, i ^ d) for i in range(count)])
        for d, part in zip(partners, parts)
    ]


def halves(one, two, first_half):
    even = jnp.where(first_half, one, pltpu.roll(two, lanes // 2, 1))
    odd = jnp.where(first_half, pltpu.roll(one, lanes // 2, 1), two)
    return even, odd


def times_x(value, high_ref, low_ref):
    high, low = split_two(value)
    return dot(high, high_ref[...]) + dot(low, high_ref[...]) + dot(high, low_ref[...])


def divergence_part(forced_ref, div, sums, shape):
    rows_y, depth_z, length_x = shape
    tiles_x = length_x // lanes
    rows = rows_y * depth_z
    level = iota((depth_z, length_x), 0)
    sums[...] = jnp.zeros_like(sums)

    def one_row(y, carry):
        after = jnp.minimum(y + 1, rows_y - 1)
        along = wide_row(forced_ref, 0, y, tiles_x, depth_z)
        second = wide_row(forced_ref, 1, y, tiles_x, depth_z)
        third = wide_row(forced_ref, 2, y, tiles_x, depth_z)
        north = wide_row(forced_ref, 1, after, tiles_x, depth_z)
        north = jnp.where(y == rows_y - 1, 0.0, north)
        upper = jnp.where(level == depth_z - 1, 0.0, pltpu.roll(third, depth_z - 1, 0))
        total = pltpu.roll(along, length_x - 1, 1) - along + (north - second) + (upper - third)
        div[pl.ds(pl.multiple_of(y * depth_z, depth_z), depth_z), :] = total
        div[pl.ds(rows + depth_z + y, 1), :] = third[0:1, :]
        folded = sum(second[:, x * lanes : (x + 1) * lanes] for x in range(tiles_x))
        sums[pl.ds(y, 1), :] = jnp.sum(folded, axis=0, keepdims=True)
        return carry

    loop(0, rows_y, one_row, 0, 6)
    div[rows : rows + depth_z, :] = wide_row(forced_ref, 1, 0, tiles_x, depth_z)


def first_body(shape, *refs):
    vel_far, scal_far, ylo, yhi, zlo, zhi, recv_ref, high_ref, low_ref, far_ref, *rest = refs
    out_refs, rest = rest[:-14], rest[-14:]
    vel_ref, scal_ref, sems, star_ref, forced_ref, out_ref, *rest = rest
    force, samp, table, div, modes, index, sem, far_sem = rest
    rows_y, depth_z, length_x = shape
    n_grp = out_ref.shape[0]
    n_wide = recv_ref.shape[0] // n_grp
    rows = rows_y * depth_z
    tiles_x = length_x // lanes
    stencil_part(
        vel_far, scal_far, ylo, yhi, zlo, zhi, vel_ref, scal_ref, forced_ref, star_ref, sems
    )
    marker_part(recv_ref, star_ref, forced_ref, force, samp, table, index, sem, tiles_x, depth_z)
    keep = pltpu.make_async_copy(forced_ref, far_ref, far_sem)
    keep.start()
    divergence_part(forced_ref, div, samp, (rows_y, depth_z, length_x))
    chunk = div.shape[0] // 4
    for start in range(0, 4 * chunk, chunk):
        modes[start : start + chunk, :] = times_x(div[start : start + chunk, :], high_ref, low_ref)
    row, plane, forces, sums_row, end = packed_rows(rows_y, depth_z, n_wide)

    def send(front, back, size, place):
        first_half = iota((size, lanes), 1) < lanes // 2
        for j in range(n_grp // 2):
            one = modes[pl.ds(front, size), j * lanes : (j + 1) * lanes]
            two = modes[pl.ds(back, size), j * lanes : (j + 1) * lanes]
            even, odd = halves(one, two, first_half)
            out_ref[2 * j, pl.ds(place, size), :] = even
            out_ref[2 * j + 1, pl.ds(place, size), :] = odd

    def shuffle(y, carry):
        front = pl.multiple_of(y * depth_z, depth_z)
        back = pl.multiple_of((y + rows_y // 2) * depth_z, depth_z)
        send(front, back, depth_z, front)
        return carry

    loop(0, rows_y // 2, shuffle, 0, 8)
    send(rows, rows + depth_z // 2, depth_z // 2, row)
    send(rows + depth_z, rows + depth_z + rows_y // 2, rows_y // 2, plane)
    total = jnp.broadcast_to(jnp.sum(samp[...].T, axis=0, keepdims=True), (end - sums_row, lanes))
    for g in range(n_grp):
        out_ref[g, forces:sums_row, :] = force[pl.ds(g, n_wide, stride=n_grp), :]
        out_ref[g, sums_row:end, :] = total
    by_partner(out_ref, out_refs)
    keep.wait()


def times_z(value, high_ref, low_ref):
    high, low = split_two(value)
    return dot(high_ref[...], high) + dot(high_ref[...], low) + dot(low_ref[...], high)


def forward_z_body(rows_y, *refs):
    recv_refs, refs = refs[:-7], refs[-7:]
    high_ref, low_ref, table_ref, coef_ref, ends_ref, small_ref, recv_ref = refs
    n_grp = recv_ref.shape[0]
    from_partner(recv_refs, recv_ref)
    n_wide = small_ref.shape[0]
    steps, full_z, _ = coef_ref.shape
    depth_z = full_z // n_grp
    row, plane, forces, sums_row, end = packed_rows(rows_y, depth_z, n_wide)
    root = table_ref[0]
    last = iota((n_grp, depth_z, lanes), 1) == depth_z - 1
    first_half = iota((full_z, lanes), 1) < lanes // 2

    def cells_of(step):
        value = recv_ref[:, pl.ds(pl.multiple_of(step * depth_z, depth_z), depth_z), :]
        edge = recv_ref[:, pl.ds(plane + step, 1), :]
        edge = jnp.concatenate([edge[1:], edge[:1]], axis=0)
        value = value + jnp.where(last, jnp.broadcast_to(edge, value.shape), 0.0)
        return value.reshape(full_z, lanes)

    def one_pair(pair, total):
        value = jnp.concatenate([cells_of(2 * pair), cells_of(2 * pair + 1)], axis=1)
        found = times_z(value, high_ref, low_ref)
        coef_ref[2 * pair] = found[:, :lanes]
        coef_ref[2 * pair + 1] = found[:, lanes:]
        return found[:, lanes:] + root * (found[:, :lanes] + root * total)

    packed = recv_ref[:, row:plane, :]
    other = jnp.stack([pltpu.roll(packed[g], lanes // 2, 1) for g in range(n_grp)], axis=0)
    extra = jnp.concatenate([packed, other], axis=1).reshape(full_z, lanes)
    extra = jnp.where(first_half, times_z(extra, high_ref, low_ref), 0.0)
    ends_ref[2] = extra
    up = loop(0, steps // 2, one_pair, extra, 6)
    down = loop(
        0,
        steps,
        lambda i, total: coef_ref[steps - 1 - i] + root * total,
        jnp.zeros((full_z, lanes), f32),
        4,
    )
    down = root * down
    ends_ref[0] = up
    ends_ref[1] = down
    over = table_ref[1]
    up_other = pltpu.roll(up, lanes // 2, 1)
    down_other = pltpu.roll(down, lanes // 2, 1)
    up = jnp.where(first_half, up_other + over * up, up + over * up_other)
    down = jnp.where(first_half, down + over * down_other, down_other + over * down)
    down = down + extra + pltpu.roll(extra, lanes // 2, 1)
    upper = full_z // 2
    share = upper // n_wide
    for k, value in enumerate((up, down)):
        value = jnp.where(first_half[:upper], value[:upper], value[upper:])
        for i in range(n_wide):
            small_ref[i, k * share : (k + 1) * share, :] = value[i * share : (i + 1) * share]
    sums = sum(recv_ref[g, sums_row:end, :] for g in range(n_grp))
    for i in range(n_wide):
        for g in range(n_grp):
            place = 2 * share + g
            small_ref[i, place : place + 1, :] = recv_ref[g, forces + i : forces + i + 1, :]
        small_ref[i, 2 * share + n_grp : 2 * share + n_grp + 8, :] = sums


def widen(small):
    first_half = iota(small.shape, 1) < lanes // 2
    other = pltpu.roll(small, lanes // 2, 1)
    return jnp.concatenate(
        [jnp.where(first_half, small, other), jnp.where(first_half, other, small)], axis=0
    )


def backward_z_body(
    rows_y, coef_ref, ends_ref, small_ref, table_ref, high_ref, low_ref, *rest
):
    out_refs, rest = rest[:-3], rest[-3:]
    out_ref, ups, small = rest
    n_grp = out_ref.shape[0]
    steps, full_z, _ = coef_ref.shape
    depth_z = full_z // n_grp
    row, plane, _, _, _ = packed_rows(rows_y, depth_z, small_ref.shape[0])
    root, over, gain = table_ref[0], table_ref[1], table_ref[2]
    first_half = iota((full_z, lanes), 1) < lanes // 2
    share = small_ref.shape[1] // 2
    for i in range(small_ref.shape[0]):
        for k in range(2):
            small[k, i * share : (i + 1) * share] = small_ref[i, k * share : (k + 1) * share]
    up_in = widen(small[0])
    down_in = widen(small[1])
    up_start = jnp.where(
        first_half,
        up_in + ends_ref[2],
        pltpu.roll(ends_ref[0], lanes // 2, 1) + over * up_in,
    )
    down = jnp.where(
        first_half, pltpu.roll(ends_ref[1], lanes // 2, 1) + over * down_in, down_in
    )

    def rising(step, total):
        total = coef_ref[step] + root * total
        ups[step] = total
        return total

    loop(0, steps, rising, up_start, 4)

    def falling(i, total):
        pair = steps // 2 - 1 - i
        second = gain * (ups[2 * pair + 1] + total)
        total = root * (coef_ref[2 * pair + 1] + total)
        first = gain * (ups[2 * pair] + total)
        total = root * (coef_ref[2 * pair] + total)
        found = times_z(jnp.concatenate([first, second], axis=1), high_ref, low_ref)
        for j in range(2):
            step = 2 * pair + j
            value = found[:, j * lanes : (j + 1) * lanes]
            start = pl.multiple_of(step * depth_z, depth_z)
            out_ref[:, pl.ds(start, depth_z), :] = value.reshape(n_grp, depth_z, lanes)
            for g in range(n_grp):
                before = (g * depth_z - 1) % full_z
                out_ref[g, pl.ds(plane + step, 1), :] = value[before : before + 1, :]
        return total

    down = loop(0, steps // 2, falling, down, 6)
    extra = times_z(gain * (up_start + down), high_ref, low_ref)
    half = depth_z // 2
    for g in range(n_grp):
        start = g * depth_z
        out_ref[g, row:plane, :] = jnp.where(
            first_half[:half],
            extra[start : start + half],
            pltpu.roll(extra[start + half : start + depth_z], lanes // 2, 1),
        )
    by_partner(out_ref, out_refs)


def last_body(far_ref, mean_ref, high_ref, low_ref, *refs):
    recv_refs, refs = refs[:-10], refs[-10:]
    vel_far, scal_far, vel_ref, scal_ref, recv_ref, forced_ref, modes, press_ref, sem, sems = refs
    fetch = pltpu.make_async_copy(far_ref, forced_ref, sem)
    fetch.start()
    from_partner(recv_refs, recv_ref)
    n_grp = recv_ref.shape[0]
    _, rows_y, depth_z, length_x = vel_ref.shape
    rows = rows_y * depth_z
    tiles_x = length_x // lanes
    row, plane, _, _, _ = packed_rows(rows_y, depth_z, 0)

    def take(front, back, size, place):
        first_half = iota((size, lanes), 1) < lanes // 2
        for j in range(n_grp // 2):
            even = recv_ref[2 * j, pl.ds(place, size), :]
            odd = recv_ref[2 * j + 1, pl.ds(place, size), :]
            one, two = halves(even, odd, first_half)
            modes[pl.ds(front, size), j * lanes : (j + 1) * lanes] = one
            modes[pl.ds(back, size), j * lanes : (j + 1) * lanes] = two

    def shuffle(y, carry):
        front = pl.multiple_of(y * depth_z, depth_z)
        back = pl.multiple_of((y + rows_y // 2) * depth_z, depth_z)
        take(front, back, depth_z, front)
        return carry

    loop(0, rows_y // 2, shuffle, 0, 8)
    take(rows, rows + depth_z // 2, depth_z // 2, row)
    take(rows + depth_z, rows + depth_z + rows_y // 2, rows_y // 2, plane)
    chunk = modes.shape[0] // 4
    for start in range(0, 4 * chunk, chunk):
        press_ref[start : start + chunk, :] = times_x(
            modes[start : start + chunk, :], high_ref, low_ref
        )
    level = iota((depth_z, length_x), 0)

    def one_row(y, carry):
        start = pl.multiple_of(y * depth_z, depth_z)
        before = pl.multiple_of(jnp.where(y == 0, rows, start - depth_z), depth_z)
        press = press_ref[pl.ds(start, depth_z), :]
        south = press_ref[pl.ds(before, depth_z), :]
        below = jnp.broadcast_to(press_ref[pl.ds(rows + depth_z + y, 1), :], press.shape)
        lower = jnp.where(level == 0, below, pltpu.roll(press, 1, 0))
        west = pltpu.roll(press, 1, 1)
        mean = mean_ref[pl.ds(y, 1), :]
        mean = jnp.concatenate([mean] * tiles_x, axis=1)
        vel_ref[0, y] = wide_row(forced_ref, 0, y, tiles_x, depth_z) - (press - west)
        vel_ref[1, y] = wide_row(forced_ref, 1, y, tiles_x, depth_z) - (press - south) - mean
        vel_ref[2, y] = wide_row(forced_ref, 2, y, tiles_x, depth_z) - (press - lower)
        scal_ref[y] = wide_row(forced_ref, 3, y, tiles_x, depth_z)
        return carry

    fetch.wait()
    pieces = sems.shape[0] // 2
    size = rows_y // pieces
    copies = []
    for piece in range(pieces):
        loop(piece * size, (piece + 1) * size, one_row, 0, 6)
        part = pl.ds(piece * size, size)
        copies += [
            pltpu.make_async_copy(
                vel_ref.at[:, part], vel_far.at[:, part], sems.at[2 * piece]
            ),
            pltpu.make_async_copy(
                scal_ref.at[part], scal_far.at[part], sems.at[2 * piece + 1]
            ),
        ]
        copies[-2].start()
        copies[-1].start()
    for copy in copies:
        copy.wait()


def ring_body(recv_ref, table_ref, out_ref):
    count, size, _ = out_ref.shape
    rising = iota((size, lanes), 0) < size // 2
    ends = [
        jnp.where(rising, recv_ref[i, 0:size, :], recv_ref[count - 1 - i, 0:size, :])
        for i in range(count)
    ]
    step, whole = table_ref[0], table_ref[1]
    total = ends[0]
    for i in range(1, count):
        total = ends[i] + step * total
    total = whole * total
    reached = []
    for i in range(count):
        reached.append(total)
        total = ends[i] + step * total
    for i in range(count):
        out_ref[i] = jnp.where(rising, reached[i], reached[count - 1 - i])


def per_device(
    tables, velocity, scalar, marker_owner, marker_tile, marker_offset, marker_target, marker_eta
):
    _, rows_y, depth_z, length_x = velocity.shape
    n_wide = lax.axis_size("wide")
    n_grp = lax.axis_size("grp")
    owners = n_wide * n_grp
    full_z = depth_z * n_grp
    rows = rows_y * depth_z
    tiles_x = length_x // lanes
    held = marker_owner.shape[0]
    x_high, x_low, xt_high, xt_low, fz_high, fz_low, bz_high, bz_low, full, small_table = tables
    my_grp = lax.axis_index("grp")
    my_wide = lax.axis_index("wide")
    full = lax.dynamic_index_in_dim(full, my_grp, 0, keepdims=False)
    small_table = lax.dynamic_slice(
        small_table, (my_grp, my_wide, 0, 0, 0), (1, 1) + small_table.shape[2:]
    )[0, 0]

    owner = marker_owner[None, :]
    send, rank, y_first, y_last, z_first, z_last = call(
        pack_body,
        [((owners, 1, 2 * lanes), f32), ((1, held), jnp.int32)]
        + [((4, depth_z, length_x), f32)] * 2
        + [((4, rows_y, length_x), f32)] * 2,
        [
            owner,
            marker_tile[None, :],
            marker_offset[None, :],
            marker_target,
            marker_eta[None, :],
            velocity,
            scalar,
        ],
        [
            pltpu.VMEM((1, held), jnp.int32),
            pltpu.VMEM((1, held), jnp.int32),
            pltpu.VMEM((1, held), jnp.int32),
            pltpu.VMEM((4, held), f32),
            pltpu.VMEM((1, held), f32),
            pltpu.SemaphoreType.DMA((13,)),
        ],
        name="pack",
        room=58,
        far_in=range(7),
    )
    z_low = passed_along(z_last, "grp", 1)
    z_high = passed_along(z_first, "grp", -1)
    y_low = passed_along(y_last, "wide", 1)
    y_high = passed_along(y_first, "wide", -1)
    recv = lax.all_to_all(send, ("wide", "grp"), split_axis=0, concat_axis=0, tiled=True)
    flat = 4 * tiles_x * rows
    sent_rows = packed_rows(rows_y, depth_z, n_wide)[-1]
    back_rows = packed_rows(rows_y, depth_z, n_wide)[2]
    with_edges = rows + depth_z + rows_y
    forced, *chunks = call(
        functools.partial(first_body, scalar.shape),
        [((flat, lanes), f32)] + [((sent_rows, lanes), f32)] * n_grp,
        [velocity, scalar, y_low, y_high, z_low, z_high, recv, x_high, x_low],
        [
            pltpu.VMEM(velocity.shape, f32),
            pltpu.VMEM(scalar.shape, f32),
            pltpu.SemaphoreType.DMA((8,)),
            pltpu.VMEM((flat, lanes), f32),
            pltpu.VMEM((flat, lanes), f32),
            pltpu.VMEM((n_grp, sent_rows, lanes), f32),
            pltpu.VMEM((owners, lanes), f32),
            pltpu.VMEM((owners, lanes), f32),
            pltpu.VMEM((owners, lanes), jnp.int32),
            pltpu.VMEM((with_edges, length_x), f32),
            pltpu.VMEM((with_edges, length_x), f32),
            pltpu.SMEM((owners, lanes), jnp.int32),
            pltpu.SemaphoreType.DMA(()),
            pltpu.SemaphoreType.DMA(()),
        ],
        name="first",
        room=50,
        micros=40,
        far_in=(0, 1),
        far_out=(0,),
    )
    chunks = exchanged(chunks)
    ends_size = full_z // n_wide
    coef, ends, small = call(
        functools.partial(forward_z_body, rows_y),
        [
            ((rows_y // 2, full_z, lanes), f32),
            ((3, full_z, lanes), f32),
            ((n_wide, ends_size + n_grp + 8, lanes), f32),
        ],
        [*chunks, fz_high, fz_low, full],
        [
            pltpu.VMEM((n_grp, sent_rows, lanes), f32),
        ],
        name="forward_z",
    )
    small = lax.all_to_all(small, "wide", split_axis=0, concat_axis=0, tiled=True)
    (reach,) = call(
        ring_body, [((n_wide, ends_size, lanes), f32)], [small, small_table], name="ring"
    )
    reach = lax.all_to_all(reach, "wide", split_axis=0, concat_axis=0, tiled=True)
    place = (jnp.arange(lanes, dtype=jnp.int32) - my_wide)[None, :]
    marker_force, mine = call(
        functools.partial(unpack_body, n_grp, n_wide * rows_y, length_x * depth_z * n_grp),
        [((4, held), f32), ((lanes, lanes), f32)],
        [owner, rank, small, place],
        name="unpack",
    )
    chunks = call(
        functools.partial(backward_z_body, rows_y),
        [((back_rows, lanes), f32)] * n_grp,
        [coef, ends, reach, full, bz_high, bz_low],
        [
            pltpu.VMEM((n_grp, back_rows, lanes), f32),
            pltpu.VMEM((rows_y // 2, full_z, lanes), f32),
            pltpu.VMEM((2, full_z // 2, lanes), f32),
        ],
        name="backward_z",
    )
    chunks = exchanged(chunks)
    velocity_out, scalar_out = call(
        last_body,
        [(velocity.shape, f32), (scalar.shape, f32)],
        [forced, mine, xt_high, xt_low, *chunks],
        [
            pltpu.VMEM(velocity.shape, f32),
            pltpu.VMEM(scalar.shape, f32),
            pltpu.VMEM((n_grp, back_rows, lanes), f32),
            pltpu.VMEM((flat, lanes), f32),
            pltpu.VMEM((with_edges, length_x), f32),
            pltpu.VMEM((with_edges, length_x), f32),
            pltpu.SemaphoreType.DMA(()),
            pltpu.SemaphoreType.DMA((8,)),
        ],
        name="last",
        room=54,
        far_in=(0,),
        far_out=(0, 1),
    )
    return velocity_out, scalar_out, marker_force


def solution(mesh):
    n_wide, n_grp = mesh.shape["wide"], mesh.shape["grp"]
    rows_y, full_z, length_x = 48, 128, 512
    basis_x, squares_x = real_basis(length_x)
    basis_z, squares_z = real_basis(full_z)
    parts = (
        two_parts(basis_x)
        + two_parts(basis_x.T)
        + two_parts(basis_z.T)
        + two_parts(basis_z)
        + decay_tables(squares_x, squares_z, n_grp, n_wide, rows_y)
    )

    def whole(*args):
        tables = tuple(jnp.asarray(part) for part in parts)
        return per_device(tables, *args)

    return jax.shard_map(
        whole,
        mesh=mesh,
        in_specs=(
            P(None, "wide", "grp", None),
            P("wide", "grp", None),
            P(("wide", "grp")),
            P(("wide", "grp")),
            P(("wide", "grp")),
            P(None, ("wide", "grp")),
            P(("wide", "grp")),
        ),
        out_specs=(P(None, "wide", "grp", None), P("wide", "grp", None), P(None, ("wide", "grp"))),
        check_vma=False,
    )
```

```python
import functools
import math

import jax
import jax.numpy as jnp
import ml_dtypes
import numpy as np
from jax import lax
from jax.experimental import pallas as pl
from jax.experimental.pallas import tpu as pltpu
from jax.sharding import PartitionSpec as P

time_step = 0.1
viscosity = 0.4
diffusivity = 0.25
f32 = jnp.float32
bf16 = jnp.bfloat16
lanes = 128
slots = 32
vmem = pl.BlockSpec(memory_space=pltpu.VMEM)
hbm = pl.BlockSpec(memory_space=pltpu.HBM)


def iota(shape, dim):
    return lax.broadcasted_iota(jnp.int32, shape, dim)


def call(body, out, args, scratch=(), name=None, micros=0, far_in=(), far_out=(), room=0):
    shapes = [jax.ShapeDtypeStruct(s, d) for s, d in out]
    moved = sum(a.size * a.dtype.itemsize for a in args)
    moved += sum(s.size * s.dtype.itemsize for s in shapes)
    near = [a for i, a in enumerate(args) if i not in far_in]
    near += [s for i, s in enumerate(shapes) if i not in far_out]
    held = sum(a.size * a.dtype.itemsize for a in near)
    held += sum(math.prod(s.shape) * 4 for s in scratch if s.shape)
    moved = max(moved, micros * 3000000)
    return pl.pallas_call(
        body,
        out_shape=shapes,
        in_specs=[hbm if i in far_in else vmem for i in range(len(args))],
        out_specs=[hbm if i in far_out else vmem for i in range(len(out))],
        scratch_shapes=list(scratch),
        compiler_params=pltpu.CompilerParams(vmem_limit_bytes=max(held + 6 * 2**20, room * 2**20)),
        cost_estimate=pl.CostEstimate(flops=0, bytes_accessed=moved, transcendentals=0),
        name=name,
    )(*args)


def loop(low, high, body, init, by):
    def several(turn, carry):
        for i in range(by):
            carry = body(low + turn * by + i, carry)
        return carry

    return lax.fori_loop(0, (high - low) // by, several, init)


def passed_along(value, axis, steps):
    count = lax.axis_size(axis)
    return lax.ppermute(value, axis, [(i, (i + steps) % count) for i in range(count)])


def real_basis(length):
    place = np.arange(length)
    columns, squares = [], []
    for k in range(length // 2 + 1):
        angle = 2.0 * np.pi * ((k * place) % length) / length
        scale = math.sqrt((1.0 if k in (0, length // 2) else 2.0) / length)
        square = 4.0 * math.sin(math.pi * k / length) ** 2
        columns.append(scale * np.cos(angle))
        squares.append(square)
        if k not in (0, length // 2):
            columns.append(scale * np.sin(angle))
            squares.append(square)
    return np.stack(columns, axis=1), np.array(squares)


def two_parts(table):
    high = table.astype(np.float32).astype(ml_dtypes.bfloat16)
    low = (table - high.astype(np.float64)).astype(np.float32).astype(ml_dtypes.bfloat16)
    return high, low


def decay_tables(squares_x, squares_z, n_grp, n_wide, rows_y):
    full_y = n_wide * rows_y
    local = squares_x.shape[0] // n_grp
    square = squares_z[None, :, None] + squares_x.reshape(n_grp, 1, local)
    mean_mode = square == 0.0
    safe = np.where(mean_mode, 1.0, square)
    root = 1.0 / (1.0 + safe / 2.0 + np.sqrt(safe + safe * safe / 4.0))
    root = np.where(mean_mode, 0.0, root)
    gain = np.where(mean_mode, 0.0, -root / (1.0 - root * root))
    half = rows_y // 2
    full = np.stack([root, root**half, gain], axis=1)
    full = np.concatenate([full, full], axis=3)
    device = root**rows_y
    small = np.stack([device, 1.0 / (1.0 - root**full_y)], axis=1)
    upper = small.shape[2] // 2
    small = np.concatenate([small[:, :, :upper], small[:, :, upper:]], axis=3)
    share = upper // n_wide
    small = small.reshape(n_grp, 2, n_wide, share, 2 * local).transpose(0, 2, 1, 3, 4)
    small = np.concatenate([small, small], axis=3)
    return full.astype(np.float32), small.astype(np.float32)


def split_two(value):
    high = value.astype(bf16)
    return high, (value - high.astype(f32)).astype(bf16)


def split_three(value):
    high = value.astype(bf16)
    rest = value - high.astype(f32)
    middle = rest.astype(bf16)
    return high, middle, (rest - middle.astype(f32)).astype(bf16)


def dot(left, right, dims=((1,), (0,))):
    return lax.dot_general(left, right, (dims, ((), ())), preferred_element_type=f32)


def pack_body(*refs):
    far, near, sems = refs[:7], refs[13:18], refs[18]
    send_ref, rank_ref, y_first, y_last, z_first, z_last = refs[7:13]
    vel_far, scal_far = far[5:]
    rows_y, depth_z, _ = scal_far.shape
    pairs = list(zip(far[:5], near))
    for y, out in ((0, y_first), (rows_y - 1, y_last)):
        pairs += [(vel_far.at[:, y], out.at[0:3]), (scal_far.at[y], out.at[3])]
    for z, out in ((0, z_first), (depth_z - 1, z_last)):
        pairs += [(vel_far.at[:, :, z, :], out.at[0:3]), (scal_far.at[:, z, :], out.at[3])]
    copies = [pltpu.make_async_copy(a, b, sems.at[i]) for i, (a, b) in enumerate(pairs)]
    for copy in copies:
        copy.start()
    for copy in copies[:5]:
        copy.wait()
    pack_markers(*near, send_ref, rank_ref)
    for copy in copies[5:]:
        copy.wait()


def pack_markers(owner_ref, tile_ref, offset_ref, target_ref, eta_ref, send_ref, rank_ref):
    owners = send_ref.shape[0]
    held = owner_ref.shape[1]
    onehot = owner_ref[...] == iota((owners, held), 0)
    onehot = jnp.where(onehot, 1.0, 0.0)
    upto = jnp.where(iota((lanes, lanes), 0) <= iota((lanes, lanes), 1), 1.0, 0.0).astype(bf16)
    carry = jnp.zeros((owners, 1), f32)
    ranks = []
    for start in range(0, held, lanes):
        piece = onehot[:, start : start + lanes]
        running = dot(piece.astype(bf16), upto) + carry
        ranks.append(jnp.sum(running * piece, axis=0, keepdims=True) - 1.0)
        carry = carry + jnp.sum(piece, axis=1, keepdims=True)
    rank = jnp.concatenate(ranks, axis=1).astype(jnp.int32)
    rank_ref[...] = rank
    chosen = rank == iota((slots, held), 0)
    cell = (tile_ref[...] * lanes + offset_ref[...]).astype(f32)
    values = [target_ref[k : k + 1, :] for k in range(4)] + [eta_ref[...], cell]
    onehot = onehot.astype(bf16)
    total = jnp.zeros((owners, 6 * slots), f32)
    for part in range(3):
        rows = [
            jnp.where(chosen, split_three(v)[part].astype(f32), 0.0).astype(bf16) for v in values
        ]
        total = total + dot(onehot, jnp.concatenate(rows, axis=0), ((1,), (1,)))
    column = iota((owners, 2 * lanes), 1)
    slot = column - 5 * slots
    spare = (slot >= 0) & (slot < slots) & (slot.astype(f32) >= carry)
    total = jnp.concatenate([total, jnp.zeros((owners, 2 * lanes - 6 * slots), f32)], axis=1)
    send_ref[:, 0, :] = total + jnp.where(spare, (slot * lanes).astype(f32), 0.0)


def unpack_body(
    n_grp, all_rows, row_cells, owner_ref, rank_ref, back_ref, place_ref, force_ref, mean_ref
):
    size = back_ref.shape[1] // 3
    owners = back_ref.shape[0] * n_grp
    held = owner_ref.shape[1]
    onehot = jnp.where(owner_ref[...] == iota((owners, held), 0), 1.0, 0.0).astype(bf16)
    sums = back_ref[:, 2 * size, :]
    sums = jnp.concatenate([sums, jnp.zeros((lanes - sums.shape[0], lanes), f32)], axis=0).T
    mine = jnp.where(place_ref[...] == 0, sums, 0.0)
    mean = jnp.sum(jnp.sum(sums, axis=1, keepdims=True), axis=0, keepdims=True)
    mine = jnp.sum(mine, axis=1, keepdims=True) * (1.0 / row_cells)
    mean_ref[...] = jnp.broadcast_to(mine - mean * (1.0 / (all_rows * row_cells)), mean_ref.shape)
    back = back_ref[:, size : 2 * size, :].reshape(owners, lanes).T
    spread = sum(dot(part, onehot) for part in split_three(back))
    chosen = rank_ref[...] == iota((slots, held), 0)
    for k in range(4):
        piece = jnp.where(chosen, spread[k * slots : (k + 1) * slots], 0.0)
        force_ref[k : k + 1, :] = jnp.sum(piece, axis=0, keepdims=True)


def swap_groups(value):
    row = iota(value.shape, 0) & 3
    group = lax.shift_right_logical(iota(value.shape, 1), 5)
    count = value.shape[0]
    out = value
    for k in (1, 2, 3):
        moved = pltpu.roll(value, 32 * k, 1)
        moved = jnp.where(
            row + k < 4, pltpu.roll(moved, count - k, 0), pltpu.roll(moved, 4 - k, 0)
        )
        out = jnp.where(((group - row) & 3) == k, moved, out)
    return out


def marker_part(recv_ref, star_ref, out_ref, force_ref, samp, table, index, sem, tiles_x, depth_z):
    sources = recv_ref.shape[0]
    wide_lane = iota((sources, lanes), 1)
    second = recv_ref[:, 0, lanes : 2 * lanes]
    cell = pltpu.roll(second.astype(jnp.int32), lanes - 32, 1)
    tile = lax.shift_right_logical(cell, 7)
    shift_x = tiles_x.bit_length() - 1
    shift_z = shift_x + depth_z.bit_length() - 1
    row = lax.shift_right_logical(tile, shift_z) * tiles_x + (tile & (tiles_x - 1))
    row = row * depth_z + (lax.shift_right_logical(tile, shift_x) & (depth_z - 1))
    spot = (iota((sources, lanes), 0) & 3) * 32 + (wide_lane & 31)
    there = (spot - cell) & (lanes - 1)
    back = (cell - spot) & (lanes - 1)
    table[...] = jnp.where(
        wide_lane < 32,
        4 * row,
        jnp.where(wide_lane < 64, pltpu.roll(there, 32, 1), pltpu.roll(back, 64, 1)),
    )
    copy = pltpu.make_async_copy(table, index, sem)
    copy.start()
    copy.wait()
    lane = iota((4, lanes), 1)

    def at(place):
        return pl.ds(pl.multiple_of(place, 4), 4)

    eta = jnp.where(wide_lane < 32, second, 0.0)
    eta = eta + pltpu.roll(eta, 32, 1)
    eta = eta + pltpu.roll(eta, 64, 1)
    force_ref[...] = swap_groups(eta)
    samp[...] = swap_groups(recv_ref[:, 0, 0:lanes])

    def rows_of(batch):
        return pl.ds(pl.multiple_of(4 * batch, 4), 4)

    def look(source, q, r, found):
        value = star_ref[at(index[source, r]), :]
        value = pltpu.roll(value, index[source, 32 + r], 1)
        return jnp.where(lane == 32 * q + r, value, found)

    def force_of(batch, found):
        force = force_ref[rows_of(batch), :] * (samp[rows_of(batch), :] - found)
        samp[rows_of(batch), :] = force
        return force

    def add(source, q, first, mine):
        places = [index[source, first + j] for j in range(2)]
        values = [out_ref[at(place), :] for place in places]
        terms = []
        for j in range(2):
            only = jnp.where(lane == 32 * q + first + j, mine, 0.0)
            terms.append(pltpu.roll(only, index[source, 64 + first + j], 1))
        values[0] = values[0] + terms[0]
        values[1] = jnp.where(places[0] == places[1], values[0], values[1]) + terms[1]
        for j in range(2):
            out_ref[at(places[j]), :] = values[j]

    def both(batch, mine):
        found = jnp.zeros((4, lanes), f32)
        for q in range(4):
            source = 4 * batch + q
            for first in range(0, slots, 4):
                for r in range(first, first + 4):
                    found = look(source, q, r, found)
                for r in (first, first + 2):
                    add(source - 4, q, r, mine)
        return force_of(batch, found)

    found = jnp.zeros((4, lanes), f32)
    for q in range(4):
        for r in range(slots):
            found = look(q, q, r, found)
    mine = lax.fori_loop(1, sources // 4, both, force_of(0, found))
    for q in range(4):
        for r in range(0, slots, 2):
            add(sources - 4 + q, q, r, mine)
    force_ref[...] = swap_groups(samp[...])


def at_row(y, x, f, tiles_x, depth_z):
    return pl.ds((y * tiles_x + x) * (4 * depth_z) + f, depth_z, stride=4)


def stencil_part(
    vel_far, scal_far, ylo_ref, yhi_ref, zlo_ref, zhi_ref, vel_ref, scal_ref, out_ref, same_ref, sems
):
    _, rows_y, depth_z, length_x = vel_ref.shape
    tiles_x = length_x // lanes
    level = iota((depth_z, length_x), 0)

    def one_row(y, carry):
        at_low = y == 0
        at_high = y == rows_y - 1
        below = jnp.maximum(y - 1, 0)
        above = jnp.minimum(y + 1, rows_y - 1)
        flow = [vel_ref[f, y] for f in range(3)]
        for f in range(4):
            if f < 3:
                center = flow[f]
                low, high = vel_ref[f, below], vel_ref[f, above]
            else:
                center = scal_ref[y]
                low, high = scal_ref[below], scal_ref[above]
            south = jnp.where(at_low, ylo_ref[f], low)
            north = jnp.where(at_high, yhi_ref[f], high)
            east = pltpu.roll(center, length_x - 1, 1)
            west = pltpu.roll(center, 1, 1)
            top = jnp.broadcast_to(zhi_ref[f, pl.ds(y, 1), :], center.shape)
            bottom = jnp.broadcast_to(zlo_ref[f, pl.ds(y, 1), :], center.shape)
            upper = jnp.where(level == depth_z - 1, top, pltpu.roll(center, depth_z - 1, 0))
            lower = jnp.where(level == 0, bottom, pltpu.roll(center, 1, 0))
            transport = (
                flow[0] * (east - west) + flow[1] * (north - south) + flow[2] * (upper - lower)
            )
            around = east + west + north + south + upper + lower
            coeff = viscosity if f < 3 else diffusivity
            star = (
                center * (1.0 - 6.0 * time_step * coeff)
                + (time_step * coeff) * around
                - (0.5 * time_step) * transport
            )
            for x in range(tiles_x):
                place = at_row(y, x, f, tiles_x, depth_z)
                out_ref[place, :] = star[:, x * lanes : (x + 1) * lanes]
                same_ref[place, :] = star[:, x * lanes : (x + 1) * lanes]
        return carry

    pieces = sems.shape[0] // 2
    size = rows_y // pieces
    fetches = []
    for piece in range(pieces):
        part = pl.ds(piece * size, size)
        fetches.append(
            [
                pltpu.make_async_copy(
                    vel_far.at[:, part], vel_ref.at[:, part], sems.at[2 * piece]
                ),
                pltpu.make_async_copy(
                    scal_far.at[part], scal_ref.at[part], sems.at[2 * piece + 1]
                ),
            ]
        )
        for copy in fetches[-1]:
            copy.start()
    for copy in fetches[0]:
        copy.wait()
    for piece in range(pieces):
        for copy in fetches[piece + 1] if piece + 1 < pieces else ():
            copy.wait()
        loop(piece * size, (piece + 1) * size, one_row, 0, 3)


def wide_row(ref, f, y, tiles_x, depth_z):
    return jnp.concatenate(
        [ref[at_row(y, x, f, tiles_x, depth_z), :] for x in range(tiles_x)], axis=1
    )


def packed_rows(rows_y, depth_z, n_wide):
    cells = rows_y // 2 * depth_z
    row = cells + depth_z // 2
    plane = row + rows_y // 2
    return cells, row, plane, plane + n_wide, plane + n_wide + 8


partners = (4, 5, 2, 3, 6, 7, 1, 0)


def by_partner(ref, parts):
    mine = lax.axis_index("grp")
    for d, part in zip(partners, parts):
        part[...] = ref[jnp.bitwise_xor(mine, d)]


def from_partner(parts, ref):
    mine = lax.axis_index("grp")
    for d, part in zip(partners, parts):
        ref[jnp.bitwise_xor(mine, d)] = part[...]


def exchanged(parts):
    count = len(parts)
    return [
        part if d == 0 else lax.ppermute(part, "grp", [(i, i ^ d) for i in range(count)])
        for d, part in zip(partners, parts)
    ]


def halves(one, two, first_half):
    even = jnp.where(first_half, one, pltpu.roll(two, lanes // 2, 1))
    odd = jnp.where(first_half, pltpu.roll(one, lanes // 2, 1), two)
    return even, odd


def times_x(value, high_ref, low_ref):
    high, low = split_two(value)
    return dot(high, high_ref[...]) + dot(low, high_ref[...]) + dot(high, low_ref[...])


def divergence_part(forced_ref, div, sums, shape):
    rows_y, depth_z, length_x = shape
    tiles_x = length_x // lanes
    rows = rows_y * depth_z
    level = iota((depth_z, length_x), 0)
    sums[...] = jnp.zeros_like(sums)

    def one_row(y, carry):
        after = jnp.minimum(y + 1, rows_y - 1)
        along = wide_row(forced_ref, 0, y, tiles_x, depth_z)
        second = wide_row(forced_ref, 1, y, tiles_x, depth_z)
        third = wide_row(forced_ref, 2, y, tiles_x, depth_z)
        north = wide_row(forced_ref, 1, after, tiles_x, depth_z)
        north = jnp.where(y == rows_y - 1, 0.0, north)
        upper = jnp.where(level == depth_z - 1, 0.0, pltpu.roll(third, depth_z - 1, 0))
        total = pltpu.roll(along, length_x - 1, 1) - along + (north - second) + (upper - third)
        div[pl.ds(pl.multiple_of(y * depth_z, depth_z), depth_z), :] = total
        div[pl.ds(rows + depth_z + y, 1), :] = third[0:1, :]
        folded = sum(second[:, x * lanes : (x + 1) * lanes] for x in range(tiles_x))
        sums[pl.ds(y, 1), :] = jnp.sum(folded, axis=0, keepdims=True)
        return carry

    loop(0, rows_y, one_row, 0, 6)
    div[rows : rows + depth_z, :] = wide_row(forced_ref, 1, 0, tiles_x, depth_z)


def first_body(shape, *refs):
    vel_far, scal_far, ylo, yhi, zlo, zhi, recv_ref, high_ref, low_ref, far_ref, *rest = refs
    out_refs, rest = rest[:-14], rest[-14:]
    vel_ref, scal_ref, sems, star_ref, forced_ref, out_ref, *rest = rest
    force, samp, table, div, modes, index, sem, far_sem = rest
    rows_y, depth_z, length_x = shape
    n_grp = out_ref.shape[0]
    n_wide = recv_ref.shape[0] // n_grp
    rows = rows_y * depth_z
    tiles_x = length_x // lanes
    stencil_part(
        vel_far, scal_far, ylo, yhi, zlo, zhi, vel_ref, scal_ref, forced_ref, star_ref, sems
    )
    marker_part(recv_ref, star_ref, forced_ref, force, samp, table, index, sem, tiles_x, depth_z)
    keep = pltpu.make_async_copy(forced_ref, far_ref, far_sem)
    keep.start()
    divergence_part(forced_ref, div, samp, (rows_y, depth_z, length_x))
    chunk = div.shape[0] // 4
    for start in range(0, 4 * chunk, chunk):
        modes[start : start + chunk, :] = times_x(div[start : start + chunk, :], high_ref, low_ref)
    row, plane, forces, sums_row, end = packed_rows(rows_y, depth_z, n_wide)

    def send(front, back, size, place):
        first_half = iota((size, lanes), 1) < lanes // 2
        for j in range(n_grp // 2):
            one = modes[pl.ds(front, size), j * lanes : (j + 1) * lanes]
            two = modes[pl.ds(back, size), j * lanes : (j + 1) * lanes]
            even, odd = halves(one, two, first_half)
            out_ref[2 * j, pl.ds(place, size), :] = even
            out_ref[2 * j + 1, pl.ds(place, size), :] = odd

    def shuffle(y, carry):
        front = pl.multiple_of(y * depth_z, depth_z)
        back = pl.multiple_of((y + rows_y // 2) * depth_z, depth_z)
        send(front, back, depth_z, front)
        return carry

    loop(0, rows_y // 2, shuffle, 0, 8)
    send(rows, rows + depth_z // 2, depth_z // 2, row)
    send(rows + depth_z, rows + depth_z + rows_y // 2, rows_y // 2, plane)
    total = jnp.broadcast_to(jnp.sum(samp[...].T, axis=0, keepdims=True), (end - sums_row, lanes))
    for g in range(n_grp):
        out_ref[g, forces:sums_row, :] = force[pl.ds(g, n_wide, stride=n_grp), :]
        out_ref[g, sums_row:end, :] = total
    by_partner(out_ref, out_refs)
    keep.wait()


def times_z(value, high_ref, low_ref):
    high, low = split_two(value)
    return dot(high_ref[...], high) + dot(high_ref[...], low) + dot(low_ref[...], high)


def forward_z_body(rows_y, *refs):
    recv_refs, refs = refs[:-7], refs[-7:]
    high_ref, low_ref, table_ref, coef_ref, ends_ref, small_ref, recv_ref = refs
    n_grp = recv_ref.shape[0]
    from_partner(recv_refs, recv_ref)
    n_wide = small_ref.shape[0]
    steps, full_z, _ = coef_ref.shape
    depth_z = full_z // n_grp
    row, plane, forces, sums_row, end = packed_rows(rows_y, depth_z, n_wide)
    root = table_ref[0]
    last = iota((n_grp, depth_z, lanes), 1) == depth_z - 1
    first_half = iota((full_z, lanes), 1) < lanes // 2

    def cells_of(step):
        value = recv_ref[:, pl.ds(pl.multiple_of(step * depth_z, depth_z), depth_z), :]
        edge = recv_ref[:, pl.ds(plane + step, 1), :]
        edge = jnp.concatenate([edge[1:], edge[:1]], axis=0)
        value = value + jnp.where(last, jnp.broadcast_to(edge, value.shape), 0.0)
        return value.reshape(full_z, lanes)

    def one_pair(pair, total):
        value = jnp.concatenate([cells_of(2 * pair), cells_of(2 * pair + 1)], axis=1)
        found = times_z(value, high_ref, low_ref)
        coef_ref[2 * pair] = found[:, :lanes]
        coef_ref[2 * pair + 1] = found[:, lanes:]
        return found[:, lanes:] + root * (found[:, :lanes] + root * total)

    packed = recv_ref[:, row:plane, :]
    other = jnp.stack([pltpu.roll(packed[g], lanes // 2, 1) for g in range(n_grp)], axis=0)
    extra = jnp.concatenate([packed, other], axis=1).reshape(full_z, lanes)
    extra = jnp.where(first_half, times_z(extra, high_ref, low_ref), 0.0)
    ends_ref[2] = extra
    up = loop(0, steps // 2, one_pair, extra, 6)
    down = loop(
        0,
        steps,
        lambda i, total: coef_ref[steps - 1 - i] + root * total,
        jnp.zeros((full_z, lanes), f32),
        4,
    )
    down = root * down
    ends_ref[0] = up
    ends_ref[1] = down
    over = table_ref[1]
    up_other = pltpu.roll(up, lanes // 2, 1)
    down_other = pltpu.roll(down, lanes // 2, 1)
    up = jnp.where(first_half, up_other + over * up, up + over * up_other)
    down = jnp.where(first_half, down + over * down_other, down_other + over * down)
    down = down + extra + pltpu.roll(extra, lanes // 2, 1)
    upper = full_z // 2
    share = upper // n_wide
    for k, value in enumerate((up, down)):
        value = jnp.where(first_half[:upper], value[:upper], value[upper:])
        for i in range(n_wide):
            small_ref[i, k * share : (k + 1) * share, :] = value[i * share : (i + 1) * share]
    sums = sum(recv_ref[g, sums_row:end, :] for g in range(n_grp))
    for i in range(n_wide):
        for g in range(n_grp):
            place = 2 * share + g
            small_ref[i, place : place + 1, :] = recv_ref[g, forces + i : forces + i + 1, :]
        small_ref[i, 2 * share + n_grp : 2 * share + n_grp + 8, :] = sums


def widen(small):
    first_half = iota(small.shape, 1) < lanes // 2
    other = pltpu.roll(small, lanes // 2, 1)
    return jnp.concatenate(
        [jnp.where(first_half, small, other), jnp.where(first_half, other, small)], axis=0
    )


def backward_z_body(
    rows_y, coef_ref, ends_ref, small_ref, table_ref, high_ref, low_ref, *rest
):
    out_refs, rest = rest[:-3], rest[-3:]
    out_ref, ups, small = rest
    n_grp = out_ref.shape[0]
    steps, full_z, _ = coef_ref.shape
    depth_z = full_z // n_grp
    row, plane, _, _, _ = packed_rows(rows_y, depth_z, small_ref.shape[0])
    root, over, gain = table_ref[0], table_ref[1], table_ref[2]
    first_half = iota((full_z, lanes), 1) < lanes // 2
    share = small_ref.shape[1] // 2
    for i in range(small_ref.shape[0]):
        for k in range(2):
            small[k, i * share : (i + 1) * share] = small_ref[i, k * share : (k + 1) * share]
    up_in = widen(small[0])
    down_in = widen(small[1])
    up_start = jnp.where(
        first_half,
        up_in + ends_ref[2],
        pltpu.roll(ends_ref[0], lanes // 2, 1) + over * up_in,
    )
    down = jnp.where(
        first_half, pltpu.roll(ends_ref[1], lanes // 2, 1) + over * down_in, down_in
    )

    def rising(step, total):
        total = coef_ref[step] + root * total
        ups[step] = total
        return total

    loop(0, steps, rising, up_start, 4)

    def falling(i, total):
        pair = steps // 2 - 1 - i
        second = gain * (ups[2 * pair + 1] + total)
        total = root * (coef_ref[2 * pair + 1] + total)
        first = gain * (ups[2 * pair] + total)
        total = root * (coef_ref[2 * pair] + total)
        found = times_z(jnp.concatenate([first, second], axis=1), high_ref, low_ref)
        for j in range(2):
            step = 2 * pair + j
            value = found[:, j * lanes : (j + 1) * lanes]
            start = pl.multiple_of(step * depth_z, depth_z)
            out_ref[:, pl.ds(start, depth_z), :] = value.reshape(n_grp, depth_z, lanes)
            for g in range(n_grp):
                before = (g * depth_z - 1) % full_z
                out_ref[g, pl.ds(plane + step, 1), :] = value[before : before + 1, :]
        return total

    down = loop(0, steps // 2, falling, down, 6)
    extra = times_z(gain * (up_start + down), high_ref, low_ref)
    half = depth_z // 2
    for g in range(n_grp):
        start = g * depth_z
        out_ref[g, row:plane, :] = jnp.where(
            first_half[:half],
            extra[start : start + half],
            pltpu.roll(extra[start + half : start + depth_z], lanes // 2, 1),
        )
    by_partner(out_ref, out_refs)


def last_body(far_ref, mean_ref, high_ref, low_ref, *refs):
    recv_refs, refs = refs[:-10], refs[-10:]
    vel_far, scal_far, vel_ref, scal_ref, recv_ref, forced_ref, modes, press_ref, sem, sems = refs
    fetch = pltpu.make_async_copy(far_ref, forced_ref, sem)
    fetch.start()
    from_partner(recv_refs, recv_ref)
    n_grp = recv_ref.shape[0]
    _, rows_y, depth_z, length_x = vel_ref.shape
    rows = rows_y * depth_z
    tiles_x = length_x // lanes
    row, plane, _, _, _ = packed_rows(rows_y, depth_z, 0)

    def take(front, back, size, place):
        first_half = iota((size, lanes), 1) < lanes // 2
        for j in range(n_grp // 2):
            even = recv_ref[2 * j, pl.ds(place, size), :]
            odd = recv_ref[2 * j + 1, pl.ds(place, size), :]
            one, two = halves(even, odd, first_half)
            modes[pl.ds(front, size), j * lanes : (j + 1) * lanes] = one
            modes[pl.ds(back, size), j * lanes : (j + 1) * lanes] = two

    def shuffle(y, carry):
        front = pl.multiple_of(y * depth_z, depth_z)
        back = pl.multiple_of((y + rows_y // 2) * depth_z, depth_z)
        take(front, back, depth_z, front)
        return carry

    loop(0, rows_y // 2, shuffle, 0, 8)
    take(rows, rows + depth_z // 2, depth_z // 2, row)
    take(rows + depth_z, rows + depth_z + rows_y // 2, rows_y // 2, plane)
    chunk = modes.shape[0] // 4
    for start in range(0, 4 * chunk, chunk):
        press_ref[start : start + chunk, :] = times_x(
            modes[start : start + chunk, :], high_ref, low_ref
        )
    level = iota((depth_z, length_x), 0)

    def one_row(y, carry):
        start = pl.multiple_of(y * depth_z, depth_z)
        before = pl.multiple_of(jnp.where(y == 0, rows, start - depth_z), depth_z)
        press = press_ref[pl.ds(start, depth_z), :]
        south = press_ref[pl.ds(before, depth_z), :]
        below = jnp.broadcast_to(press_ref[pl.ds(rows + depth_z + y, 1), :], press.shape)
        lower = jnp.where(level == 0, below, pltpu.roll(press, 1, 0))
        west = pltpu.roll(press, 1, 1)
        mean = mean_ref[pl.ds(y, 1), :]
        mean = jnp.concatenate([mean] * tiles_x, axis=1)
        vel_ref[0, y] = wide_row(forced_ref, 0, y, tiles_x, depth_z) - (press - west)
        vel_ref[1, y] = wide_row(forced_ref, 1, y, tiles_x, depth_z) - (press - south) - mean
        vel_ref[2, y] = wide_row(forced_ref, 2, y, tiles_x, depth_z) - (press - lower)
        scal_ref[y] = wide_row(forced_ref, 3, y, tiles_x, depth_z)
        return carry

    fetch.wait()
    pieces = sems.shape[0] // 2
    size = rows_y // pieces
    copies = []
    for piece in range(pieces):
        loop(piece * size, (piece + 1) * size, one_row, 0, 6)
        part = pl.ds(piece * size, size)
        copies += [
            pltpu.make_async_copy(
                vel_ref.at[:, part], vel_far.at[:, part], sems.at[2 * piece]
            ),
            pltpu.make_async_copy(
                scal_ref.at[part], scal_far.at[part], sems.at[2 * piece + 1]
            ),
        ]
        copies[-2].start()
        copies[-1].start()
    for copy in copies:
        copy.wait()


def ring_body(recv_ref, table_ref, out_ref):
    count, size, _ = out_ref.shape
    rising = iota((size, lanes), 0) < size // 2
    ends = [
        jnp.where(rising, recv_ref[i, 0:size, :], recv_ref[count - 1 - i, 0:size, :])
        for i in range(count)
    ]
    step, whole = table_ref[0], table_ref[1]
    total = ends[0]
    for i in range(1, count):
        total = ends[i] + step * total
    total = whole * total
    reached = []
    for i in range(count):
        reached.append(total)
        total = ends[i] + step * total
    for i in range(count):
        out_ref[i] = jnp.where(rising, reached[i], reached[count - 1 - i])


def per_device(
    tables, velocity, scalar, marker_owner, marker_tile, marker_offset, marker_target, marker_eta
):
    _, rows_y, depth_z, length_x = velocity.shape
    n_wide = lax.axis_size("wide")
    n_grp = lax.axis_size("grp")
    owners = n_wide * n_grp
    full_z = depth_z * n_grp
    rows = rows_y * depth_z
    tiles_x = length_x // lanes
    held = marker_owner.shape[0]
    x_high, x_low, xt_high, xt_low, fz_high, fz_low, bz_high, bz_low, full, small_table = tables
    my_grp = lax.axis_index("grp")
    my_wide = lax.axis_index("wide")
    full = lax.dynamic_index_in_dim(full, my_grp, 0, keepdims=False)
    small_table = lax.dynamic_slice(
        small_table, (my_grp, my_wide, 0, 0, 0), (1, 1) + small_table.shape[2:]
    )[0, 0]

    owner = marker_owner[None, :]
    send, rank, y_first, y_last, z_first, z_last = call(
        pack_body,
        [((owners, 1, 2 * lanes), f32), ((1, held), jnp.int32)]
        + [((4, depth_z, length_x), f32)] * 2
        + [((4, rows_y, length_x), f32)] * 2,
        [
            owner,
            marker_tile[None, :],
            marker_offset[None, :],
            marker_target,
            marker_eta[None, :],
            velocity,
            scalar,
        ],
        [
            pltpu.VMEM((1, held), jnp.int32),
            pltpu.VMEM((1, held), jnp.int32),
            pltpu.VMEM((1, held), jnp.int32),
            pltpu.VMEM((4, held), f32),
            pltpu.VMEM((1, held), f32),
            pltpu.SemaphoreType.DMA((13,)),
        ],
        name="pack",
        room=58,
        far_in=range(7),
    )
    z_low = passed_along(z_last, "grp", 1)
    z_high = passed_along(z_first, "grp", -1)
    y_low = passed_along(y_last, "wide", 1)
    y_high = passed_along(y_first, "wide", -1)
    recv = lax.all_to_all(send, ("wide", "grp"), split_axis=0, concat_axis=0, tiled=True)
    flat = 4 * tiles_x * rows
    sent_rows = packed_rows(rows_y, depth_z, n_wide)[-1]
    back_rows = packed_rows(rows_y, depth_z, n_wide)[2]
    with_edges = rows + depth_z + rows_y
    forced, *chunks = call(
        functools.partial(first_body, scalar.shape),
        [((flat, lanes), f32)] + [((sent_rows, lanes), f32)] * n_grp,
        [velocity, scalar, y_low, y_high, z_low, z_high, recv, x_high, x_low],
        [
            pltpu.VMEM(velocity.shape, f32),
            pltpu.VMEM(scalar.shape, f32),
            pltpu.SemaphoreType.DMA((8,)),
            pltpu.VMEM((flat, lanes), f32),
            pltpu.VMEM((flat, lanes), f32),
            pltpu.VMEM((n_grp, sent_rows, lanes), f32),
            pltpu.VMEM((owners, lanes), f32),
            pltpu.VMEM((owners, lanes), f32),
            pltpu.VMEM((owners, lanes), jnp.int32),
            pltpu.VMEM((with_edges, length_x), f32),
            pltpu.VMEM((with_edges, length_x), f32),
            pltpu.SMEM((owners, lanes), jnp.int32),
            pltpu.SemaphoreType.DMA(()),
            pltpu.SemaphoreType.DMA(()),
        ],
        name="first",
        room=50,
        micros=40,
        far_in=(0, 1),
        far_out=(0,),
    )
    chunks = exchanged(chunks)
    ends_size = full_z // n_wide
    coef, ends, small = call(
        functools.partial(forward_z_body, rows_y),
        [
            ((rows_y // 2, full_z, lanes), f32),
            ((3, full_z, lanes), f32),
            ((n_wide, ends_size + n_grp + 8, lanes), f32),
        ],
        [*chunks, fz_high, fz_low, full],
        [
            pltpu.VMEM((n_grp, sent_rows, lanes), f32),
        ],
        name="forward_z",
    )
    small = lax.all_to_all(small, "wide", split_axis=0, concat_axis=0, tiled=True)
    (reach,) = call(
        ring_body, [((n_wide, ends_size, lanes), f32)], [small, small_table], name="ring"
    )
    reach = lax.all_to_all(reach, "wide", split_axis=0, concat_axis=0, tiled=True)
    place = (jnp.arange(lanes, dtype=jnp.int32) - my_wide)[None, :]
    marker_force, mine = call(
        functools.partial(unpack_body, n_grp, n_wide * rows_y, length_x * depth_z * n_grp),
        [((4, held), f32), ((lanes, lanes), f32)],
        [owner, rank, small, place],
        name="unpack",
    )
    chunks = call(
        functools.partial(backward_z_body, rows_y),
        [((back_rows, lanes), f32)] * n_grp,
        [coef, ends, reach, full, bz_high, bz_low],
        [
            pltpu.VMEM((n_grp, back_rows, lanes), f32),
            pltpu.VMEM((rows_y // 2, full_z, lanes), f32),
            pltpu.VMEM((2, full_z // 2, lanes), f32),
        ],
        name="backward_z",
    )
    chunks = exchanged(chunks)
    velocity_out, scalar_out = call(
        last_body,
        [(velocity.shape, f32), (scalar.shape, f32)],
        [forced, mine, xt_high, xt_low, *chunks],
        [
            pltpu.VMEM(velocity.shape, f32),
            pltpu.VMEM(scalar.shape, f32),
            pltpu.VMEM((n_grp, back_rows, lanes), f32),
            pltpu.VMEM((flat, lanes), f32),
            pltpu.VMEM((with_edges, length_x), f32),
            pltpu.VMEM((with_edges, length_x), f32),
            pltpu.SemaphoreType.DMA(()),
            pltpu.SemaphoreType.DMA((8,)),
        ],
        name="last",
        room=51,
        far_in=(0,),
        far_out=(0, 1),
    )
    return velocity_out, scalar_out, marker_force


def solution(mesh):
    n_wide, n_grp = mesh.shape["wide"], mesh.shape["grp"]
    rows_y, full_z, length_x = 48, 128, 512
    basis_x, squares_x = real_basis(length_x)
    basis_z, squares_z = real_basis(full_z)
    parts = (
        two_parts(basis_x)
        + two_parts(basis_x.T)
        + two_parts(basis_z.T)
        + two_parts(basis_z)
        + decay_tables(squares_x, squares_z, n_grp, n_wide, rows_y)
    )

    def whole(*args):
        tables = tuple(jnp.asarray(part) for part in parts)
        return per_device(tables, *args)

    return jax.shard_map(
        whole,
        mesh=mesh,
        in_specs=(
            P(None, "wide", "grp", None),
            P("wide", "grp", None),
            P(("wide", "grp")),
            P(("wide", "grp")),
            P(("wide", "grp")),
            P(None, ("wide", "grp")),
            P(("wide", "grp")),
        ),
        out_specs=(P(None, "wide", "grp", None), P("wide", "grp", None), P(None, ("wide", "grp"))),
        check_vma=False,
    )
```
